32 devices in a mesh: wide: 8 (over z, y), ep: 4 (over x, core).
Axes of the slice: x: 2, y: 2, z: 4, core: 2. Of those that a mesh axis runs over, the one named last changes fastest.
Arguments:
- activations: bfloat16 [8192, 1280], P(('wide', 'ep')), may hold values from -6 to 6
- segment: int32 [8192], P(('wide', 'ep')), may hold values from 0 to 2, as said below
- routes: int32 [8192, 7], P(('wide', 'ep')), may hold values from 0 to 15, all different within a row; in each aligned block of 256 rows (0 to 255, 256 to 511, ...) at most 160 rows name the same one
- gain_attention: bfloat16 [1280], P(('wide', 'ep')), may hold values from 0.5 to 1.5
- query_weight: bfloat16 [1280, 1280], P(('wide', 'ep')), may hold values from -0.15625 to 0.15625
- key_weight: bfloat16 [1280, 1280], P(('wide', 'ep')), may hold values from -0.15625 to 0.15625
- value_weight: bfloat16 [1280, 1280], P(('wide', 'ep')), may hold values from -0.15625 to 0.15625
- output_weight: bfloat16 [1280, 1280], P(('wide', 'ep')), may hold values from -6 to 6
- gain_experts: bfloat16 [1280], P(('wide', 'ep')), may hold values from 0.5 to 1.5
- router_weight: bfloat16 [1280, 16], P(('wide', 'ep')), may hold values from -0.078125 to 0.078125
- shared_gate: bfloat16 [1280, 896], P(('wide', 'ep')), may hold values from -0.15625 to 0.15625
- shared_up: bfloat16 [1280, 896], P(('wide', 'ep')), may hold values from -0.15625 to 0.15625
- shared_down: bfloat16 [896, 1280], P(('wide', 'ep')), may hold values from -0.1875 to 0.1875
- expert_gate: bfloat16 [16, 1280, 896], P('ep'), may hold values from -0.15625 to 0.15625
- expert_up: bfloat16 [16, 1280, 896], P('ep'), may hold values from -0.15625 to 0.15625
- expert_down: bfloat16 [16, 896, 1280], P('ep'), may hold values from -1.5 to 1.5
- cotangent: bfloat16 [8192, 1280], P(('wide', 'ep')), may hold values from -6 to 6
Outputs:
- block_out: bfloat16 [8192, 1280], P(('wide', 'ep'))
- input_grad: float32 [8192, 1280], P(('wide', 'ep'))
- gain_attention_grad: float32 [1280], P(('wide', 'ep'))
- query_grad: float32 [1280, 1280], P(('wide', 'ep'))
- key_grad: float32 [1280, 1280], P(('wide', 'ep'))
- value_grad: float32 [1280, 1280], P(('wide', 'ep'))
- output_weight_grad: float32 [1280, 1280], P(('wide', 'ep'))
- gain_experts_grad: float32 [1280], P(('wide', 'ep'))
- router_grad: float32 [1280, 16], P(('wide', 'ep'))
- shared_gate_grad: float32 [1280, 896], P(('wide', 'ep'))
- shared_up_grad: float32 [1280, 896], P(('wide', 'ep'))
- shared_down_grad: float32 [896, 1280], P(('wide', 'ep'))
- expert_gate_grad: float32 [16, 1280, 896], P('ep', 'wide')
- expert_up_grad: float32 [16, 1280, 896], P('ep', 'wide')
- expert_down_grad: float32 [16, 896, 1280], P('ep', 'wide')
- expert_counts: int32 [16], P('ep')
The draws below stay inside these ranges and needn't reach their ends.
Inputs may be any that keep to these rules, and one draw needn't show every extreme that they name: `segment`: within each block of 1024 consecutive tokens the numbers start at 0, never fall and end at 2; document 1 begins in the first quarter of the block's first 256 tokens and ends in the last quarter of its last 256 tokens. `routes`: each row names 7 different experts; among the rows of one device no expert is named more than 160 times, and some device's rows name some expert exactly 160 times.
All inputs are finite; a program needn't handle non-finite values.
Results may differ from the reference program's by a relative error of at most 0.018.
Values may be sent and summed in bfloat16 or wider, within the bound.
A program may use at most 384 MiB of HBM per device.

```python
import math
import jax
import jax.numpy as jnp
import numpy as np
from jax import lax

D = 1280
HEADS = 10
HD = 128
FF = 896
TOPK = 7
TOK_DEV = 256
EXPERTS = 16
GROUP = 1024
TOKENS = 8192
CAP = 160
N_WIDE = 8
N_EP = 4


def draw_segment(key, part):
    key = jax.random.fold_in(key, 17)
    first_key, second_key = jax.random.split(key)
    group_count = TOKENS // GROUP
    cut_range = max(TOK_DEV // 4, 2)
    early_cut = jax.random.randint(first_key, (group_count, 1), 1, cut_range)
    late_cut = GROUP - jax.random.randint(second_key, (group_count, 1), 1, cut_range)
    places = jnp.arange(GROUP, dtype=jnp.int32)[None, :]
    numbers = (places >= early_cut).astype(jnp.int32) + (places >= late_cut).astype(jnp.int32)
    return numbers.reshape(TOKENS)


def block_levels(stream_key, dims, shards, least, high):
    def one(position, blocks):
        heights = jax.random.uniform(jax.random.fold_in(jax.random.fold_in(stream_key, 6), position), (blocks,), jnp.float32, least / len(shards), high / len(shards))
        return jnp.repeat(jnp.exp(heights), dims[position] // blocks).reshape((-1,) + (1,) * (len(dims) - position - 1))

    level = one(*shards[0])
    for cut in shards[1:]:
        level = level * one(*cut)
    return level


def assign_block(key, own, number, rows, number_of, top, limit, skew):
    sequence = jax.random.permutation(key, number_of)
    crowded, common = shares(number_of, rows * top, limit, skew, True), shares(number_of, rows * top, limit, skew, False)
    places = jnp.arange(number_of)

    def named(sizes, rotation):
        used = int((sizes > 0).sum())
        fixed = max(1, used // 4)
        moved = fixed + (places - fixed + rotation * (used - fixed)) % max(1, number_of - fixed)
        return jnp.zeros((number_of,), jnp.int32).at[sequence[jnp.where(places < fixed, places, moved)]].set(jnp.asarray(sizes, jnp.int32))

    sizes = jnp.where(number % 4 == 0, named(crowded, number // 4), named(common, number - number // 4 - 1))
    mixed = jax.random.permutation(jax.random.fold_in(own, 3), number_of)
    giver, taker = mixed[0:number_of // 2 * 2:2], mixed[1:number_of // 2 * 2:2]
    margin = jnp.minimum(sizes[giver] - 1, limit - sizes[taker]) // 2
    margin = jnp.where((giver == sequence[0]) | (taker == sequence[0]) | (sizes[taker] == 0), 0, jnp.maximum(margin, 0))
    moved = jax.random.randint(jax.random.fold_in(own, 4), (number_of // 2,), 0, 1 << 20) % (margin + 1)
    sizes = sizes.at[giver].add(-moved).at[taker].add(moved)
    items = jnp.searchsorted(jnp.cumsum(sizes), jnp.arange(rows * top), side="right").astype(jnp.int32)
    listing = items.reshape(top, rows).T
    listing = listing[jax.random.permutation(jax.random.fold_in(own, 1), rows)]
    rotation = jax.random.randint(jax.random.fold_in(own, 2), (rows, 1), 0, top)
    return jnp.take_along_axis(listing, (jnp.arange(top)[None, :] + rotation) % top, axis=1)


def shares(amount, total, most, slope, full):
    loads = [(1 << 20) // math.isqrt(grade ** slope) + 1 for grade in range(1, amount + 1)]
    largest = most if full else min(most, max(-(-total // amount), total * loads[0] // sum(loads)))
    least = 1 if total - largest >= amount - 1 else 0
    given, spare = [largest] + [least] * (amount - 1), total - largest - least * (amount - 1)
    while spare > 0:
        movable = [i for i in range(1, amount) if given[i] < largest] or [i for i in range(1, amount) if given[i] < most]
        mass, budget = sum([loads[i] for i in movable]), spare
        for i in movable:
            extra = min(most - given[i], max(1, budget * loads[i] // mass), spare)
            given[i] = given[i] + extra
            spare = spare - extra
    return np.array(given)


def noise(own_key, dims, spread, reach, cuts=(), kind=jnp.bfloat16):
    values = jax.random.normal(own_key, dims, jnp.float32) * spread
    if len(cuts) > 0:
        values = block_levels(own_key, dims, cuts, -0.22, 0.18) * values
    return jnp.clip(values, min=-reach, max=reach).astype(kind)


def setup_inputs(seed: int = 0) -> dict:
    streams_of = jax.random.split(jax.random.key(seed), 18)
    activations = noise(streams_of[0], (TOKENS, D), 1.0, 6.0, ((0, 32),))
    segment = draw_segment(jax.random.fold_in(streams_of[17], 71), 0)
    routes_keys = jax.random.split(jax.random.fold_in(streams_of[2], 1), TOKENS // TOK_DEV)
    routes_turns = jax.random.permutation(jax.random.fold_in(streams_of[2], 3), TOKENS // TOK_DEV)
    routes = jax.vmap(lambda own, number: assign_block(jax.random.fold_in(streams_of[2], 2), own, number, TOK_DEV, EXPERTS, TOPK, CAP, 1))(routes_keys, routes_turns).reshape((TOKENS, TOPK))
    gain_attention = jnp.clip(1.0 + 0.1 * jax.random.normal(streams_of[3], (D,), jnp.float32), 0.5, 1.5).astype(jnp.bfloat16)
    query_weight = noise(streams_of[4], (D, D), D ** -0.5, 0.15625, ((0, 32),))
    key_weight = noise(streams_of[5], (D, D), D ** -0.5, 0.15625, ((0, 32),))
    value_weight = noise(streams_of[6], (D, D), D ** -0.5, 0.15625, ((0, 32),))
    output_weight = noise(streams_of[7], (D, D), (max(D // 1024, 1)) ** -0.5, 6.0, ((0, 32),))
    gain_experts = jnp.clip(1.0 + 0.1 * jax.random.normal(streams_of[8], (D,), jnp.float32), 0.5, 1.5).astype(jnp.bfloat16)
    router_weight = noise(streams_of[9], (D, EXPERTS), (4 * D) ** -0.5, 0.078125, ((0, 32),))
    shared_gate = noise(streams_of[10], (D, FF), D ** -0.5, 0.15625, ((0, 32),))
    shared_up = noise(streams_of[11], (D, FF), D ** -0.5, 0.15625, ((0, 32),))
    shared_down = noise(streams_of[12], (FF, D), FF ** -0.5, 0.1875, ((0, 32),))
    expert_gate = noise(streams_of[13], (EXPERTS, D, FF), D ** -0.5, 0.15625, ((0, 4),))
    expert_up = noise(streams_of[14], (EXPERTS, D, FF), D ** -0.5, 0.15625, ((0, 4),))
    expert_down = noise(streams_of[15], (EXPERTS, FF, D), (max(FF * 4 // (EXPERTS * EXPERTS), 1)) ** -0.5, 1.5, ((0, 4),))
    cotangent = noise(streams_of[16], (TOKENS, D), 1.0, 6.0, ((0, 32),))
    return dict(activations=activations, segment=segment, routes=routes, gain_attention=gain_attention, query_weight=query_weight, key_weight=key_weight, value_weight=value_weight, output_weight=output_weight, gain_experts=gain_experts, router_weight=router_weight, shared_gate=shared_gate, shared_up=shared_up, shared_down=shared_down, expert_gate=expert_gate, expert_up=expert_up, expert_down=expert_down, cotangent=cotangent)


@jax.custom_vjp
def low(v):
    return lax.optimization_barrier(v.astype(jnp.bfloat16)).astype(jnp.float32)

@jax.custom_vjp
def low_back(v):
    return v

def low_keep(v):
    return (low(v), None)

def low_pass(kept, grad):
    return (grad,)

def back_keep(v):
    return (v, None)

def back_low(kept, grad):
    return (low(grad),)
low.defvjp(low_keep, low_pass)
low_back.defvjp(back_keep, back_low)
epsilon = 1e-06
highest = lax.Precision.HIGHEST
masked_value = -1e+30

def matmul(left, right):
    return jnp.dot(left, right, precision=highest, preferred_element_type=jnp.float32)

def rms_norm(values, gain):
    inverse = lax.rsqrt(lax.optimization_barrier(jnp.mean(values * values, axis=-1, keepdims=True)) + epsilon)
    return values * inverse * gain

def group_attention(operands):
    queries, keys_in, values_in, labels = operands
    length = queries.shape[0]
    query_heads = queries.reshape(length, HEADS, HD)
    key_heads = keys_in.reshape(length, HEADS, HD)
    value_heads = values_in.reshape(length, HEADS, HD)
    scores = jnp.einsum('qhd,khd->hqk', query_heads, key_heads, precision=highest) * HD ** (-0.5)
    scores = low_back(scores)
    places = jnp.arange(length, dtype=jnp.int32)
    allowed = (labels[:, None] == labels[None, :]) & (places[:, None] >= places[None, :])
    scores = jnp.where(allowed[None, :, :], scores, masked_value)
    weights = jax.nn.softmax(scores, axis=-1)
    mixed = jnp.einsum('hqk,khd->qhd', low(weights), value_heads, precision=highest)
    return low(low_back(mixed.reshape(length, HEADS * HD)))

def reference(activations, segment, routes, gain_attention, query_weight, key_weight, value_weight, output_weight, gain_experts, router_weight, shared_gate, shared_up, shared_down, expert_gate, expert_up, expert_down, cotangent):
    blocks = N_WIDE * N_EP
    column = blocks * CAP
    block_routes = routes.reshape(blocks, TOK_DEV * TOPK).astype(jnp.int32)
    numbers = jnp.arange(EXPERTS, dtype=jnp.int32)
    marks = (block_routes[:, :, None] == numbers[None, None, :]).astype(jnp.int32)
    earlier = jnp.cumsum(marks, axis=1) - marks
    slots = lax.optimization_barrier(jnp.sum(earlier * marks, axis=-1)).astype(jnp.int32)
    places = (jnp.arange(blocks, dtype=jnp.int32)[:, None] * CAP + slots).astype(jnp.int32)
    sources = jnp.repeat(jnp.arange(TOKENS, dtype=jnp.int32), TOPK).reshape(blocks, TOK_DEV * TOPK)
    table = jnp.zeros((EXPERTS, column), jnp.int32).at[block_routes, places].set(sources)
    filled = jnp.zeros((EXPERTS, column), jnp.float32).at[block_routes, places].set(1.0)
    lookup = (block_routes * column + places).reshape(TOKENS, TOPK).astype(jnp.int32)
    counts = lax.optimization_barrier(jnp.sum(marks, axis=(0, 1))).astype(jnp.int32)
    labels = segment.reshape(N_WIDE, GROUP)

    def forward(inputs, gain_one, w_query, w_key, w_value, w_out, gain_two, w_router, s_gate, s_up, s_down, e_gate, e_up, e_down):
        normed = low(rms_norm(inputs, gain_one))
        queries = low(low_back(matmul(normed, w_query)))
        keys_all = low(low_back(matmul(normed, w_key)))
        values_all = low(low_back(matmul(normed, w_value)))
        group_shape = (N_WIDE, GROUP, HEADS * HD)
        attended = lax.map(jax.checkpoint(group_attention), (queries.reshape(group_shape), keys_all.reshape(group_shape), values_all.reshape(group_shape), labels))
        middle = inputs + low_back(matmul(attended.reshape(TOKENS, D), w_out))
        normed_two = low(rms_norm(middle, gain_two))
        router_probs = jax.nn.softmax(matmul(normed_two, w_router), axis=-1)
        gates = jnp.take_along_axis(router_probs, routes, axis=1)
        shared_gate_act = low_back(matmul(normed_two, s_gate))
        shared_up_act = low_back(matmul(normed_two, s_up))
        shared_out = matmul(low(jax.nn.silu(shared_gate_act) * shared_up_act), s_down)

        def expert_rows(operands):
            row_index, row_live, gate_w, up_w, down_w = operands
            picked = low_back(normed_two[row_index]) * row_live[:, None]
            gate_act = low_back(matmul(picked, gate_w))
            up_act = low_back(matmul(picked, up_w))
            hidden = low(jax.nn.silu(gate_act) * up_act)
            return low(low_back(matmul(hidden, down_w)))
        produced = lax.map(jax.checkpoint(expert_rows), (table, filled, e_gate, e_up, e_down)).reshape(EXPERTS * column, D)
        routed = jnp.zeros((TOKENS, D), jnp.float32)
        for pick_index in range(TOPK):
            routed = routed + gates[:, pick_index:pick_index + 1] * produced[lookup[:, pick_index]]
        return middle + shared_out + routed
    primals = (activations.astype(jnp.float32), gain_attention.astype(jnp.float32), query_weight.astype(jnp.float32), key_weight.astype(jnp.float32), value_weight.astype(jnp.float32), output_weight.astype(jnp.float32), gain_experts.astype(jnp.float32), router_weight.astype(jnp.float32), shared_gate.astype(jnp.float32), shared_up.astype(jnp.float32), shared_down.astype(jnp.float32), expert_gate.astype(jnp.float32), expert_up.astype(jnp.float32), expert_down.astype(jnp.float32))
    result, pullback = jax.vjp(forward, *primals)
    grads = pullback(cotangent.astype(jnp.float32))
    return (result.astype(jnp.bfloat16), grads[0], grads[1], grads[2], grads[3], grads[4], grads[5], grads[6], grads[7], grads[8], grads[9], grads[10], grads[11], grads[12], grads[13], counts)
```

```python
import functools

import jax
import jax.numpy as jnp
from jax import lax
from jax.sharding import PartitionSpec as P

HD = 128
NC = 2
NZ = 4
ZP = 2
epsilon = 1e-06
masked_value = -1e30
BOTH = ("wide", "ep")
f32 = jnp.float32
bf16 = jnp.bfloat16


def contract_rows(left, right):
    return lax.dot_general(
        left, right, (((0,), (0,)), ((), ())), preferred_element_type=f32
    )


def times_transposed(left, right):
    return lax.dot_general(
        left, right, (((1,), (1,)), ((), ())), preferred_element_type=f32
    )


def times(left, right):
    return jnp.dot(left, right, preferred_element_type=f32)


def norm_scale(values):
    return lax.rsqrt(jnp.mean(values * values, axis=-1, keepdims=True) + epsilon)


def norm_backward(values, inverse, gain, normed_grad):
    weighted = normed_grad * gain
    gain_grad = jnp.sum(normed_grad * values * inverse, axis=0)
    cubed = inverse * inverse * inverse
    values_grad = inverse * weighted - values * cubed * jnp.mean(
        weighted * values, axis=-1, keepdims=True
    )
    return (gain_grad, values_grad)


def silu_parts(gate_act):
    logistic = jax.nn.sigmoid(gate_act)
    return (gate_act * logistic, logistic * (1.0 + gate_act * (1.0 - logistic)))


class Grid:
    def __init__(self, wide, ep):
        self.ny, self.nx, self.ep = wide // NZ, ep // NC, ep
        w, e = lax.axis_index("wide"), lax.axis_index("ep")
        self.z, self.y, self.x, self.c = w // self.ny, w % self.ny, e // NC, e % NC
        self.zm = self.z % ZP

    def pairs(self, move):
        made = []
        for z in range(NZ):
            for y in range(self.ny):
                for x in range(self.nx):
                    for c in range(NC):
                        tz, ty, tx, tc = move(z, y, x, c)
                        made.append(
                            (
                                (z * self.ny + y) * self.ep + x * NC + c,
                                (tz * self.ny + ty) * self.ep + tx * NC + tc,
                            )
                        )
        return made

    def send(self, value, axis, step):
        moves = {
            "c": lambda z, y, x, c: (z, y, x, (c + step) % NC),
            "x": lambda z, y, x, c: (z, y, (x + step) % self.nx, c),
            "y": lambda z, y, x, c: (z, (y + step) % self.ny, x, c),
            "z": lambda z, y, x, c: ((z + step) % NZ, y, x, c),
            "p": lambda z, y, x, c: (z // ZP * ZP + (z % ZP + step) % ZP, y, x, c),
        }
        return lax.ppermute(value, BOTH, self.pairs(moves[axis]))

    def size(self, axis):
        return {"c": NC, "x": self.nx, "y": self.ny, "z": NZ, "p": ZP}[axis]

    def place(self, axis):
        return {"c": self.c, "x": self.x, "y": self.y, "z": self.z, "p": self.zm}[axis]

    def gather(self, value, axis, at):
        parts = [value] + [
            self.send(value, axis, -d) for d in range(1, self.size(axis))
        ]
        return jnp.stack(parts, axis=at)

    def scatter(self, value, axis, at):
        total = lax.index_in_dim(value, 0, at, keepdims=False).astype(f32)
        for d in range(1, self.size(axis)):
            part = lax.index_in_dim(value, d, at, keepdims=False)
            total = total + self.send(part, axis, d).astype(f32)
        return total.astype(value.dtype)

    def scatter_absolute(self, value, axis, at):
        n, me = self.size(axis), self.place(axis)
        take = lambda i: lax.dynamic_index_in_dim(value, i, at, keepdims=False)
        total = take(me).astype(f32)
        for d in range(1, n):
            total = total + self.send(take((me + d) % n), axis, d).astype(f32)
        return total.astype(value.dtype)


def attention_bias(segment, labels_all, query_places, key_places):
    same_doc = segment[:, None] == labels_all[None, :]
    allowed = same_doc & (query_places[:, None] >= key_places[None, :])
    return jnp.where(allowed, 0.0, masked_value).astype(f32)


def make_probs(query_heads, key_heads, bias):
    scores = (
        jnp.einsum("qhd,khd->hqk", query_heads, key_heads, preferred_element_type=f32)
        * HD ** (-0.5)
    )
    scores = scores + bias[None]
    largest = jnp.max(scores, axis=-1, keepdims=True)
    weights = jnp.exp(scores - largest)
    return weights * (1.0 / jnp.sum(weights, axis=-1, keepdims=True))


def reduce_dense(grid, value, order):
    names = ["z", "y", "x", "c"]
    for axis in order:
        at = names.index(axis)
        value = grid.scatter_absolute(value, axis, at)
        names.pop(at)
    return value


def reduce_experts(grid, value):
    mine, rows, columns = value.shape
    value = value.reshape(mine, NZ, grid.ny, rows // (NZ * grid.ny), columns)
    value = grid.scatter_absolute(value, "y", 2)
    take = lambda i: lax.dynamic_index_in_dim(value, i, 1, keepdims=False)
    sums = [take(grid.z).astype(f32), None]
    for d in range(1, NZ):
        got = grid.send(take((grid.z + d) % NZ), "z", d).astype(f32)
        sums[d % ZP] = got if sums[d % ZP] is None else sums[d % ZP] + got
    first = jnp.where(grid.zm == 0, sums[0], sums[1])
    second = jnp.where(grid.zm == 0, sums[1], sums[0])
    return jnp.concatenate([first, second], axis=0)


def body(
    wide,
    ep,
    activations,
    segment,
    routes,
    gain_attention,
    query_weight,
    key_weight,
    value_weight,
    output_weight,
    gain_experts,
    router_weight,
    shared_gate,
    shared_up,
    shared_down,
    expert_gate,
    expert_up,
    expert_down,
    cotangent,
):
    grid = Grid(wide, ep)
    nx, ny = grid.nx, grid.ny
    tok_rows, width = activations.shape
    heads = width // HD
    top_count = routes.shape[1]
    experts = router_weight.shape[1]
    local_experts = expert_gate.shape[0]
    mine = local_experts // ZP
    hidden_width = expert_gate.shape[2]
    sources = ZP * nx * NC
    capacity = min((tok_rows * top_count * 10 // (7 * experts) + 7) // 8 * 8, tok_rows)

    small = jnp.concatenate(
        [
            router_weight,
            gain_attention[:, None],
            gain_experts[:, None],
            jnp.zeros((gain_experts.shape[0], 128 - experts - 2), bf16),
        ],
        axis=1,
    )
    gather_all = lambda v: lax.all_gather(v, BOTH, axis=0, tiled=True)
    small_all = gather_all(small)
    w_query = gather_all(query_weight)
    w_key = gather_all(key_weight)
    w_value = gather_all(value_weight)
    w_out = gather_all(output_weight)
    s_gate = gather_all(shared_gate)
    s_up = gather_all(shared_up)
    s_down = gather_all(shared_down)
    w_router = small_all[:, :experts]
    gain_one = small_all[:, experts].astype(f32)
    gain_two = small_all[:, experts + 1].astype(f32)

    def gather_group(v):
        return grid.gather(grid.gather(v, "c", 0), "x", 0)

    def gather_pair(v):
        return grid.gather(gather_group(v), "p", 0)

    integers = jnp.concatenate([routes.T, segment[None, :]], axis=0)
    integers_all = gather_pair(integers).reshape(sources, top_count + 1, tok_rows)
    group_rows = gather_group(activations).reshape(nx * NC * tok_rows, width)
    cot_all = gather_pair(cotangent).reshape(sources, tok_rows, width)

    inputs = activations.astype(f32)
    inverse_one = norm_scale(inputs)
    group_inputs = group_rows.astype(f32)
    normed_group = (group_inputs * norm_scale(group_inputs) * gain_one).astype(bf16)
    normed_one = normed_group[:tok_rows]
    queries = times(normed_one, w_query).astype(bf16)
    keys_all = times(normed_group, w_key).astype(bf16)
    values_all = times(normed_group, w_value).astype(bf16)
    labels_all = integers_all[: nx * NC, top_count].reshape(-1)
    steps = jnp.arange(tok_rows, dtype=jnp.int32)
    block_places = (
        (grid.x + jnp.arange(nx, dtype=jnp.int32)[:, None]) % nx * NC
        + (grid.c + jnp.arange(NC, dtype=jnp.int32)[None, :]) % NC
    ).reshape(-1)
    key_places = (block_places[:, None] * tok_rows + steps[None, :]).reshape(-1)
    query_places = (grid.x * NC + grid.c) * tok_rows + steps
    bias = attention_bias(segment, labels_all, query_places, key_places)
    query_heads = queries.reshape(-1, heads, HD)
    key_heads = keys_all.reshape(-1, heads, HD)
    value_heads = values_all.reshape(-1, heads, HD)
    probs = make_probs(query_heads, key_heads, bias)
    attended = (
        jnp.einsum(
            "hqk,khd->qhd", probs.astype(bf16), value_heads, preferred_element_type=f32
        )
        .reshape(tok_rows, width)
        .astype(bf16)
    )
    middle = inputs + times(attended, w_out)
    inverse_two = norm_scale(middle)
    normed_two = (middle * inverse_two * gain_two).astype(bf16)

    rows_all = gather_pair(normed_two).reshape(sources, tok_rows, width)
    router_probs_all = jax.nn.softmax(
        times(rows_all.reshape(-1, width), w_router).reshape(sources, tok_rows, experts),
        axis=-1,
    )
    router_probs = router_probs_all[0]
    first_expert = (grid.x * NC + grid.c) * local_experts + grid.zm * mine
    routes_all = integers_all[:, :top_count]
    numbers = first_expert + jnp.arange(mine, dtype=jnp.int32)
    marks = jnp.any(
        routes_all[None] == numbers[:, None, None, None], axis=2
    )
    earlier = (steps[:, None] < steps[None, :]).astype(bf16)
    ranks = jnp.einsum(
        "irt,tu->iru", marks.astype(bf16), earlier, preferred_element_type=f32
    ).astype(jnp.int32)
    slots = jnp.arange(capacity, dtype=jnp.int32)
    chosen = marks[:, :, None, :] & (ranks[:, :, None, :] == slots[None, None, :, None])
    picks = chosen.astype(bf16)
    gates_mine = jnp.moveaxis(
        lax.dynamic_slice_in_dim(router_probs_all, first_expert, mine, axis=2), 2, 0
    )
    gate_rows = jnp.sum(
        jnp.where(chosen, gates_mine[:, :, None, :], 0.0), axis=-1
    ).reshape(mine, sources * capacity, 1)
    out_parts = 0.0
    row_parts = 0.0
    prob_parts = []
    gate_w_grads, up_w_grads, down_w_grads = [], [], []
    w_gates = lax.dynamic_slice_in_dim(expert_gate, grid.zm * mine, mine, axis=0)
    w_ups = lax.dynamic_slice_in_dim(expert_up, grid.zm * mine, mine, axis=0)
    w_downs = lax.dynamic_slice_in_dim(expert_down, grid.zm * mine, mine, axis=0)
    for i in range(mine):
        pick = lambda v: (
            jnp.einsum("rst,rtd->rsd", picks[i], v, preferred_element_type=f32)
            .astype(bf16)
            .reshape(sources * capacity, width)
        )
        unpick = lambda v: jnp.einsum(
            "rst,rsd->rtd",
            picks[i],
            v.reshape(sources, capacity, width),
            preferred_element_type=f32,
        )
        rows_here = pick(rows_all)
        cot_here = pick(cot_all).astype(f32)
        slot_here = (gate_rows[i] * cot_here).astype(bf16)
        gate_act = times(rows_here, w_gates[i])
        up_act = times(rows_here, w_ups[i])
        activated, slope = silu_parts(gate_act)
        hidden = (activated * up_act).astype(bf16)
        produced = times(hidden, w_downs[i]).astype(bf16).astype(f32)
        row_probs = jnp.sum(produced * cot_here, axis=-1).reshape(sources, capacity, 1)
        prob_parts.append(jnp.sum(jnp.where(chosen[i], row_probs, 0.0), axis=1))
        out_parts = out_parts + unpick((gate_rows[i] * produced).astype(bf16))
        hidden_grad = times_transposed(slot_here, w_downs[i])
        act_gate = (hidden_grad * up_act * slope).astype(bf16)
        act_up = (hidden_grad * activated).astype(bf16)
        down_w_grads.append(contract_rows(hidden, slot_here).astype(bf16))
        gate_w_grads.append(contract_rows(rows_here, act_gate).astype(bf16))
        up_w_grads.append(contract_rows(rows_here, act_up).astype(bf16))
        row_grad = (
            times_transposed(act_gate, w_gates[i]) + times_transposed(act_up, w_ups[i])
        ).astype(bf16)
        row_parts = row_parts + unpick(row_grad)

    def scatter_pair(v):
        v = v.reshape((ZP, nx, NC) + v.shape[1:])
        return grid.scatter(grid.scatter(grid.scatter(v, "c", 2), "x", 1), "p", 0)

    routed_grad = scatter_pair(row_parts.astype(bf16)).astype(f32)
    routed = scatter_pair(out_parts.astype(bf16)).astype(f32)
    expert_down_grad = reduce_experts(grid, jnp.stack(down_w_grads))
    expert_gate_grad = reduce_experts(grid, jnp.stack(gate_w_grads))
    expert_up_grad = reduce_experts(grid, jnp.stack(up_w_grads))
    sent = jnp.stack(prob_parts, axis=1).reshape(ZP, nx, NC, mine, tok_rows)
    for axis, at in (("c", 2), ("x", 1), ("p", 0)):
        n = grid.size(axis)
        parts = [lax.index_in_dim(sent, d, at, keepdims=False) for d in range(n)]
        got = [parts[0]] + [grid.send(parts[n - d], axis, n - d) for d in range(1, n)]
        sent = jnp.stack(got, axis=at)
    dz = (grid.zm + jnp.arange(ZP, dtype=jnp.int32)) % ZP
    owner = block_places.reshape(1, nx, NC, 1) * local_experts
    owner = owner + dz[:, None, None, None] * mine + jnp.arange(mine, dtype=jnp.int32)
    same = owner.reshape(-1)[None, :] == jnp.arange(experts, dtype=jnp.int32)[:, None]
    prob_grad = jnp.sum(
        jnp.where(same[:, :, None], sent.reshape(1, experts, tok_rows), 0.0), axis=1
    ).T

    shared_gate_act = times(normed_two, s_gate)
    shared_up_act = times(normed_two, s_up)
    shared_act, shared_slope = silu_parts(shared_gate_act)
    shared_hidden = (shared_act * shared_up_act).astype(bf16)
    shared_out = times(shared_hidden, s_down)
    out_grad = cotangent.astype(f32)
    shared_down_grad = contract_rows(shared_hidden, cotangent)
    shared_hidden_grad = times_transposed(cotangent, s_down)
    shared_gate_act_grad = (shared_hidden_grad * shared_up_act * shared_slope).astype(
        bf16
    )
    shared_up_act_grad = (shared_hidden_grad * shared_act).astype(bf16)
    shared_gate_grad = contract_rows(normed_two, shared_gate_act_grad)
    shared_up_grad = contract_rows(normed_two, shared_up_act_grad)
    normed_two_grad = times_transposed(shared_gate_act_grad, s_gate) + times_transposed(
        shared_up_act_grad, s_up
    )
    block_out = (middle + shared_out + routed).astype(bf16)

    logit_grad = router_probs * (
        prob_grad - jnp.sum(router_probs * prob_grad, axis=-1, keepdims=True)
    )
    router_grad = lax.dot_general(
        normed_two.astype(f32),
        logit_grad,
        (((0,), (0,)), ((), ())),
        precision=lax.Precision.HIGHEST,
        preferred_element_type=f32,
    )
    normed_two_grad = (
        normed_two_grad
        + routed_grad
        + lax.dot_general(
            logit_grad,
            w_router.astype(f32),
            (((1,), (1,)), ((), ())),
            precision=lax.Precision.HIGHEST,
            preferred_element_type=f32,
        )
    )
    gain_two_grad, middle_part = norm_backward(
        middle, inverse_two, gain_two, normed_two_grad
    )
    middle_grad = out_grad + middle_part
    branch_grad = middle_grad.astype(bf16)
    output_weight_grad = contract_rows(attended, branch_grad)
    attended_grad = times_transposed(branch_grad, w_out).astype(bf16)

    grad_heads = attended_grad.reshape(tok_rows, heads, HD)
    prob_grad_att = jnp.einsum(
        "qhd,khd->hqk", grad_heads, value_heads, preferred_element_type=f32
    )
    centre = jnp.sum(probs * prob_grad_att, axis=-1, keepdims=True)
    score_grad = (probs * (prob_grad_att - centre)).astype(bf16)
    query_act_grad = (
        (
            jnp.einsum("hqk,khd->qhd", score_grad, key_heads, preferred_element_type=f32)
            * HD ** (-0.5)
        )
        .reshape(tok_rows, width)
        .astype(bf16)
    )
    key_part = (
        jnp.einsum("hqk,qhd->khd", score_grad, query_heads, preferred_element_type=f32)
        * HD ** (-0.5)
    )
    value_part = jnp.einsum(
        "hqk,qhd->khd", probs.astype(bf16), grad_heads, preferred_element_type=f32
    )

    def scatter_group(v):
        v = v.astype(bf16).reshape(nx, NC, tok_rows, width)
        return grid.scatter(grid.scatter(v, "c", 1), "x", 0)

    value_act_grad = scatter_group(value_part)
    key_act_grad = scatter_group(key_part)
    query_w_grad = contract_rows(normed_one, query_act_grad)
    key_w_grad = contract_rows(normed_one, key_act_grad)
    value_w_grad = contract_rows(normed_one, value_act_grad)
    normed_one_grad = (
        times_transposed(query_act_grad, w_query)
        + times_transposed(key_act_grad, w_key)
        + times_transposed(value_act_grad, w_value)
    )
    gain_one_grad, input_part = norm_backward(
        inputs, inverse_one, gain_one, normed_one_grad
    )
    input_grad = middle_grad + input_part

    def by_place(v):
        return v.reshape((NZ, ny, nx, NC, v.shape[0] // (wide * ep)) + v.shape[1:])

    def reduce_all(v, order):
        return reduce_dense(grid, by_place(v.astype(bf16)), order).astype(f32)

    output_weight_sum = reduce_all(output_weight_grad, "cxyz")
    shared_gate_sum = reduce_all(shared_gate_grad, "cyxz")
    shared_up_sum = reduce_all(shared_up_grad, "cxyz")
    shared_down_sum = reduce_all(shared_down_grad, "cyxz")
    query_sum = reduce_all(query_w_grad, "cxyz")
    key_sum = reduce_all(key_w_grad, "cyxz")
    value_sum = reduce_all(value_w_grad, "cxyz")
    counts = jnp.sum(
        (routes[:, :, None] == jnp.arange(experts, dtype=jnp.int32)).astype(f32),
        axis=(0, 1),
    )
    share = gain_attention.shape[0]
    count_block = jnp.pad(
        jnp.tile(counts.reshape(1, ep, 1, local_experts), (wide, 1, 1, 1)),
        ((0, 0), (0, 0), (0, 0), (0, 128 - local_experts)),
    )
    extras = jnp.concatenate(
        [
            router_grad,
            gain_one_grad[:, None],
            gain_two_grad[:, None],
            jnp.zeros((width, 128 - experts - 2), f32),
        ],
        axis=1,
    ).reshape(wide, ep, share, 128)
    extras = jnp.concatenate(
        [extras, count_block, jnp.zeros((wide, ep, 7, 128), f32)], axis=2
    )
    extra_sum = lax.psum_scatter(
        extras.reshape(wide * ep, share + 8, 128),
        BOTH,
        scatter_dimension=0,
        tiled=True,
    )[0]
    return (
        block_out,
        input_grad,
        extra_sum[:share, experts],
        query_sum,
        key_sum,
        value_sum,
        output_weight_sum,
        extra_sum[:share, experts + 1],
        extra_sum[:share, :experts],
        shared_gate_sum,
        shared_up_sum,
        shared_down_sum,
        expert_gate_grad,
        expert_up_grad,
        expert_down_grad,
        extra_sum[share, :local_experts].astype(jnp.int32),
    )


def solution(mesh):
    split = P(BOTH, None)
    line = P(BOTH)
    held = P("ep", None, None)
    out_held = P("ep", "wide", None)
    in_specs = (
        (split, line, split, line)
        + (split,) * 4
        + (line,)
        + (split,) * 4
        + (held,) * 3
        + (split,)
    )
    out_specs = (
        (split, split, line)
        + (split,) * 4
        + (line,)
        + (split,) * 4
        + (out_held,) * 3
        + (P("ep"),)
    )
    return jax.shard_map(
        functools.partial(body, mesh.shape["wide"], mesh.shape["ep"]),
        mesh=mesh,
        in_specs=in_specs,
        out_specs=out_specs,
        check_vma=False,
    )
```

```python
import functools

import jax
import jax.numpy as jnp
from jax import lax
from jax.experimental import pallas as pl
from jax.experimental.pallas import tpu as pltpu
from jax.sharding import PartitionSpec as P

HD = 128
NC = 2
NZ = 4
ZP = 2
epsilon = 1e-06
masked_value = -1e30
BOTH = ("wide", "ep")
f32 = jnp.float32
bf16 = jnp.bfloat16


def contract_rows(left, right):
    return lax.dot_general(
        left, right, (((0,), (0,)), ((), ())), preferred_element_type=f32
    )


def times_transposed(left, right):
    return lax.dot_general(
        left, right, (((1,), (1,)), ((), ())), preferred_element_type=f32
    )


def times(left, right):
    return jnp.dot(left, right, preferred_element_type=f32)


def norm_scale(values):
    return lax.rsqrt(jnp.mean(values * values, axis=-1, keepdims=True) + epsilon)


def norm_backward(values, inverse, gain, normed_grad):
    weighted = normed_grad * gain
    gain_grad = jnp.sum(normed_grad * values * inverse, axis=0)
    cubed = inverse * inverse * inverse
    values_grad = inverse * weighted - values * cubed * jnp.mean(
        weighted * values, axis=-1, keepdims=True
    )
    return (gain_grad, values_grad)


def silu_parts(gate_act):
    logistic = jax.nn.sigmoid(gate_act)
    return (gate_act * logistic, logistic * (1.0 + gate_act * (1.0 - logistic)))


class Grid:
    def __init__(self, wide, ep):
        self.ny, self.nx, self.ep = wide // NZ, ep // NC, ep
        w, e = lax.axis_index("wide"), lax.axis_index("ep")
        self.z, self.y, self.x, self.c = w // self.ny, w % self.ny, e // NC, e % NC
        self.zm = self.z % ZP

    def pairs(self, move):
        made = []
        for z in range(NZ):
            for y in range(self.ny):
                for x in range(self.nx):
                    for c in range(NC):
                        tz, ty, tx, tc = move(z, y, x, c)
                        made.append(
                            (
                                (z * self.ny + y) * self.ep + x * NC + c,
                                (tz * self.ny + ty) * self.ep + tx * NC + tc,
                            )
                        )
        return made

    def send(self, value, axis, step):
        moves = {
            "c": lambda z, y, x, c: (z, y, x, (c + step) % NC),
            "x": lambda z, y, x, c: (z, y, (x + step) % self.nx, c),
            "y": lambda z, y, x, c: (z, (y + step) % self.ny, x, c),
            "z": lambda z, y, x, c: ((z + step) % NZ, y, x, c),
            "p": lambda z, y, x, c: (z // ZP * ZP + (z % ZP + step) % ZP, y, x, c),
        }
        return lax.ppermute(value, BOTH, self.pairs(moves[axis]))

    def size(self, axis):
        return {"c": NC, "x": self.nx, "y": self.ny, "z": NZ, "p": ZP}[axis]

    def place(self, axis):
        return {"c": self.c, "x": self.x, "y": self.y, "z": self.z, "p": self.zm}[axis]

    def gather(self, value, axis, at):
        parts = [value] + [
            self.send(value, axis, -d) for d in range(1, self.size(axis))
        ]
        return jnp.stack(parts, axis=at)

    def scatter(self, value, axis, at):
        total = lax.index_in_dim(value, 0, at, keepdims=False).astype(f32)
        for d in range(1, self.size(axis)):
            part = lax.index_in_dim(value, d, at, keepdims=False)
            total = total + self.send(part, axis, d).astype(f32)
        return total.astype(value.dtype)

    def scatter_absolute(self, value, axis, at):
        n, me = self.size(axis), self.place(axis)
        take = lambda i: lax.dynamic_index_in_dim(value, i, at, keepdims=False)
        total = take(me).astype(f32)
        for d in range(1, n):
            total = total + self.send(take((me + d) % n), axis, d).astype(f32)
        return total.astype(value.dtype)


def gather_kernel(
    grid_of,
    cut,
    w_ref,
    rows_ref,
    ints_ref,
    w_all,
    rows_all,
    ints_all,
    plane_sem,
    core_sem,
    rows_sem,
    ints_sem,
    send_sem,
    local_sem,
):
    grid = grid_of()
    z, y, x, c, nx, ny = grid.z, grid.y, grid.x, grid.c, grid.nx, grid.ny
    width = w_ref.shape[1]

    def device(tz, ty, tx, tc):
        return (tz * ny + ty, tx * NC + tc)

    def slot(tz, ty, tx, tc):
        return (tz * ny + ty) * (nx * NC) + tx * NC + tc

    shift_z = lambda d: (z + d) % NZ
    shift_p = lambda d: z // ZP * ZP + (z % ZP + d) % ZP
    shift_y = lambda d: (y + d) % ny
    shift_x = lambda d: (x + d) % nx
    other = (c + 1) % NC
    octet = [
        (dz, dx, dc)
        for dz in range(ZP)
        for dx in range(nx)
        for dc in range(NC)
        if (dz, dx, dc) != (0, 0, 0)
    ]

    barrier = pltpu.get_barrier_semaphore()
    greeted = (
        [device(shift_z(d), y, x, c) for d in range(1, NZ)]
        + [device(z, shift_y(d), x, c) for d in range(1, ny)]
        + [device(shift_p(a), y, shift_x(b), (c + e) % NC) for a, b, e in octet]
    )
    for target in greeted:
        pl.semaphore_signal(
            barrier, inc=1, device_id=target, device_id_type=pl.DeviceIdType.MESH
        )
    pl.semaphore_wait(barrier, len(greeted))

    started = []

    def send(src, dst, sem, target):
        copy = pltpu.make_async_remote_copy(
            src_ref=src,
            dst_ref=dst,
            send_sem=send_sem.at[len(started)],
            recv_sem=sem,
            device_id=target,
            device_id_type=pl.DeviceIdType.MESH,
        )
        copy.start()
        started.append(copy)

    def arrived(dst, sem):
        pltpu.make_async_copy(dst, dst, sem).wait()

    half = (pl.ds(0, cut), pl.ds(cut, width - cut))
    block = lambda dz, dy, dx, tc: w_all.at[
        slot(shift_z(-dz), shift_y(-dy), shift_x(-dx), tc)
    ]

    own = pltpu.make_async_copy(w_ref, block(0, 0, 0, c), local_sem)
    own.start()
    my_slot = w_all.at[slot(z, y, x, c)]
    for d in range(1, nx):
        send(rows_ref, rows_all.at[nx - d, 0], rows_sem.at[nx - d, 0], device(z, y, shift_x(d), c))
    for d in range(1, NZ):
        send(w_ref, my_slot, plane_sem.at[d, 0, 0, 0], device(shift_z(d), y, x, c))
    send(rows_ref, rows_all.at[0, 1], rows_sem.at[0, 1], device(z, y, x, other))
    for a, b, e in octet:
        send(
            ints_ref,
            ints_all.at[(ZP - a) % ZP, (nx - b) % nx, e],
            ints_sem.at[(ZP - a) % ZP, (nx - b) % nx, e],
            device(shift_p(a), y, shift_x(b), (c + e) % NC),
        )

    def spread(src, dst, dz):
        for d in range(1, ny):
            send(src, dst, plane_sem.at[dz, d, 0, 0], device(z, shift_y(d), x, c))
        for d in range(1, nx):
            send(src, dst, plane_sem.at[dz, 0, d, 0], device(z, y, shift_x(d), c))
        send(src, dst, core_sem.at[dz, 0, 0], device(z, y, x, other))

    spread(w_ref, my_slot, 0)
    for d in range(1, NZ):
        here = block(d, 0, 0, c)
        arrived(here, plane_sem.at[d, 0, 0, 0])
        spread(here, here, d)
    for d in range(1, nx):
        arrived(rows_all.at[nx - d, 0], rows_sem.at[nx - d, 0])
        send(rows_all.at[nx - d, 0], rows_all.at[nx - d, 1], rows_sem.at[nx - d, 1], device(z, y, x, other))
    for dz in range(NZ):
        for dy in range(1, ny):
            here = block(dz, dy, 0, c)
            arrived(here, plane_sem.at[dz, dy, 0, 0])
            for d in range(1, nx):
                send(
                    here.at[:, half[0]],
                    here.at[:, half[0]],
                    plane_sem.at[dz, dy, d, 0],
                    device(z, y, shift_x(d), c),
                )
            send(here, here, core_sem.at[dz, dy, 0], device(z, y, x, other))
        for dx in range(1, nx):
            here = block(dz, 0, dx, c)
            arrived(here, plane_sem.at[dz, 0, dx, 0])
            for d in range(1, ny):
                send(
                    here.at[:, half[1]],
                    here.at[:, half[1]],
                    plane_sem.at[dz, d, dx, 1],
                    device(z, shift_y(d), x, c),
                )
            send(here, here, core_sem.at[dz, 0, dx], device(z, y, x, other))
    for dz in range(NZ):
        for dy in range(1, ny):
            for dx in range(1, nx):
                here = block(dz, dy, dx, c)
                for part in range(2):
                    arrived(here.at[:, half[part]], plane_sem.at[dz, dy, dx, part])
                send(here, here, core_sem.at[dz, dy, dx], device(z, y, x, other))
    for dx in range(nx):
        arrived(rows_all.at[dx, 1], rows_sem.at[dx, 1])
    for a, b, e in octet:
        arrived(ints_all.at[a, b, e], ints_sem.at[a, b, e])
    for dz in range(NZ):
        for dy in range(ny):
            for dx in range(nx):
                arrived(block(dz, dy, dx, other), core_sem.at[dz, dy, dx])
    own.wait()
    for copy in started:
        copy.wait_send()


def gather_first(grid_of, w, rows, ints):
    grid = grid_of()
    nx, ny = grid.nx, grid.ny
    places = NZ * ny * nx * NC
    cut = w.shape[1] // 2 // 128 * 128
    sends = (
        (nx - 1) * 2 + 1 + (NZ - 1) + (ZP * nx * NC - 1)
        + NZ * (ny + nx - 1)
        + NZ * ((ny - 1) * nx + (nx - 1) * ny + (ny - 1) * (nx - 1))
    )
    anywhere = pl.BlockSpec(memory_space=pl.ANY)
    dma = pltpu.SemaphoreType.DMA
    return pl.pallas_call(
        functools.partial(gather_kernel, grid_of, cut),
        out_shape=(
            jax.ShapeDtypeStruct((places,) + w.shape, w.dtype),
            jax.ShapeDtypeStruct((nx, NC) + rows.shape, rows.dtype),
            jax.ShapeDtypeStruct((ZP, nx, NC) + ints.shape, ints.dtype),
        ),
        in_specs=[anywhere] * 3,
        out_specs=(anywhere,) * 3,
        scratch_shapes=[
            dma((NZ, ny, nx, 2)),
            dma((NZ, ny, nx)),
            dma((nx, NC)),
            dma((ZP, nx, NC)),
            dma((sends,)),
            dma,
        ],
        compiler_params=pltpu.CompilerParams(collective_id=0, has_side_effects=True),
    )(w, rows, ints)


class Sender:
    def __init__(self, sems):
        self.sems, self.started = sems, []

    def __call__(self, src, dst, sem, target):
        copy = pltpu.make_async_remote_copy(
            src_ref=src,
            dst_ref=dst,
            send_sem=self.sems.at[len(self.started)],
            recv_sem=sem,
            device_id=target,
            device_id_type=pl.DeviceIdType.MESH,
        )
        copy.start()
        self.started.append(copy)

    def finish(self):
        for copy in self.started:
            copy.wait_send()


def arrived(dst, sem):
    pltpu.make_async_copy(dst, dst, sem).wait()


def greet(targets):
    barrier = pltpu.get_barrier_semaphore()
    for target in targets:
        pl.semaphore_signal(
            barrier, inc=1, device_id=target, device_id_type=pl.DeviceIdType.MESH
        )
    pl.semaphore_wait(barrier, len(targets))


def around(grid, zp):
    steps = [(a, b, e) for a in range(zp) for b in range(grid.nx) for e in range(NC)]
    return steps[1:]


def stepped(grid, zp, a, b, e):
    z = grid.z // zp * zp + (grid.z % zp + a) % zp
    return (
        z * grid.ny + grid.y,
        (grid.x + b) % grid.nx * NC + (grid.c + e) % NC,
    )


def exchange_kernel(grid_of, zp, cut, count, *refs):
    grid = grid_of()
    nx = grid.nx
    ins, outs = refs[:count], refs[count : 2 * count]
    plane_sem, core_sem, local_sem, send_sem = refs[2 * count :]
    send = Sender(send_sem)
    to = functools.partial(stepped, grid, zp)
    greet([to(*s) for s in around(grid, zp)])
    back = lambda d: (nx - d) % nx
    for k in range(count):
        src, out = ins[k], outs[k]
        for a in range(1, zp):
            send(src, out.at[zp - a, 0, 0], plane_sem.at[k, zp - a, 0, 0], to(a, 0, 0))
        for b in range(1, nx):
            send(src, out.at[0, back(b), 0], plane_sem.at[k, 0, back(b), 0], to(0, b, 0))
        send(src, out.at[0, 0, 1], core_sem.at[k, 0, 0], to(0, 0, 1))
        pltpu.make_async_copy(src, out.at[0, 0, 0], local_sem.at[k]).start()
    for k in range(count):
        out = outs[k]
        h0 = (slice(None), pl.ds(0, cut))
        h1 = (slice(None), pl.ds(cut, ins[k].shape[1] - cut))
        for a in range(1, zp):
            here = out.at[a, 0, 0]
            arrived(here, plane_sem.at[k, a, 0, 0])
            for b in range(1, nx):
                send(here.at[h0], out.at[a, back(b), 0].at[h0], plane_sem.at[k, a, back(b), 0], to(0, b, 0))
            send(here, out.at[a, 0, 1], core_sem.at[k, a, 0], to(0, 0, 1))
        for b in range(1, nx):
            here = out.at[0, b, 0]
            arrived(here, plane_sem.at[k, 0, b, 0])
            for a in range(1, zp):
                send(here.at[h1], out.at[zp - a, b, 0].at[h1], plane_sem.at[k, zp - a, b, 1], to(a, 0, 0))
            send(here, out.at[0, b, 1], core_sem.at[k, 0, b], to(0, 0, 1))
    for k in range(count):
        out = outs[k]
        h0 = (slice(None), pl.ds(0, cut))
        h1 = (slice(None), pl.ds(cut, ins[k].shape[1] - cut))
        for a in range(1, zp):
            for b in range(1, nx):
                here = out.at[a, b, 0]
                arrived(here.at[h0], plane_sem.at[k, a, b, 0])
                arrived(here.at[h1], plane_sem.at[k, a, b, 1])
                send(here, out.at[a, b, 1], core_sem.at[k, a, b], to(0, 0, 1))
    for k in range(count):
        for a in range(zp):
            for b in range(nx):
                arrived(outs[k].at[a, b, 1], core_sem.at[k, a, b])
        pltpu.make_async_copy(ins[k], outs[k].at[0, 0, 0], local_sem.at[k]).wait()
    send.finish()


def exchange(grid_of, zp, number, *arrays):
    grid = grid_of()
    nx = grid.nx
    count = len(arrays)
    sends = count * (zp * nx * 2 + zp * nx * nx * 2)
    anywhere = pl.BlockSpec(memory_space=pl.ANY)
    dma = pltpu.SemaphoreType.DMA
    return pl.pallas_call(
        functools.partial(
            exchange_kernel, grid_of, zp, arrays[0].shape[1] // 256 * 128, count
        ),
        out_shape=tuple(
            jax.ShapeDtypeStruct((zp, nx, NC) + v.shape, v.dtype) for v in arrays
        ),
        in_specs=[anywhere] * count,
        out_specs=(anywhere,) * count,
        scratch_shapes=[
            dma((count, zp, nx, 2)),
            dma((count, zp, nx)),
            dma((count,)),
            dma((sends,)),
        ],
        compiler_params=pltpu.CompilerParams(
            collective_id=number, has_side_effects=True
        ),
    )(*arrays)


def add_into(dst, src, rows):
    for k in range(dst.shape[0]):

        @pl.loop(0, dst.shape[1], step=rows)
        def _(i):
            at = pl.ds(pl.multiple_of(i, rows), rows)
            dst[k, at] = (dst[k, at].astype(f32) + src[k, at].astype(f32)).astype(
                dst.dtype
            )


def sum_kernel(grid_of, zp, cut, small, parts, *refs):
    grid = grid_of()
    nx = grid.nx
    if small:
        pieces, out, pieces_out = refs[:3]
        refs = refs[3:]
    else:
        out = refs[0]
        refs = refs[1:]
    own, got_c, turn_x, turn_p, got_p, got_x = refs[:6]
    local_sem, c_sem, turn_sem, p_sem, x_sem, small_sem, send_sem = refs[6:]
    send = Sender(send_sem)
    to = functools.partial(stepped, grid, zp)
    greet([to(*s) for s in around(grid, zp)])
    width = parts.shape[-1]
    h0, h1 = pl.ds(0, cut), pl.ds(cut, width - cut)
    order = (
        [(a, b) for a in range(1, zp) for b in range(1, nx)]
        + [(a, 0) for a in range(1, zp)]
        + [(0, b) for b in range(1, nx)]
        + [(0, 0)]
    )
    for a, b in order:
        send(parts.at[:, a, b, 1], got_c.at[:, a, b], c_sem.at[a, b], to(0, 0, 1))
        pltpu.make_async_copy(
            parts.at[:, a, b, 0], own.at[:, a, b], local_sem.at[a, b]
        ).start()
    if small:
        for a, b, e in around(grid, zp):
            mirror = ((zp - a) % zp, (nx - b) % nx, e)
            send(
                pieces.at[a, b, e],
                pieces_out.at[mirror],
                small_sem.at[mirror],
                to(a, b, e),
            )
        pltpu.make_async_copy(
            pieces.at[0, 0, 0], pieces_out.at[0, 0, 0], small_sem.at[0, 0, 0]
        ).start()
    rows = 32

    def ready(a, b):
        arrived(got_c.at[:, a, b], c_sem.at[a, b])
        pltpu.make_async_copy(
            parts.at[:, a, b, 0], own.at[:, a, b], local_sem.at[a, b]
        ).wait()
        add_into(own.at[:, a, b], got_c.at[:, a, b], rows)

    for a in range(1, zp):
        for b in range(1, nx):
            ready(a, b)
            send(own.at[:, a, b, :, h0], turn_x.at[:, a - 1, b - 1], turn_sem.at[a - 1, b - 1, 0], to(0, b, 0))
            send(own.at[:, a, b, :, h1], turn_p.at[:, a - 1, b - 1], turn_sem.at[a - 1, b - 1, 1], to(a, 0, 0))
    for a in range(1, zp):
        ready(a, 0)
    for b in range(1, nx):
        ready(0, b)
    for a in range(1, zp):
        for b in range(1, nx):
            arrived(turn_x.at[:, a - 1, b - 1], turn_sem.at[a - 1, b - 1, 0])
            add_into(own.at[:, a, 0, :, h0], turn_x.at[:, a - 1, b - 1], rows)
        send(own.at[:, a, 0], got_p.at[:, a - 1], p_sem.at[a - 1], to(a, 0, 0))
    for b in range(1, nx):
        for a in range(1, zp):
            arrived(turn_p.at[:, a - 1, b - 1], turn_sem.at[a - 1, b - 1, 1])
            add_into(own.at[:, 0, b, :, h1], turn_p.at[:, a - 1, b - 1], rows)
        send(own.at[:, 0, b], got_x.at[:, b - 1], x_sem.at[b - 1], to(0, b, 0))
    ready(0, 0)
    for a in range(1, zp):
        arrived(got_p.at[:, a - 1], p_sem.at[a - 1])
        add_into(own.at[:, 0, 0], got_p.at[:, a - 1], rows)
    for b in range(1, nx):
        arrived(got_x.at[:, b - 1], x_sem.at[b - 1])
        add_into(own.at[:, 0, 0], got_x.at[:, b - 1], rows)
    result = pltpu.make_async_copy(own.at[:, 0, 0], out, local_sem.at[0, 0])
    result.start()
    if small:
        for a, b, e in [(0, 0, 0)] + around(grid, zp):
            arrived(pieces_out.at[a, b, e], small_sem.at[a, b, e])
    result.wait()
    send.finish()


def sum_around(grid_of, zp, number, parts, pieces=None):
    grid = grid_of()
    nx = grid.nx
    payloads, rows, width = parts.shape[0], parts.shape[-2], parts.shape[-1]
    cut = width // 256 * 128
    anywhere = pl.BlockSpec(memory_space=pl.ANY)
    dma = pltpu.SemaphoreType.DMA
    small = pieces is not None
    out_shape = [jax.ShapeDtypeStruct((payloads, rows, width), parts.dtype)]
    args = [parts]
    if small:
        out_shape.append(jax.ShapeDtypeStruct(pieces.shape, pieces.dtype))
        args.append(pieces)
    turns = (max(zp - 1, 1), max(nx - 1, 1))
    vmem = lambda shape: pltpu.VMEM(shape, parts.dtype)
    made = pl.pallas_call(
        functools.partial(sum_kernel, grid_of, zp, cut, small),
        out_shape=tuple(out_shape),
        in_specs=[anywhere] * len(args),
        out_specs=(anywhere,) * len(args),
        scratch_shapes=[
            vmem((payloads, zp, nx, rows, width)),
            vmem((payloads, zp, nx, rows, width)),
            vmem((payloads,) + turns + (rows, cut)),
            vmem((payloads,) + turns + (rows, width - cut)),
            vmem((payloads, turns[0], rows, width)),
            vmem((payloads, turns[1], rows, width)),
            dma((zp, nx)),
            dma((zp, nx)),
            dma(turns + (2,)),
            dma((turns[0],)),
            dma((turns[1],)),
            dma((zp, nx, NC)),
            dma((zp * nx * 6 + 8,)),
        ],
        compiler_params=pltpu.CompilerParams(
            collective_id=number,
            has_side_effects=True,
            vmem_limit_bytes=56 * 2**20,
        ),
    )(*args)
    return made if small else made[0]


def attention_bias(segment, labels_all, query_places, key_places):
    same_doc = segment[:, None] == labels_all[None, :]
    allowed = same_doc & (query_places[:, None] >= key_places[None, :])
    return jnp.where(allowed, 0.0, masked_value).astype(f32)


def make_probs(query_heads, key_heads, bias):
    scores = (
        jnp.einsum("qhd,khd->hqk", query_heads, key_heads, preferred_element_type=f32)
        * HD ** (-0.5)
    )
    scores = scores + bias[None]
    largest = jnp.max(scores, axis=-1, keepdims=True)
    weights = jnp.exp(scores - largest)
    return weights * (1.0 / jnp.sum(weights, axis=-1, keepdims=True))


def reduce_dense(grid, value, order):
    names = ["z", "y", "x", "c"]
    for axis in order:
        at = names.index(axis)
        value = grid.scatter_absolute(value, axis, at)
        names.pop(at)
    return value


def reduce_experts(grid, value):
    mine, rows, columns = value.shape
    value = value.reshape(mine, NZ, grid.ny, rows // (NZ * grid.ny), columns)
    value = grid.scatter_absolute(value, "y", 2)
    take = lambda i: lax.dynamic_index_in_dim(value, i, 1, keepdims=False)
    sums = [take(grid.z).astype(f32), None]
    for d in range(1, NZ):
        got = grid.send(take((grid.z + d) % NZ), "z", d).astype(f32)
        sums[d % ZP] = got if sums[d % ZP] is None else sums[d % ZP] + got
    first = jnp.where(grid.zm == 0, sums[0], sums[1])
    second = jnp.where(grid.zm == 0, sums[1], sums[0])
    return jnp.concatenate([first, second], axis=0)


def body(
    wide,
    ep,
    activations,
    segment,
    routes,
    gain_attention,
    query_weight,
    key_weight,
    value_weight,
    output_weight,
    gain_experts,
    router_weight,
    shared_gate,
    shared_up,
    shared_down,
    expert_gate,
    expert_up,
    expert_down,
    cotangent,
):
    grid_of = functools.partial(Grid, wide, ep)
    grid = grid_of()
    nx, ny = grid.nx, grid.ny
    tok_rows, width = activations.shape
    heads = width // HD
    top_count = routes.shape[1]
    experts = router_weight.shape[1]
    local_experts = expert_gate.shape[0]
    mine = local_experts // ZP
    hidden_width = expert_gate.shape[2]
    sources = ZP * nx * NC
    capacity = min((tok_rows * top_count * 10 // (7 * experts) + 7) // 8 * 8, tok_rows)

    bundle = jnp.concatenate(
        [
            query_weight,
            key_weight,
            value_weight,
            output_weight,
            router_weight,
            gain_attention[:, None],
            gain_experts[:, None],
            jnp.zeros((gain_experts.shape[0], 128 - experts - 2), bf16),
        ],
        axis=1,
    )
    integers = jnp.concatenate([routes.T, segment[None, :]], axis=0)
    bundle_all, group_rows, integers_all = gather_first(
        grid_of, bundle, activations, integers
    )
    group_rows = group_rows.at[0, 0].set(activations).reshape(-1, width)
    integers_all = integers_all.at[0, 0, 0].set(integers)
    integers_all = integers_all.reshape(sources, top_count + 1, tok_rows)
    bundle_all = bundle_all.reshape(width, bundle.shape[1])
    w_query, w_key, w_value, w_out = (
        bundle_all[:, i * width : (i + 1) * width] for i in range(4)
    )
    small_all = bundle_all[:, 4 * width :]
    gather_all = lambda v: lax.all_gather(v, BOTH, axis=0, tiled=True)
    s_both = gather_all(jnp.concatenate([shared_gate, shared_up], axis=1))
    s_gate, s_up = s_both[:, :hidden_width], s_both[:, hidden_width:]
    s_down = gather_all(shared_down)
    w_router = small_all[:, :experts]
    gain_one = small_all[:, experts].astype(f32)
    gain_two = small_all[:, experts + 1].astype(f32)

    inputs = activations.astype(f32)
    inverse_one = norm_scale(inputs)
    group_inputs = group_rows.astype(f32)
    normed_group = (group_inputs * norm_scale(group_inputs) * gain_one).astype(bf16)
    normed_one = normed_group[:tok_rows]
    queries = times(normed_one, w_query).astype(bf16)
    keys_all = times(normed_group, w_key).astype(bf16)
    values_all = times(normed_group, w_value).astype(bf16)
    labels_all = integers_all[: nx * NC, top_count].reshape(-1)
    steps = jnp.arange(tok_rows, dtype=jnp.int32)
    block_places = (
        (grid.x + jnp.arange(nx, dtype=jnp.int32)[:, None]) % nx * NC
        + (grid.c + jnp.arange(NC, dtype=jnp.int32)[None, :]) % NC
    ).reshape(-1)
    key_places = (block_places[:, None] * tok_rows + steps[None, :]).reshape(-1)
    query_places = (grid.x * NC + grid.c) * tok_rows + steps
    bias = attention_bias(segment, labels_all, query_places, key_places)
    query_heads = queries.reshape(-1, heads, HD)
    key_heads = keys_all.reshape(-1, heads, HD)
    value_heads = values_all.reshape(-1, heads, HD)
    probs = make_probs(query_heads, key_heads, bias)
    attended = (
        jnp.einsum(
            "hqk,khd->qhd", probs.astype(bf16), value_heads, preferred_element_type=f32
        )
        .reshape(tok_rows, width)
        .astype(bf16)
    )
    middle = inputs + times(attended, w_out)
    inverse_two = norm_scale(middle)
    normed_two = (middle * inverse_two * gain_two).astype(bf16)

    rows_all, cot_all = exchange(grid_of, ZP, 1, normed_two, cotangent)
    rows_all = rows_all.reshape(sources, tok_rows, width)
    cot_all = cot_all.reshape(sources, tok_rows, width)
    router_probs_all = jax.nn.softmax(
        times(rows_all.reshape(-1, width), w_router).reshape(sources, tok_rows, experts),
        axis=-1,
    )
    router_probs = router_probs_all[0]
    first_expert = (grid.x * NC + grid.c) * local_experts + grid.zm * mine
    routes_all = integers_all[:, :top_count]
    numbers = first_expert + jnp.arange(mine, dtype=jnp.int32)
    marks = jnp.any(
        routes_all[None] == numbers[:, None, None, None], axis=2
    )
    earlier = (steps[:, None] < steps[None, :]).astype(bf16)
    ranks = jnp.einsum(
        "irt,tu->iru", marks.astype(bf16), earlier, preferred_element_type=f32
    ).astype(jnp.int32)
    slots = jnp.arange(capacity, dtype=jnp.int32)
    chosen = marks[:, :, None, :] & (ranks[:, :, None, :] == slots[None, None, :, None])
    picks = chosen.astype(bf16)
    gates_mine = jnp.moveaxis(
        lax.dynamic_slice_in_dim(router_probs_all, first_expert, mine, axis=2), 2, 0
    )
    gate_rows = jnp.sum(
        jnp.where(chosen, gates_mine[:, :, None, :], 0.0), axis=-1
    ).reshape(mine, sources * capacity, 1)
    out_parts = 0.0
    row_parts = 0.0
    prob_parts = []
    gate_w_grads, up_w_grads, down_w_grads = [], [], []
    w_gates = lax.dynamic_slice_in_dim(expert_gate, grid.zm * mine, mine, axis=0)
    w_ups = lax.dynamic_slice_in_dim(expert_up, grid.zm * mine, mine, axis=0)
    w_downs = lax.dynamic_slice_in_dim(expert_down, grid.zm * mine, mine, axis=0)
    for i in range(mine):
        pick = lambda v: (
            jnp.einsum("rst,rtd->rsd", picks[i], v, preferred_element_type=f32)
            .astype(bf16)
            .reshape(sources * capacity, width)
        )
        unpick = lambda v: jnp.einsum(
            "rst,rsd->rtd",
            picks[i],
            v.reshape(sources, capacity, width),
            preferred_element_type=f32,
        )
        rows_here = pick(rows_all)
        cot_here = pick(cot_all).astype(f32)
        slot_here = (gate_rows[i] * cot_here).astype(bf16)
        gate_act = times(rows_here, w_gates[i])
        up_act = times(rows_here, w_ups[i])
        activated, slope = silu_parts(gate_act)
        hidden = (activated * up_act).astype(bf16)
        produced = times(hidden, w_downs[i]).astype(bf16).astype(f32)
        row_probs = jnp.sum(produced * cot_here, axis=-1).reshape(sources, capacity, 1)
        prob_parts.append(jnp.sum(jnp.where(chosen[i], row_probs, 0.0), axis=1))
        out_parts = out_parts + unpick((gate_rows[i] * produced).astype(bf16))
        hidden_grad = times_transposed(slot_here, w_downs[i])
        act_gate = (hidden_grad * up_act * slope).astype(bf16)
        act_up = (hidden_grad * activated).astype(bf16)
        down_w_grads.append(contract_rows(hidden, slot_here).astype(bf16))
        gate_w_grads.append(contract_rows(rows_here, act_gate).astype(bf16))
        up_w_grads.append(contract_rows(rows_here, act_up).astype(bf16))
        row_grad = (
            times_transposed(act_gate, w_gates[i]) + times_transposed(act_up, w_ups[i])
        ).astype(bf16)
        row_parts = row_parts + unpick(row_grad)

    both_parts = jnp.stack([row_parts.astype(bf16), out_parts.astype(bf16)])
    sums, sent = sum_around(
        grid_of,
        ZP,
        2,
        both_parts.reshape(2, ZP, nx, NC, tok_rows, width),
        jnp.stack(prob_parts, axis=1).reshape(ZP, nx, NC, mine, tok_rows),
    )
    routed_grad = sums[0].astype(f32)
    routed = sums[1].astype(f32)
    expert_down_grad = reduce_experts(grid, jnp.stack(down_w_grads))
    expert_gate_grad = reduce_experts(grid, jnp.stack(gate_w_grads))
    expert_up_grad = reduce_experts(grid, jnp.stack(up_w_grads))
    dz = (grid.zm + jnp.arange(ZP, dtype=jnp.int32)) % ZP
    owner = block_places.reshape(1, nx, NC, 1) * local_experts
    owner = owner + dz[:, None, None, None] * mine + jnp.arange(mine, dtype=jnp.int32)
    same = owner.reshape(-1)[None, :] == jnp.arange(experts, dtype=jnp.int32)[:, None]
    prob_grad = jnp.sum(
        jnp.where(same[:, :, None], sent.reshape(1, experts, tok_rows), 0.0), axis=1
    ).T

    shared_gate_act = times(normed_two, s_gate)
    shared_up_act = times(normed_two, s_up)
    shared_act, shared_slope = silu_parts(shared_gate_act)
    shared_hidden = (shared_act * shared_up_act).astype(bf16)
    shared_out = times(shared_hidden, s_down)
    out_grad = cotangent.astype(f32)
    shared_down_grad = contract_rows(shared_hidden, cotangent)
    shared_hidden_grad = times_transposed(cotangent, s_down)
    shared_gate_act_grad = (shared_hidden_grad * shared_up_act * shared_slope).astype(
        bf16
    )
    shared_up_act_grad = (shared_hidden_grad * shared_act).astype(bf16)
    shared_gate_grad = contract_rows(normed_two, shared_gate_act_grad)
    shared_up_grad = contract_rows(normed_two, shared_up_act_grad)
    normed_two_grad = times_transposed(shared_gate_act_grad, s_gate) + times_transposed(
        shared_up_act_grad, s_up
    )
    block_out = (middle + shared_out + routed).astype(bf16)

    logit_grad = router_probs * (
        prob_grad - jnp.sum(router_probs * prob_grad, axis=-1, keepdims=True)
    )
    router_grad = lax.dot_general(
        normed_two.astype(f32),
        logit_grad,
        (((0,), (0,)), ((), ())),
        precision=lax.Precision.HIGHEST,
        preferred_element_type=f32,
    )
    normed_two_grad = (
        normed_two_grad
        + routed_grad
        + lax.dot_general(
            logit_grad,
            w_router.astype(f32),
            (((1,), (1,)), ((), ())),
            precision=lax.Precision.HIGHEST,
            preferred_element_type=f32,
        )
    )
    gain_two_grad, middle_part = norm_backward(
        middle, inverse_two, gain_two, normed_two_grad
    )
    middle_grad = out_grad + middle_part
    branch_grad = middle_grad.astype(bf16)
    output_weight_grad = contract_rows(attended, branch_grad)
    attended_grad = times_transposed(branch_grad, w_out).astype(bf16)

    grad_heads = attended_grad.reshape(tok_rows, heads, HD)
    prob_grad_att = jnp.einsum(
        "qhd,khd->hqk", grad_heads, value_heads, preferred_element_type=f32
    )
    centre = jnp.sum(probs * prob_grad_att, axis=-1, keepdims=True)
    score_grad = (probs * (prob_grad_att - centre)).astype(bf16)
    query_act_grad = (
        (
            jnp.einsum("hqk,khd->qhd", score_grad, key_heads, preferred_element_type=f32)
            * HD ** (-0.5)
        )
        .reshape(tok_rows, width)
        .astype(bf16)
    )
    key_part = (
        jnp.einsum("hqk,qhd->khd", score_grad, query_heads, preferred_element_type=f32)
        * HD ** (-0.5)
    )
    value_part = jnp.einsum(
        "hqk,qhd->khd", probs.astype(bf16), grad_heads, preferred_element_type=f32
    )

    parts = jnp.stack([value_part.astype(bf16), key_part.astype(bf16)])
    value_act_grad, key_act_grad = sum_around(
        grid_of, 1, 3, parts.reshape(2, 1, nx, NC, tok_rows, width)
    )
    query_w_grad = contract_rows(normed_one, query_act_grad)
    key_w_grad = contract_rows(normed_one, key_act_grad)
    value_w_grad = contract_rows(normed_one, value_act_grad)
    normed_one_grad = (
        times_transposed(query_act_grad, w_query)
        + times_transposed(key_act_grad, w_key)
        + times_transposed(value_act_grad, w_value)
    )
    gain_one_grad, input_part = norm_backward(
        inputs, inverse_one, gain_one, normed_one_grad
    )
    input_grad = middle_grad + input_part

    def by_place(v):
        return v.reshape((NZ, ny, nx, NC, v.shape[0] // (wide * ep)) + v.shape[1:])

    def reduce_all(v, order):
        return reduce_dense(grid, by_place(v.astype(bf16)), order).astype(f32)

    output_weight_sum = reduce_all(output_weight_grad, "cxyz")
    shared_gate_sum = reduce_all(shared_gate_grad, "cyxz")
    shared_up_sum = reduce_all(shared_up_grad, "cxyz")
    shared_down_sum = reduce_all(shared_down_grad, "cyxz")
    query_sum = reduce_all(query_w_grad, "cxyz")
    key_sum = reduce_all(key_w_grad, "cyxz")
    value_sum = reduce_all(value_w_grad, "cxyz")
    counts = jnp.sum(
        (routes[:, :, None] == jnp.arange(experts, dtype=jnp.int32)).astype(f32),
        axis=(0, 1),
    )
    share = gain_attention.shape[0]
    count_block = jnp.pad(
        jnp.tile(counts.reshape(1, ep, 1, local_experts), (wide, 1, 1, 1)),
        ((0, 0), (0, 0), (0, 0), (0, 128 - local_experts)),
    )
    extras = jnp.concatenate(
        [
            router_grad,
            gain_one_grad[:, None],
            gain_two_grad[:, None],
            jnp.zeros((width, 128 - experts - 2), f32),
        ],
        axis=1,
    ).reshape(wide, ep, share, 128)
    extras = jnp.concatenate(
        [extras, count_block, jnp.zeros((wide, ep, 7, 128), f32)], axis=2
    )
    extra_sum = reduce_dense(
        grid, extras.reshape(NZ, ny, nx, NC, share + 8, 128), "cxyz"
    )
    return (
        block_out,
        input_grad,
        extra_sum[:share, experts],
        query_sum,
        key_sum,
        value_sum,
        output_weight_sum,
        extra_sum[:share, experts + 1],
        extra_sum[:share, :experts],
        shared_gate_sum,
        shared_up_sum,
        shared_down_sum,
        expert_gate_grad,
        expert_up_grad,
        expert_down_grad,
        extra_sum[share, :local_experts].astype(jnp.int32),
    )


def solution(mesh):
    split = P(BOTH, None)
    line = P(BOTH)
    held = P("ep", None, None)
    out_held = P("ep", "wide", None)
    in_specs = (
        (split, line, split, line)
        + (split,) * 4
        + (line,)
        + (split,) * 4
        + (held,) * 3
        + (split,)
    )
    out_specs = (
        (split, split, line)
        + (split,) * 4
        + (line,)
        + (split,) * 4
        + (out_held,) * 3
        + (P("ep"),)
    )
    return jax.shard_map(
        functools.partial(body, mesh.shape["wide"], mesh.shape["ep"]),
        mesh=mesh,
        in_specs=in_specs,
        out_specs=out_specs,
        check_vma=False,
    )
```

```python
import functools

import jax
import jax.numpy as jnp
from jax import lax
from jax.experimental import pallas as pl
from jax.experimental.pallas import tpu as pltpu
from jax.sharding import PartitionSpec as P

HD = 128
NC = 2
NZ = 4
ZP = 2
epsilon = 1e-06
masked_value = -1e30
BOTH = ("wide", "ep")
f32 = jnp.float32
bf16 = jnp.bfloat16


def contract_rows(left, right):
    return lax.dot_general(
        left, right, (((0,), (0,)), ((), ())), preferred_element_type=f32
    )


def times_transposed(left, right):
    return lax.dot_general(
        left, right, (((1,), (1,)), ((), ())), preferred_element_type=f32
    )


def times(left, right):
    return jnp.dot(left, right, preferred_element_type=f32)


def norm_scale(values):
    return lax.rsqrt(jnp.mean(values * values, axis=-1, keepdims=True) + epsilon)


def norm_backward(values, inverse, gain, normed_grad):
    weighted = normed_grad * gain
    gain_grad = jnp.sum(normed_grad * values * inverse, axis=0)
    cubed = inverse * inverse * inverse
    values_grad = inverse * weighted - values * cubed * jnp.mean(
        weighted * values, axis=-1, keepdims=True
    )
    return (gain_grad, values_grad)


def silu_parts(gate_act):
    logistic = jax.nn.sigmoid(gate_act)
    return (gate_act * logistic, logistic * (1.0 + gate_act * (1.0 - logistic)))


class Grid:
    def __init__(self, wide, ep):
        self.ny, self.nx, self.ep = wide // NZ, ep // NC, ep
        w, e = lax.axis_index("wide"), lax.axis_index("ep")
        self.z, self.y, self.x, self.c = w // self.ny, w % self.ny, e // NC, e % NC
        self.zm = self.z % ZP

    def pairs(self, move):
        made = []
        for z in range(NZ):
            for y in range(self.ny):
                for x in range(self.nx):
                    for c in range(NC):
                        tz, ty, tx, tc = move(z, y, x, c)
                        made.append(
                            (
                                (z * self.ny + y) * self.ep + x * NC + c,
                                (tz * self.ny + ty) * self.ep + tx * NC + tc,
                            )
                        )
        return made

    def send(self, value, axis, step):
        moves = {
            "c": lambda z, y, x, c: (z, y, x, (c + step) % NC),
            "x": lambda z, y, x, c: (z, y, (x + step) % self.nx, c),
            "y": lambda z, y, x, c: (z, (y + step) % self.ny, x, c),
            "z": lambda z, y, x, c: ((z + step) % NZ, y, x, c),
            "p": lambda z, y, x, c: (z // ZP * ZP + (z % ZP + step) % ZP, y, x, c),
        }
        return lax.ppermute(value, BOTH, self.pairs(moves[axis]))

    def size(self, axis):
        return {"c": NC, "x": self.nx, "y": self.ny, "z": NZ, "p": ZP}[axis]

    def place(self, axis):
        return {"c": self.c, "x": self.x, "y": self.y, "z": self.z, "p": self.zm}[axis]

    def gather(self, value, axis, at):
        parts = [value] + [
            self.send(value, axis, -d) for d in range(1, self.size(axis))
        ]
        return jnp.stack(parts, axis=at)

    def scatter(self, value, axis, at):
        total = lax.index_in_dim(value, 0, at, keepdims=False).astype(f32)
        for d in range(1, self.size(axis)):
            part = lax.index_in_dim(value, d, at, keepdims=False)
            total = total + self.send(part, axis, d).astype(f32)
        return total.astype(value.dtype)

    def scatter_absolute(self, value, axis, at):
        n, me = self.size(axis), self.place(axis)
        take = lambda i: lax.dynamic_index_in_dim(value, i, at, keepdims=False)
        total = take(me).astype(f32)
        for d in range(1, n):
            total = total + self.send(take((me + d) % n), axis, d).astype(f32)
        return total.astype(value.dtype)


class Sender:
    def __init__(self, sems):
        self.sems, self.started = sems, []

    def __call__(self, src, dst, sem, target):
        copy = pltpu.make_async_remote_copy(
            src_ref=src,
            dst_ref=dst,
            send_sem=self.sems.at[len(self.started)],
            recv_sem=sem,
            device_id=target,
            device_id_type=pl.DeviceIdType.MESH,
        )
        copy.start()
        self.started.append(copy)

    def finish(self):
        for copy in self.started:
            copy.wait_send()


def arrived(dst, sem):
    pltpu.make_async_copy(dst, dst, sem).wait()


def greet(targets):
    barrier = pltpu.get_barrier_semaphore()
    for target in targets:
        pl.semaphore_signal(
            barrier, inc=1, device_id=target, device_id_type=pl.DeviceIdType.MESH
        )
    pl.semaphore_wait(barrier, len(targets))


def around(grid, zp):
    steps = [(a, b, e) for a in range(zp) for b in range(grid.nx) for e in range(NC)]
    return steps[1:]


def stepped(grid, zp, a, b, e):
    z = grid.z // zp * zp + (grid.z % zp + a) % zp
    return (
        z * grid.ny + grid.y,
        (grid.x + b) % grid.nx * NC + (grid.c + e) % NC,
    )


def gather_kernel(
    grid_of,
    w_ref,
    rows_ref,
    cot_ref,
    ints_ref,
    w_all,
    rows_all,
    cot_all,
    ints_all,
    plane_sem,
    core_sem,
    rows_sem,
    cot_sem,
    ints_sem,
    send_sem,
    local_sem,
):
    grid = grid_of()
    z, y, x, c, nx, ny = grid.z, grid.y, grid.x, grid.c, grid.nx, grid.ny

    def device(tz, ty, tx, tc):
        return (tz * ny + ty, tx * NC + tc)

    def block(dz, dy, dx, tc):
        place = (z + NZ - dz) % NZ * ny + (y + ny - dy) % ny
        return w_all.at[place * (nx * NC) + (x + nx - dx) % nx * NC + tc]

    shift_z = lambda d: (z + d) % NZ
    shift_y = lambda d: (y + d) % ny
    shift_x = lambda d: (x + d) % nx
    back = lambda d: (nx - d) % nx
    other = (c + 1) % NC
    to = functools.partial(stepped, grid, ZP)
    greet(
        [device(shift_z(d), y, x, c) for d in range(1, NZ)]
        + [device(z, shift_y(d), x, c) for d in range(1, ny)]
        + [to(*s) for s in around(grid, ZP)]
    )
    send = Sender(send_sem)
    locals_ = [
        (w_ref, block(0, 0, 0, c)),
        (rows_ref, rows_all.at[0, 0]),
        (cot_ref, cot_all.at[0, 0, 0]),
        (ints_ref, ints_all.at[0, 0, 0]),
    ]
    locals_ = [
        pltpu.make_async_copy(src, dst, local_sem.at[k])
        for k, (src, dst) in enumerate(locals_)
    ]
    for copy in locals_:
        copy.start()
    mine = block(0, 0, 0, c)
    for d in range(1, NZ):
        send(w_ref, mine, plane_sem.at[d, 0, 0], device(shift_z(d), y, x, c))

    def spread(src, dst, dz):
        for d in range(1, nx):
            send(src, dst, plane_sem.at[dz, 0, d], device(z, y, shift_x(d), c))
        for d in range(1, ny):
            send(src, dst, plane_sem.at[dz, d, 0], device(z, shift_y(d), x, c))
        send(src, dst, core_sem.at[dz, 0, 0], device(z, y, x, other))

    spread(w_ref, mine, 0)
    for d in range(1, nx):
        send(rows_ref, rows_all.at[back(d), 0], rows_sem.at[back(d), 0], to(0, d, 0))
    send(rows_ref, rows_all.at[0, 1], rows_sem.at[0, 1], to(0, 0, 1))
    for a, b, e in around(grid, ZP):
        mirror = ((ZP - a) % ZP, back(b), e)
        send(ints_ref, ints_all.at[mirror], ints_sem.at[mirror], to(a, b, e))

    for d in range(1, NZ):
        here = block(d, 0, 0, c)
        arrived(here, plane_sem.at[d, 0, 0])
        spread(here, here, d)
        if d == 1:
            for a in range(1, ZP):
                send(cot_ref, cot_all.at[ZP - a, 0, 0], cot_sem.at[ZP - a, 0, 0, 0], to(a, 0, 0))
            for b in range(1, nx):
                send(cot_ref, cot_all.at[0, back(b), 0], cot_sem.at[0, back(b), 0, 0], to(0, b, 0))
            send(cot_ref, cot_all.at[0, 0, 1], cot_sem.at[0, 0, 1, 0], to(0, 0, 1))
    for dz in range(NZ):
        for dx in range(1, nx):
            here = block(dz, 0, dx, c)
            arrived(here, plane_sem.at[dz, 0, dx])
            for d in range(1, ny):
                send(here, here, plane_sem.at[dz, d, dx], device(z, shift_y(d), x, c))
            send(here, here, core_sem.at[dz, 0, dx], device(z, y, x, other))
    for d in range(1, nx):
        here = rows_all.at[d, 0]
        arrived(here, rows_sem.at[d, 0])
        send(here, rows_all.at[d, 1], rows_sem.at[d, 1], to(0, 0, 1))
    width = cot_ref.shape[1]
    halves = [
        (slice(None), pl.ds(0, width // 2)),
        (slice(None), pl.ds(width // 2, width // 2)),
    ]
    for a in range(1, ZP):
        here = cot_all.at[a, 0, 0]
        arrived(here, cot_sem.at[a, 0, 0, 0])
        for b in range(1, nx):
            send(here.at[halves[0]], cot_all.at[a, back(b), 0].at[halves[0]], cot_sem.at[a, back(b), 0, 0], to(0, b, 0))
        send(here, cot_all.at[a, 0, 1], cot_sem.at[a, 0, 1, 0], to(0, 0, 1))
    for b in range(1, nx):
        here = cot_all.at[0, b, 0]
        arrived(here, cot_sem.at[0, b, 0, 0])
        for a in range(1, ZP):
            send(here.at[halves[1]], cot_all.at[ZP - a, b, 0].at[halves[1]], cot_sem.at[ZP - a, b, 0, 1], to(a, 0, 0))
        send(here, cot_all.at[0, b, 1], cot_sem.at[0, b, 1, 0], to(0, 0, 1))
    for dz in range(NZ):
        for dy in range(1, ny):
            for dx in range(nx):
                here = block(dz, dy, dx, c)
                arrived(here, plane_sem.at[dz, dy, dx])
                send(here, here, core_sem.at[dz, dy, dx], device(z, y, x, other))
    for a in range(1, ZP):
        for b in range(1, nx):
            here = cot_all.at[a, b, 0]
            for part in range(2):
                arrived(here.at[halves[part]], cot_sem.at[a, b, 0, part])
            send(here, cot_all.at[a, b, 1], cot_sem.at[a, b, 1, 0], to(0, 0, 1))
    for dx in range(nx):
        arrived(rows_all.at[dx, 1], rows_sem.at[dx, 1])
        for a in range(ZP):
            arrived(cot_all.at[a, dx, 1], cot_sem.at[a, dx, 1, 0])
    for a, b, e in around(grid, ZP):
        arrived(ints_all.at[a, b, e], ints_sem.at[a, b, e])
    for dz in range(NZ):
        for dy in range(ny):
            for dx in range(nx):
                arrived(block(dz, dy, dx, other), core_sem.at[dz, dy, dx])
    for copy in locals_:
        copy.wait()
    send.finish()


def gather_first(grid_of, w, rows, cot, ints):
    grid = grid_of()
    nx, ny = grid.nx, grid.ny
    places = NZ * ny * nx * NC
    octet = ZP * nx * NC
    sends = (NZ - 1) + NZ * (nx + ny) + 2 * nx + octet * 4 + NZ * nx * ny * (ny + 1)
    anywhere = pl.BlockSpec(memory_space=pl.ANY)
    dma = pltpu.SemaphoreType.DMA
    return pl.pallas_call(
        functools.partial(gather_kernel, grid_of),
        out_shape=(
            jax.ShapeDtypeStruct((places,) + w.shape, w.dtype),
            jax.ShapeDtypeStruct((nx, NC) + rows.shape, rows.dtype),
            jax.ShapeDtypeStruct((ZP, nx, NC) + cot.shape, cot.dtype),
            jax.ShapeDtypeStruct((ZP, nx, NC) + ints.shape, ints.dtype),
        ),
        in_specs=[anywhere] * 4,
        out_specs=(anywhere,) * 4,
        scratch_shapes=[
            dma((NZ, ny, nx)),
            dma((NZ, ny, nx)),
            dma((nx, NC)),
            dma((ZP, nx, NC, 2)),
            dma((ZP, nx, NC)),
            dma((sends,)),
            dma((4,)),
        ],
        compiler_params=pltpu.CompilerParams(collective_id=0, has_side_effects=True),
    )(w, rows, cot, ints)


def exchange_kernel(grid_of, zp, cut, count, *refs):
    grid = grid_of()
    nx = grid.nx
    ins, outs = refs[:count], refs[count : 2 * count]
    plane_sem, core_sem, local_sem, send_sem = refs[2 * count :]
    send = Sender(send_sem)
    to = functools.partial(stepped, grid, zp)
    greet([to(*s) for s in around(grid, zp)])
    back = lambda d: (nx - d) % nx
    for k in range(count):
        src, out = ins[k], outs[k]
        for a in range(1, zp):
            send(src, out.at[zp - a, 0, 0], plane_sem.at[k, zp - a, 0, 0], to(a, 0, 0))
        for b in range(1, nx):
            send(src, out.at[0, back(b), 0], plane_sem.at[k, 0, back(b), 0], to(0, b, 0))
        send(src, out.at[0, 0, 1], core_sem.at[k, 0, 0], to(0, 0, 1))
        pltpu.make_async_copy(src, out.at[0, 0, 0], local_sem.at[k]).start()
    for k in range(count):
        out = outs[k]
        h0 = (slice(None), pl.ds(0, cut))
        h1 = (slice(None), pl.ds(cut, ins[k].shape[1] - cut))
        for a in range(1, zp):
            here = out.at[a, 0, 0]
            arrived(here, plane_sem.at[k, a, 0, 0])
            for b in range(1, nx):
                send(here.at[h0], out.at[a, back(b), 0].at[h0], plane_sem.at[k, a, back(b), 0], to(0, b, 0))
            send(here, out.at[a, 0, 1], core_sem.at[k, a, 0], to(0, 0, 1))
        for b in range(1, nx):
            here = out.at[0, b, 0]
            arrived(here, plane_sem.at[k, 0, b, 0])
            for a in range(1, zp):
                send(here.at[h1], out.at[zp - a, b, 0].at[h1], plane_sem.at[k, zp - a, b, 1], to(a, 0, 0))
            send(here, out.at[0, b, 1], core_sem.at[k, 0, b], to(0, 0, 1))
    for k in range(count):
        out = outs[k]
        h0 = (slice(None), pl.ds(0, cut))
        h1 = (slice(None), pl.ds(cut, ins[k].shape[1] - cut))
        for a in range(1, zp):
            for b in range(1, nx):
                here = out.at[a, b, 0]
                arrived(here.at[h0], plane_sem.at[k, a, b, 0])
                arrived(here.at[h1], plane_sem.at[k, a, b, 1])
                send(here, out.at[a, b, 1], core_sem.at[k, a, b], to(0, 0, 1))
    for k in range(count):
        for a in range(zp):
            for b in range(nx):
                arrived(outs[k].at[a, b, 1], core_sem.at[k, a, b])
        pltpu.make_async_copy(ins[k], outs[k].at[0, 0, 0], local_sem.at[k]).wait()
    send.finish()


def exchange(grid_of, zp, number, *arrays):
    grid = grid_of()
    nx = grid.nx
    count = len(arrays)
    sends = count * (zp * nx * 2 + zp * nx * nx * 2)
    anywhere = pl.BlockSpec(memory_space=pl.ANY)
    dma = pltpu.SemaphoreType.DMA
    return pl.pallas_call(
        functools.partial(
            exchange_kernel, grid_of, zp, arrays[0].shape[1] // 256 * 128, count
        ),
        out_shape=tuple(
            jax.ShapeDtypeStruct((zp, nx, NC) + v.shape, v.dtype) for v in arrays
        ),
        in_specs=[anywhere] * count,
        out_specs=(anywhere,) * count,
        scratch_shapes=[
            dma((count, zp, nx, 2)),
            dma((count, zp, nx)),
            dma((count,)),
            dma((sends,)),
        ],
        compiler_params=pltpu.CompilerParams(
            collective_id=number, has_side_effects=True
        ),
    )(*arrays)


def add_into(dst, src, rows):
    for k in range(dst.shape[0]):

        @pl.loop(0, dst.shape[1], step=rows)
        def _(i):
            at = pl.ds(pl.multiple_of(i, rows), rows)
            dst[k, at] = (dst[k, at].astype(f32) + src[k, at].astype(f32)).astype(
                dst.dtype
            )


def sum_kernel(grid_of, zp, cut, small, jobs, parts, *refs):
    grid = grid_of()
    nx = grid.nx
    if small:
        pieces, refs = refs[0], refs[1:]
    job_ins, refs = refs[: len(jobs)], refs[len(jobs) :]
    out, refs = refs[0], refs[1:]
    if small:
        pieces_out, refs = refs[0], refs[1:]
    job_outs, refs = refs[: len(jobs)], refs[len(jobs) :]
    refs, (job_send, job_recv) = refs[:-2], refs[-2:]
    each = functools.partial(each_job, grid, jobs, job_ins, job_outs, job_send, job_recv)
    own, got_c, turn_x, turn_p, got_p, got_x = refs[:6]
    local_sem, c_sem, turn_sem, p_sem, x_sem, small_sem, send_sem = refs[6:]
    send = Sender(send_sem)
    to = functools.partial(stepped, grid, zp)
    greet([to(*s) for s in around(grid, zp)] + job_targets(grid, jobs))
    width = parts.shape[-1]
    h0, h1 = pl.ds(0, cut), pl.ds(cut, width - cut)
    order = (
        [(a, b) for a in range(1, zp) for b in range(1, nx)]
        + [(a, 0) for a in range(1, zp)]
        + [(0, b) for b in range(1, nx)]
        + [(0, 0)]
    )
    for a, b in order:
        send(parts.at[:, a, b, 1], got_c.at[:, a, b], c_sem.at[a, b], to(0, 0, 1))
        pltpu.make_async_copy(
            parts.at[:, a, b, 0], own.at[:, a, b], local_sem.at[a, b]
        ).start()
    if small:
        for a, b, e in around(grid, zp):
            mirror = ((zp - a) % zp, (nx - b) % nx, e)
            send(
                pieces.at[a, b, e],
                pieces_out.at[mirror],
                small_sem.at[mirror],
                to(a, b, e),
            )
        pltpu.make_async_copy(
            pieces.at[0, 0, 0], pieces_out.at[0, 0, 0], small_sem.at[0, 0, 0]
        ).start()
    each(lambda copy: copy.start())
    rows = 32

    def ready(a, b):
        arrived(got_c.at[:, a, b], c_sem.at[a, b])
        pltpu.make_async_copy(
            parts.at[:, a, b, 0], own.at[:, a, b], local_sem.at[a, b]
        ).wait()
        add_into(own.at[:, a, b], got_c.at[:, a, b], rows)

    for a in range(1, zp):
        for b in range(1, nx):
            ready(a, b)
            send(own.at[:, a, b, :, h0], turn_x.at[:, a - 1, b - 1], turn_sem.at[a - 1, b - 1, 0], to(0, b, 0))
            send(own.at[:, a, b, :, h1], turn_p.at[:, a - 1, b - 1], turn_sem.at[a - 1, b - 1, 1], to(a, 0, 0))
    for a in range(1, zp):
        ready(a, 0)
    for b in range(1, nx):
        ready(0, b)
    for a in range(1, zp):
        for b in range(1, nx):
            arrived(turn_x.at[:, a - 1, b - 1], turn_sem.at[a - 1, b - 1, 0])
            add_into(own.at[:, a, 0, :, h0], turn_x.at[:, a - 1, b - 1], rows)
        send(own.at[:, a, 0], got_p.at[:, a - 1], p_sem.at[a - 1], to(a, 0, 0))
    for b in range(1, nx):
        for a in range(1, zp):
            arrived(turn_p.at[:, a - 1, b - 1], turn_sem.at[a - 1, b - 1, 1])
            add_into(own.at[:, 0, b, :, h1], turn_p.at[:, a - 1, b - 1], rows)
        send(own.at[:, 0, b], got_x.at[:, b - 1], x_sem.at[b - 1], to(0, b, 0))
    ready(0, 0)
    for a in range(1, zp):
        arrived(got_p.at[:, a - 1], p_sem.at[a - 1])
        add_into(own.at[:, 0, 0], got_p.at[:, a - 1], rows)
    for b in range(1, nx):
        arrived(got_x.at[:, b - 1], x_sem.at[b - 1])
        add_into(own.at[:, 0, 0], got_x.at[:, b - 1], rows)
    result = pltpu.make_async_copy(own.at[:, 0, 0], out, local_sem.at[0, 0])
    result.start()
    if small:
        for a, b, e in [(0, 0, 0)] + around(grid, zp):
            arrived(pieces_out.at[a, b, e], small_sem.at[a, b, e])
    result.wait()
    each(lambda copy: copy.wait())
    send.finish()


def sum_around(grid_of, zp, number, parts, pieces=None, jobs=(), job_arrays=()):
    grid = grid_of()
    nx = grid.nx
    payloads, rows, width = parts.shape[0], parts.shape[-2], parts.shape[-1]
    cut = width // 256 * 128
    anywhere = pl.BlockSpec(memory_space=pl.ANY)
    dma = pltpu.SemaphoreType.DMA
    small = pieces is not None
    out_shape = [jax.ShapeDtypeStruct((payloads, rows, width), parts.dtype)]
    args = [parts]
    if small:
        out_shape.append(jax.ShapeDtypeStruct(pieces.shape, pieces.dtype))
        args.append(pieces)
    plain = len(out_shape)
    out_shape += job_shapes(grid, jobs, job_arrays)
    args += list(job_arrays)
    turns = (max(zp - 1, 1), max(nx - 1, 1))
    vmem = lambda shape: pltpu.VMEM(shape, parts.dtype)
    made = pl.pallas_call(
        functools.partial(sum_kernel, grid_of, zp, cut, small, jobs),
        out_shape=tuple(out_shape),
        in_specs=[anywhere] * len(args),
        out_specs=(anywhere,) * len(out_shape),
        scratch_shapes=[
            vmem((payloads, zp, nx, rows, width)),
            vmem((payloads, zp, nx, rows, width)),
            vmem((payloads,) + turns + (rows, cut)),
            vmem((payloads,) + turns + (rows, width - cut)),
            vmem((payloads, turns[0], rows, width)),
            vmem((payloads, turns[1], rows, width)),
            dma((zp, nx)),
            dma((zp, nx)),
            dma(turns + (2,)),
            dma((turns[0],)),
            dma((turns[1],)),
            dma((zp, nx, NC)),
            dma((zp * nx * 6 + 8,)),
        ]
        + job_sems(grid, jobs),
        compiler_params=pltpu.CompilerParams(
            collective_id=number,
            has_side_effects=True,
            vmem_limit_bytes=56 * 2**20,
        ),
    )(*args)
    return made[:plain], made[plain:]


def attention_kernel(q_ref, k_ref, v_ref, bias_ref, out_ref):
    scores = times_transposed(q_ref[...], k_ref[...]) * HD ** (-0.5) + bias_ref[...]
    weights = jnp.exp(scores - jnp.max(scores, axis=1, keepdims=True))
    probs = weights * (1.0 / jnp.sum(weights, axis=1, keepdims=True))
    out_ref[...] = times(probs.astype(bf16), v_ref[...]).astype(bf16)


def attention_forward(queries, keys, values, bias):
    rows, width = queries.shape
    length = keys.shape[0]
    by_head = lambda n: pl.BlockSpec((n, HD), lambda h: (0, h))
    return pl.pallas_call(
        attention_kernel,
        grid=(width // HD,),
        out_shape=jax.ShapeDtypeStruct((rows, width), bf16),
        in_specs=[
            by_head(rows),
            by_head(length),
            by_head(length),
            pl.BlockSpec((rows, length), lambda h: (0, 0)),
        ],
        out_specs=by_head(rows),
        compiler_params=pltpu.CompilerParams(vmem_limit_bytes=40 * 2**20),
        cost_estimate=pl.CostEstimate(
            flops=4 * rows * length * width,
            bytes_accessed=4 * (rows + length) * width + 4 * rows * length,
            transcendentals=rows * length * width // HD,
        ),
    )(queries, keys, values, bias)


def attention_back_kernel(grid_of, jobs, q_ref, k_ref, v_ref, g_ref, bias_ref, *refs):
    grid = grid_of()
    count = len(jobs)
    dq_ref, parts_ref = refs[count : count + 2]
    job_send, job_recv = refs[-2:]
    each = functools.partial(
        each_job, grid, jobs, refs[:count], refs[count + 2 : -2], job_send, job_recv
    )
    if jobs:

        @pl.when(pl.program_id(0) == 0)
        def _():
            greet(job_targets(grid, jobs))
            each(lambda copy: copy.start())

    q, k, g = q_ref[...], k_ref[...], g_ref[...]
    scores = times_transposed(k, q) * HD ** (-0.5) + bias_ref[...]
    weights = jnp.exp(scores - jnp.max(scores, axis=0, keepdims=True))
    probs = weights * (1.0 / jnp.sum(weights, axis=0, keepdims=True))
    prob_grad = times_transposed(v_ref[...], g)
    centre = jnp.sum(probs * prob_grad, axis=0, keepdims=True)
    score_grad = (probs * (prob_grad - centre)).astype(bf16)
    parts_ref[0] = times(probs.astype(bf16), g).astype(bf16)
    parts_ref[1] = (times(score_grad, q) * HD ** (-0.5)).astype(bf16)
    dq_ref[...] = (contract_rows(score_grad, k) * HD ** (-0.5)).astype(bf16)
    if jobs:

        @pl.when(pl.program_id(0) == pl.num_programs(0) - 1)
        def _():
            each(lambda copy: copy.wait())


def attention_backward(grid_of, number, queries, keys, values, grads, bias, jobs, job_arrays):
    grid = grid_of()
    rows, width = queries.shape
    length = keys.shape[0]
    by_head = lambda n: pl.BlockSpec((n, HD), lambda h: (0, h))
    anywhere = pl.BlockSpec(memory_space=pl.ANY)
    made = pl.pallas_call(
        functools.partial(attention_back_kernel, grid_of, jobs),
        grid=(width // HD,),
        out_shape=tuple(
            [
                jax.ShapeDtypeStruct((rows, width), bf16),
                jax.ShapeDtypeStruct((2, length, width), bf16),
            ]
            + job_shapes(grid, jobs, job_arrays)
        ),
        in_specs=[
            by_head(rows),
            by_head(length),
            by_head(length),
            by_head(rows),
            pl.BlockSpec((length, rows), lambda h: (0, 0)),
        ]
        + [anywhere] * len(jobs),
        out_specs=(by_head(rows), pl.BlockSpec((2, length, HD), lambda h: (0, 0, h)))
        + (anywhere,) * len(jobs),
        scratch_shapes=job_sems(grid, jobs),
        compiler_params=pltpu.CompilerParams(
            vmem_limit_bytes=40 * 2**20,
            **(dict(collective_id=number, has_side_effects=True) if jobs else {}),
        ),
        cost_estimate=pl.CostEstimate(
            flops=10 * rows * length * width,
            bytes_accessed=6 * rows * width + 8 * length * width + 4 * rows * length,
            transcendentals=rows * length * width // HD,
        ),
    )(queries, keys, values, grads, bias, *job_arrays)
    return made[0], made[1], made[2:]


ROW_SOURCES = 2


def expert_kernel(grid_of, capacity, steps, jobs, carry, *refs):
    grid = grid_of()
    count = len(jobs)
    take = lambda n: (refs[:n], refs[n:])
    (rows_ref, cot_ref, rank_row_ref, rank_col_ref, gate_ref, wg_ref, wu_ref, wd_ref), refs = take(8)
    before, refs = take(1 if carry else 0)
    job_ins, refs = take(count)
    (parts_ref, prob_ref, dg_ref, du_ref, dd_ref), refs = take(5)
    job_outs, refs = take(count)
    (x_keep, s_keep, c_keep, h_keep, ag_keep, au_keep, ht_keep), refs = take(7)
    each = functools.partial(each_job, grid, jobs, job_ins, job_outs, *refs)
    step = pl.program_id(0)
    width, hidden = x_keep.shape[1], h_keep.shape[1]
    tokens = rows_ref.shape[1]
    size = ROW_SOURCES * capacity
    strip = 256
    if jobs:

        @pl.when(step == 0)
        def _():
            greet(job_targets(grid, jobs))
            each(lambda copy: copy.start())

    @pl.when(step < steps)
    def _():
        at = pl.ds(pl.multiple_of(step * size, 32), size)
        picks, columns, gates = [], [], []
        for s in range(ROW_SOURCES):
            slots = lax.broadcasted_iota(jnp.int32, (capacity, tokens), 0)
            hit = slots == rank_row_ref[s]
            gate = jnp.sum(jnp.where(hit, gate_ref[s], 0.0), axis=1, keepdims=True)
            pick = hit.astype(f32).astype(bf16)
            picks.append(hit)
            gates.append(gate)
            across = lax.broadcasted_iota(jnp.int32, (tokens, capacity), 1)
            columns.append((across == rank_col_ref[s]).astype(f32).astype(bf16))
            to = pl.ds(pl.multiple_of(step * size + s * capacity, 16), capacity)
            x_keep[to] = times(pick, rows_ref[s]).astype(bf16)
            cot = times(pick, cot_ref[s])
            c_keep[pl.ds(s * capacity, capacity)] = cot.astype(bf16)
            s_keep[to] = (gate * cot).astype(bf16)
        x, slot = x_keep[at], s_keep[at]
        for low in range(0, hidden, strip):
            cut = slice(low, min(low + strip, hidden))
            gate_act = times(x, wg_ref[0, :, cut])
            up_act = times(x, wu_ref[0, :, cut])
            hidden_grad = times_transposed(slot, wd_ref[0, cut])
            activated, slope = silu_parts(gate_act)
            h_keep[at, cut] = (activated * up_act).astype(bf16)
            ag_keep[at, cut] = (hidden_grad * up_act * slope).astype(bf16)
            au_keep[at, cut] = (hidden_grad * activated).astype(bf16)
        h, ag, au = h_keep[at], ag_keep[at], au_keep[at]
        probs = jnp.zeros((size, 1), f32)
        for low in range(0, width, strip):
            cut = slice(low, low + strip)
            made = times(h, wd_ref[0, :, cut]).astype(bf16).astype(f32)
            probs += jnp.sum(made * c_keep[:, cut].astype(f32), axis=1, keepdims=True)
            back = (
                times_transposed(ag, wg_ref[0, cut]) + times_transposed(au, wu_ref[0, cut])
            ).astype(bf16)
            for s in range(ROW_SOURCES):
                mine = slice(s * capacity, (s + 1) * capacity)
                row = times(columns[s], back[mine])
                out = times(columns[s], (gates[s] * made[mine]).astype(bf16))
                if carry:
                    row += before[0][0, s, :, cut].astype(f32)
                    out += before[0][1, s, :, cut].astype(f32)
                parts_ref[0, s, :, cut] = row.astype(bf16)
                parts_ref[1, s, :, cut] = out.astype(bf16)
        for s in range(ROW_SOURCES):
            mine = slice(s * capacity, (s + 1) * capacity)
            prob_ref[s] = jnp.sum(
                jnp.where(picks[s], probs[mine], 0.0), axis=0, keepdims=True
            )

    @pl.when(step == steps)
    def _():
        ht_keep[...] = h_keep[...].T

    @pl.when(step >= steps)
    def _():
        cut = pl.ds(pl.multiple_of((step - steps) * strip, strip), strip)
        turned = x_keep[:, cut].T
        dg_ref[...] = times(turned, ag_keep[...]).astype(bf16)
        du_ref[...] = times(turned, au_keep[...]).astype(bf16)
        dd_ref[...] = times(ht_keep[...], s_keep[:, cut]).astype(bf16)

    if jobs:

        @pl.when(step == pl.num_programs(0) - 1)
        def _():
            each(lambda copy: copy.wait())


def run_expert(grid_of, number, expert, rows, cot, ranks, gates, weights, capacity, before, jobs, job_arrays):
    grid = grid_of()
    sources, tokens = ranks.shape
    width, hidden = weights[0].shape[1:]
    mine = weights[0].shape[0] // ZP
    steps = sources // ROW_SOURCES
    strip = 256
    strips = width // strip
    total = sources * capacity
    turn = lambda s: jnp.minimum(s, steps - 1)
    later = lambda s: jnp.maximum(s - steps, 0)
    block = pl.BlockSpec
    by_source = lambda *rest: block(
        (ROW_SOURCES,) + rest, lambda s: (turn(s),) + (0,) * len(rest)
    )
    held = lambda *rest: block(
        (1,) + rest,
        lambda s: (lax.axis_index("wide") // grid.ny % ZP * mine + expert, 0, 0),
    )
    parts = block((2, ROW_SOURCES, tokens, width), lambda s: (0, turn(s), 0, 0))
    anywhere = block(memory_space=pl.ANY)
    carry = before is not None
    made = pl.pallas_call(
        functools.partial(expert_kernel, grid_of, capacity, steps, jobs, carry),
        grid=(steps + strips,),
        in_specs=[
            by_source(tokens, width),
            by_source(tokens, width),
            by_source(1, tokens),
            by_source(tokens, 1),
            by_source(1, tokens),
            held(width, hidden),
            held(width, hidden),
            held(hidden, width),
        ]
        + [parts] * carry
        + [anywhere] * len(jobs),
        out_specs=[
            parts,
            by_source(1, tokens),
            block((strip, hidden), lambda s: (later(s), 0)),
            block((strip, hidden), lambda s: (later(s), 0)),
            block((hidden, strip), lambda s: (0, later(s))),
        ]
        + [anywhere] * len(jobs),
        scratch_shapes=[
            pltpu.VMEM((total, width), bf16),
            pltpu.VMEM((total, width), bf16),
            pltpu.VMEM((ROW_SOURCES * capacity, width), bf16),
            pltpu.VMEM((total, hidden), bf16),
            pltpu.VMEM((total, hidden), bf16),
            pltpu.VMEM((total, hidden), bf16),
            pltpu.VMEM((hidden, total), bf16),
        ]
        + job_sems(grid, jobs),
        out_shape=[
            jax.ShapeDtypeStruct((2, sources, tokens, width), bf16),
            jax.ShapeDtypeStruct((sources, 1, tokens), f32),
            jax.ShapeDtypeStruct((width, hidden), bf16),
            jax.ShapeDtypeStruct((width, hidden), bf16),
            jax.ShapeDtypeStruct((hidden, width), bf16),
        ]
        + job_shapes(grid, jobs, job_arrays),
        compiler_params=pltpu.CompilerParams(
            vmem_limit_bytes=58 * 2**20,
            **(dict(collective_id=number, has_side_effects=True) if jobs else {}),
        ),
        cost_estimate=pl.CostEstimate(
            flops=total * width * hidden * 18,
            bytes_accessed=width * hidden * 12 + 16 * sources * tokens * width,
            transcendentals=total * hidden,
        ),
    )(
        rows,
        cot,
        ranks[:, None, :],
        ranks[:, :, None],
        gates[:, None, :],
        *weights,
        *([before] if carry else []),
        *job_arrays,
    )
    return made[:5], made[5:]


def jobs_count(grid, jobs):
    return sum({"y": grid.ny, "z": NZ}[axis] - 1 for axis in jobs)


def job_targets(grid, jobs):
    axes = set(jobs)
    place = lambda z, y: (z * grid.ny + y, grid.x * NC + grid.c)
    made = []
    if "y" in axes:
        made += [place(grid.z, (grid.y + d) % grid.ny) for d in range(1, grid.ny)]
    if "z" in axes:
        made += [place((grid.z + d) % NZ, grid.y) for d in range(1, NZ)]
    return made


def each_job(grid, jobs, ins, outs, send_sem, recv_sem, act):
    at = 0
    for axis, src, out in zip(jobs, ins, outs):
        for d in range(1, {"y": grid.ny, "z": NZ}[axis]):
            if axis == "y":
                to = (grid.y + d) % grid.ny
                piece, target = src.at[:, to], (grid.z * grid.ny + to)
            else:
                to = (grid.z + d) % NZ
                piece, target = src.at[to], (to * grid.ny + grid.y)
            act(
                pltpu.make_async_remote_copy(
                    src_ref=piece,
                    dst_ref=out.at[d - 1],
                    send_sem=send_sem.at[at],
                    recv_sem=recv_sem.at[at],
                    device_id=(target, grid.x * NC + grid.c),
                    device_id_type=pl.DeviceIdType.MESH,
                )
            )
            at += 1


def job_shapes(grid, jobs, arrays):
    made = []
    for axis, v in zip(jobs, arrays):
        shape = (grid.ny - 1, NZ) + v.shape[2:] if axis == "y" else (NZ - 1,) + v.shape[1:]
        made.append(jax.ShapeDtypeStruct(shape, v.dtype))
    return made


def job_sems(grid, jobs):
    count = max(jobs_count(grid, jobs), 1)
    return [pltpu.SemaphoreType.DMA((count,)), pltpu.SemaphoreType.DMA((count,))]


def dense_kernel(grid_of, orders, jobs, *refs):
    grid = grid_of()
    z, y, x, c, nx, ny = grid.z, grid.y, grid.x, grid.c, grid.nx, grid.ny
    count, more = len(orders), len(jobs)
    take = lambda n: (refs[:n], refs[n:])
    ins, refs = take(count)
    job_ins, refs = take(more)
    outs, refs = take(count)
    job_outs, refs = take(more)
    held, refs = take(count)
    got_c, refs = take(count)
    got_one, refs = take(count)
    got_two, refs = take(count)
    got_z, refs = take(count)
    local_sem, c_sem, one_sem, two_sem, z_sem, out_sem, send_sem, job_send, job_recv = refs
    device = lambda tz, ty, tx, tc: (tz * ny + ty, tx * NC + tc)
    other = (c + 1) % NC
    greet(
        [device(z, y, x, other)]
        + [device(z, y, (x + d) % nx, c) for d in range(1, nx)]
        + [device(z, (y + d) % ny, x, c) for d in range(1, ny)]
        + [device((z + d) % NZ, y, x, c) for d in range(1, NZ)]
    )
    send = Sender(send_sem)
    loads = []
    for k in range(count):
        send(ins[k].at[:, :, :, other], got_c[k], c_sem.at[k], device(z, y, x, other))
        load = pltpu.make_async_copy(ins[k].at[:, :, :, c], held[k], local_sem.at[k])
        load.start()
        loads.append(load)
    each_job(grid, jobs, job_ins, job_outs, job_send, job_recv, lambda copy: copy.start())

    def add(dst, src):
        lead = dst.shape[:-2]
        total = 1
        for n in lead:
            total *= n

        @pl.loop(0, total)
        def _(i):
            index = []
            for n in reversed(lead):
                index.insert(0, i % n)
                i = i // n
            index = tuple(index)
            dst[index] = (dst[index].astype(f32) + src[index].astype(f32)).astype(dst.dtype)

    def first(k):
        loads[k].wait()
        arrived(got_c[k], c_sem.at[k])
        add(held[k], got_c[k])
        if orders[k] == "xy":
            for d in range(1, nx):
                to = (x + d) % nx
                send(held[k].at[:, :, to], got_one[k].at[d - 1], one_sem.at[k, d - 1], device(z, y, to, c))
        else:
            for d in range(1, ny):
                to = (y + d) % ny
                send(held[k].at[:, to], got_one[k].at[d - 1], one_sem.at[k, d - 1], device(z, to, x, c))

    def second(k):
        mine = held[k].at[:, :, x] if orders[k] == "xy" else held[k].at[:, y]
        for d in range(1, nx if orders[k] == "xy" else ny):
            arrived(got_one[k].at[d - 1], one_sem.at[k, d - 1])
            add(mine, got_one[k].at[d - 1])
        if orders[k] == "xy":
            for d in range(1, ny):
                to = (y + d) % ny
                send(held[k].at[:, to, x], got_two[k].at[d - 1], two_sem.at[k, d - 1], device(z, to, x, c))
        else:
            for d in range(1, nx):
                to = (x + d) % nx
                send(held[k].at[:, y, to], got_two[k].at[d - 1], two_sem.at[k, d - 1], device(z, y, to, c))

    results = []

    def third(k):
        mine = held[k].at[:, y, x]
        for d in range(1, ny if orders[k] == "xy" else nx):
            arrived(got_two[k].at[d - 1], two_sem.at[k, d - 1])
            add(mine, got_two[k].at[d - 1])
        near = z // ZP * ZP + (z + 1) % ZP
        for n in range(NZ // ZP):
            to = (z + 1) % ZP + n * ZP
            send(held[k].at[to, y, x], got_z[k].at[n], z_sem.at[k, n], device(near, y, x, c))

    def fourth(k):
        for n in range(NZ // ZP):
            arrived(got_z[k].at[n], z_sem.at[k, n])
            at = (z % ZP + n * ZP, y, x)
            held[k][at] = (held[k][at].astype(f32) + got_z[k][n].astype(f32)).astype(held[k].dtype)
        for n in range(1, NZ // ZP):
            to = (z + n * ZP) % NZ
            send(held[k].at[to, y, x], outs[k].at[n], z_sem.at[k, NZ // ZP + n - 1], device(to, y, x, c))
        result = pltpu.make_async_copy(held[k].at[z, y, x], outs[k].at[0], out_sem.at[k])
        result.start()
        results.append(result)

    for t in range(count + 6):
        for stage, late in ((first, 0), (second, 2), (third, 4), (fourth, 6)):
            if 0 <= t - late < count:
                stage(t - late)
    for k in range(count):
        for n in range(1, NZ // ZP):
            arrived(outs[k].at[n], z_sem.at[k, NZ // ZP + n - 1])
        results[k].wait()
    each_job(grid, jobs, job_ins, job_outs, job_send, job_recv, lambda copy: copy.wait())
    send.finish()


def reduce_dense(grid_of, number, arrays, orders, jobs, job_arrays):
    grid = grid_of()
    nx, ny = grid.nx, grid.ny
    count = len(arrays)
    anywhere = pl.BlockSpec(memory_space=pl.ANY)
    dma = pltpu.SemaphoreType.DMA
    block = [v.shape[4:] for v in arrays]
    kind = [v.dtype for v in arrays]
    far = max(nx, ny)
    held = [pltpu.VMEM((NZ, ny, nx) + b, t) for b, t in zip(block, kind)]
    one = [
        pltpu.VMEM((nx - 1, NZ, ny) + b if o == "xy" else (ny - 1, NZ, nx) + b, t)
        for b, t, o in zip(block, kind, orders)
    ]
    two = [
        pltpu.VMEM(((ny if o == "xy" else nx) - 1, NZ) + b, t)
        for b, t, o in zip(block, kind, orders)
    ]
    made = pl.pallas_call(
        functools.partial(dense_kernel, grid_of, orders, jobs),
        out_shape=tuple(
            [jax.ShapeDtypeStruct((NZ // ZP,) + b, t) for b, t in zip(block, kind)]
            + job_shapes(grid, jobs, job_arrays)
        ),
        in_specs=[anywhere] * (count + len(jobs)),
        out_specs=(anywhere,) * (count + len(jobs)),
        scratch_shapes=held
        + held
        + one
        + two
        + [pltpu.VMEM((NZ // ZP,) + b, t) for b, t in zip(block, kind)]
        + [
            dma((count,)),
            dma((count,)),
            dma((count, far)),
            dma((count, far)),
            dma((count, NZ - 1)),
            dma((count,)),
            dma((count * (1 + nx + ny + NZ),)),
        ]
        + job_sems(grid, jobs),
        compiler_params=pltpu.CompilerParams(
            collective_id=number,
            has_side_effects=True,
            vmem_limit_bytes=60 * 2**20,
        ),
    )(*arrays, *job_arrays)
    return made[:count], made[count:]


def attention_bias(segment, labels_all, query_places, key_places):
    same_doc = segment[:, None] == labels_all[None, :]
    allowed = same_doc & (query_places[:, None] >= key_places[None, :])
    return jnp.where(allowed, 0.0, masked_value).astype(f32)


def body(
    wide,
    ep,
    activations,
    segment,
    routes,
    gain_attention,
    query_weight,
    key_weight,
    value_weight,
    output_weight,
    gain_experts,
    router_weight,
    shared_gate,
    shared_up,
    shared_down,
    expert_gate,
    expert_up,
    expert_down,
    cotangent,
):
    grid_of = functools.partial(Grid, wide, ep)
    grid = grid_of()
    nx, ny = grid.nx, grid.ny
    tok_rows, width = activations.shape
    heads = width // HD
    top_count = routes.shape[1]
    experts = router_weight.shape[1]
    local_experts = expert_gate.shape[0]
    mine = local_experts // ZP
    hidden_width = expert_gate.shape[2]
    sources = ZP * nx * NC
    capacity = min((tok_rows * top_count * 10 // (7 * experts) + 7) // 8 * 8, tok_rows)

    bundle = jnp.concatenate(
        [
            query_weight,
            key_weight,
            value_weight,
            output_weight,
            router_weight,
            gain_attention[:, None],
            gain_experts[:, None],
            jnp.zeros((gain_experts.shape[0], 128 - experts - 2), bf16),
        ],
        axis=1,
    )
    integers = jnp.concatenate([routes.T, segment[None, :]], axis=0)
    bundle_all, group_rows, cot_all, integers_all = gather_first(
        grid_of, bundle, activations, cotangent, integers
    )
    group_rows = group_rows.reshape(-1, width)
    integers_all = integers_all.reshape(sources, top_count + 1, tok_rows)
    bundle_all = bundle_all.reshape(width, bundle.shape[1])
    w_query, w_key, w_value, w_out = (
        bundle_all[:, i * width : (i + 1) * width] for i in range(4)
    )
    small_all = bundle_all[:, 4 * width :]
    gather_all = lambda v: lax.all_gather(v, BOTH, axis=0, tiled=True)
    s_both = gather_all(jnp.concatenate([shared_gate, shared_up], axis=1))
    s_gate, s_up = s_both[:, :hidden_width], s_both[:, hidden_width:]
    s_down = gather_all(shared_down)
    w_router = small_all[:, :experts]
    gain_one = small_all[:, experts].astype(f32)
    gain_two = small_all[:, experts + 1].astype(f32)

    inputs = activations.astype(f32)
    inverse_one = norm_scale(inputs)
    group_inputs = group_rows.astype(f32)
    normed_group = (group_inputs * norm_scale(group_inputs) * gain_one).astype(bf16)
    normed_one = normed_group[:tok_rows]
    queries = times(normed_one, w_query).astype(bf16)
    keys_all = times(normed_group, w_key).astype(bf16)
    values_all = times(normed_group, w_value).astype(bf16)
    labels_all = integers_all[: nx * NC, top_count].reshape(-1)
    steps = jnp.arange(tok_rows, dtype=jnp.int32)
    block_places = (
        (grid.x + jnp.arange(nx, dtype=jnp.int32)[:, None]) % nx * NC
        + (grid.c + jnp.arange(NC, dtype=jnp.int32)[None, :]) % NC
    ).reshape(-1)
    key_places = (block_places[:, None] * tok_rows + steps[None, :]).reshape(-1)
    query_places = (grid.x * NC + grid.c) * tok_rows + steps
    bias = attention_bias(segment, labels_all, query_places, key_places)
    attended = attention_forward(queries, keys_all, values_all, bias)
    middle = inputs + times(attended, w_out)
    inverse_two = norm_scale(middle)
    normed_two = (middle * inverse_two * gain_two).astype(bf16)

    (rows_all,) = exchange(grid_of, ZP, 1, normed_two)
    rows_all = rows_all.reshape(sources, tok_rows, width)
    cot_all = cot_all.reshape(sources, tok_rows, width)
    router_probs_all = jax.nn.softmax(
        times(rows_all.reshape(-1, width), w_router).reshape(sources, tok_rows, experts),
        axis=-1,
    )
    router_probs = router_probs_all[0]
    first_expert = (grid.x * NC + grid.c) * local_experts + grid.zm * mine
    routes_all = integers_all[:, :top_count]
    numbers = first_expert + jnp.arange(mine, dtype=jnp.int32)
    marks = jnp.any(
        routes_all[None] == numbers[:, None, None, None], axis=2
    )
    earlier = (steps[:, None] < steps[None, :]).astype(bf16)
    ranks = jnp.einsum(
        "irt,tu->iru", marks.astype(bf16), earlier, preferred_element_type=f32
    ).astype(jnp.int32)
    ranks = jnp.where(marks, ranks, -1)
    gates_mine = jnp.moveaxis(
        lax.dynamic_slice_in_dim(router_probs_all, first_expert, mine, axis=2), 2, 0
    )
    def by_wide(v):
        return v.reshape(NZ, ny, v.shape[0] // wide, v.shape[1])

    names = [(i, k) for i in range(mine) for k in range(3)]
    grads, along_y, along_z = {}, {}, {}

    def jobs_of(which_y, which_z):
        tags = tuple("y" for _ in which_y) + tuple("z" for _ in which_z)
        return tags, [grads[n] for n in which_y] + [column[n] for n in which_z]

    def landed(which_y, which_z, moved):
        along_y.update(zip(which_y, moved))
        along_z.update(zip(which_z, moved[len(which_y) :]))

    def summed(name):
        total = lax.dynamic_index_in_dim(grads[name], grid.y, 1, keepdims=False).astype(f32)
        for d in range(ny - 1):
            total = total + along_y[name][d].astype(f32)
        return total.astype(bf16)

    column = {}
    both_parts = None
    prob_parts = []
    for i in range(mine):
        behind = (names[3 * i - 3 : 3 * i - 1], []) if i else ([], [])
        (both_parts, probs_here, *made), moved = run_expert(
            grid_of,
            5 + i,
            i,
            rows_all,
            cot_all,
            ranks[i],
            gates_mine[i],
            (expert_gate, expert_up, expert_down),
            capacity,
            both_parts,
            *jobs_of(*behind),
        )
        landed(*behind, moved)
        prob_parts.append(probs_here[:, 0])
        grads.update({(i, k): by_wide(v) for k, v in enumerate(made)})
    column.update({name: summed(name) for name in along_y})
    behind = (names[2:4], names[:1])
    (sums, sent), moved = sum_around(
        grid_of,
        ZP,
        2,
        both_parts.reshape(2, ZP, nx, NC, tok_rows, width),
        jnp.stack(prob_parts, axis=1).reshape(ZP, nx, NC, mine, tok_rows),
        *jobs_of(*behind),
    )
    landed(*behind, moved)
    column.update({name: summed(name) for name in behind[0]})
    routed_grad = sums[0].astype(f32)
    routed = sums[1].astype(f32)
    dz = (grid.zm + jnp.arange(ZP, dtype=jnp.int32)) % ZP
    owner = block_places.reshape(1, nx, NC, 1) * local_experts
    owner = owner + dz[:, None, None, None] * mine + jnp.arange(mine, dtype=jnp.int32)
    same = owner.reshape(-1)[None, :] == jnp.arange(experts, dtype=jnp.int32)[:, None]
    prob_grad = jnp.sum(
        jnp.where(same[:, :, None], sent.reshape(1, experts, tok_rows), 0.0), axis=1
    ).T

    shared_gate_act = times(normed_two, s_gate)
    shared_up_act = times(normed_two, s_up)
    shared_act, shared_slope = silu_parts(shared_gate_act)
    shared_hidden = (shared_act * shared_up_act).astype(bf16)
    shared_out = times(shared_hidden, s_down)
    out_grad = cotangent.astype(f32)
    shared_down_grad = contract_rows(shared_hidden, cotangent)
    shared_hidden_grad = times_transposed(cotangent, s_down)
    shared_gate_act_grad = (shared_hidden_grad * shared_up_act * shared_slope).astype(
        bf16
    )
    shared_up_act_grad = (shared_hidden_grad * shared_act).astype(bf16)
    shared_gate_grad = contract_rows(normed_two, shared_gate_act_grad)
    shared_up_grad = contract_rows(normed_two, shared_up_act_grad)
    normed_two_grad = times_transposed(shared_gate_act_grad, s_gate) + times_transposed(
        shared_up_act_grad, s_up
    )
    block_out = (middle + shared_out + routed).astype(bf16)

    logit_grad = router_probs * (
        prob_grad - jnp.sum(router_probs * prob_grad, axis=-1, keepdims=True)
    )
    router_grad = lax.dot_general(
        normed_two.astype(f32),
        logit_grad,
        (((0,), (0,)), ((), ())),
        precision=lax.Precision.HIGHEST,
        preferred_element_type=f32,
    )
    normed_two_grad = (
        normed_two_grad
        + routed_grad
        + lax.dot_general(
            logit_grad,
            w_router.astype(f32),
            (((1,), (1,)), ((), ())),
            precision=lax.Precision.HIGHEST,
            preferred_element_type=f32,
        )
    )
    gain_two_grad, middle_part = norm_backward(
        middle, inverse_two, gain_two, normed_two_grad
    )
    middle_grad = out_grad + middle_part
    branch_grad = middle_grad.astype(bf16)
    output_weight_grad = contract_rows(attended, branch_grad)
    attended_grad = times_transposed(branch_grad, w_out).astype(bf16)

    behind = (names[4:5], names[1:2])
    query_act_grad, parts, moved = attention_backward(
        grid_of,
        1 + 8,
        queries,
        keys_all,
        values_all,
        attended_grad,
        bias.T,
        *jobs_of(*behind),
    )
    landed(*behind, moved)
    behind = (names[5:], names[2:4])
    ((value_key,), moved) = sum_around(
        grid_of,
        1,
        3,
        parts.reshape(2, 1, nx, NC, tok_rows, width),
        None,
        *jobs_of(*behind),
    )
    value_act_grad, key_act_grad = value_key
    landed(*behind, moved)
    column.update({name: summed(name) for name in names[4:]})
    query_w_grad = contract_rows(normed_one, query_act_grad)
    key_w_grad = contract_rows(normed_one, key_act_grad)
    value_w_grad = contract_rows(normed_one, value_act_grad)
    normed_one_grad = (
        times_transposed(query_act_grad, w_query)
        + times_transposed(key_act_grad, w_key)
        + times_transposed(value_act_grad, w_value)
    )
    gain_one_grad, input_part = norm_backward(
        inputs, inverse_one, gain_one, normed_one_grad
    )
    input_grad = middle_grad + input_part

    def by_place(v):
        return v.reshape((NZ, ny, nx, NC, v.shape[0] // (wide * ep)) + v.shape[1:])

    counts = jnp.sum(
        (routes[:, :, None] == jnp.arange(experts, dtype=jnp.int32)).astype(f32),
        axis=(0, 1),
    )
    share = gain_attention.shape[0]
    count_block = jnp.pad(
        jnp.tile(counts.reshape(1, ep, 1, local_experts), (wide, 1, 1, 1)),
        ((0, 0), (0, 0), (0, 0), (0, 128 - local_experts)),
    )
    extras = jnp.concatenate(
        [
            router_grad,
            gain_one_grad[:, None],
            gain_two_grad[:, None],
            jnp.zeros((width, 128 - experts - 2), f32),
        ],
        axis=1,
    ).reshape(wide, ep, share, 128)
    extras = jnp.concatenate(
        [extras, count_block, jnp.zeros((wide, ep, 7, 128), f32)], axis=2
    )
    dense = [
        output_weight_grad,
        shared_down_grad,
        shared_gate_grad,
        shared_up_grad,
        query_w_grad,
        key_w_grad,
        value_w_grad,
    ]
    terms, moved = reduce_dense(
        grid_of,
        4,
        [by_place(v.astype(bf16)) for v in dense]
        + [extras.reshape(NZ, ny, nx, NC, share + 8, 128)],
        ("xy", "yx", "xy", "yx", "xy", "yx", "xy", "xy"),
        *jobs_of([], names[4:]),
    )
    landed([], names[4:], moved)
    (
        output_weight_sum,
        shared_down_sum,
        shared_gate_sum,
        shared_up_sum,
        query_sum,
        key_sum,
        value_sum,
        extra_sum,
    ) = (jnp.sum(v.astype(f32), axis=0) for v in terms)

    def expert_sum(kind):
        halves = [[], []]
        for i in range(mine):
            name = (i, kind)
            same = lax.dynamic_index_in_dim(column[name], grid.z, 0, keepdims=False)
            same = same.astype(f32)
            far = 0.0
            for d in range(1, NZ):
                got = along_z[name][d - 1].astype(f32)
                if d % ZP == 0:
                    same = same + got
                else:
                    far = far + got
            halves[0].append(jnp.where(grid.zm == 0, same, far))
            halves[1].append(jnp.where(grid.zm == 0, far, same))
        return jnp.stack(halves[0] + halves[1])

    expert_gate_grad, expert_up_grad, expert_down_grad = (expert_sum(k) for k in range(3))
    return (
        block_out,
        input_grad,
        extra_sum[:share, experts],
        query_sum,
        key_sum,
        value_sum,
        output_weight_sum,
        extra_sum[:share, experts + 1],
        extra_sum[:share, :experts],
        shared_gate_sum,
        shared_up_sum,
        shared_down_sum,
        expert_gate_grad,
        expert_up_grad,
        expert_down_grad,
        extra_sum[share, :local_experts].astype(jnp.int32),
    )


def solution(mesh):
    split = P(BOTH, None)
    line = P(BOTH)
    held = P("ep", None, None)
    out_held = P("ep", "wide", None)
    in_specs = (
        (split, line, split, line)
        + (split,) * 4
        + (line,)
        + (split,) * 4
        + (held,) * 3
        + (split,)
    )
    out_specs = (
        (split, split, line)
        + (split,) * 4
        + (line,)
        + (split,) * 4
        + (out_held,) * 3
        + (P("ep"),)
    )
    return jax.shard_map(
        functools.partial(body, mesh.shape["wide"], mesh.shape["ep"]),
        mesh=mesh,
        in_specs=in_specs,
        out_specs=out_specs,
        check_vma=False,
    )
```

```python
import functools

import jax
import jax.numpy as jnp
from jax import lax
from jax.experimental import pallas as pl
from jax.experimental.pallas import tpu as pltpu
from jax.sharding import PartitionSpec as P

HD = 128
NC = 2
NZ = 4
ZP = 2
epsilon = 1e-06
masked_value = -1e30
BOTH = ("wide", "ep")
f32 = jnp.float32
bf16 = jnp.bfloat16


def contract_rows(left, right):
    return lax.dot_general(
        left, right, (((0,), (0,)), ((), ())), preferred_element_type=f32
    )


def times_transposed(left, right):
    return lax.dot_general(
        left, right, (((1,), (1,)), ((), ())), preferred_element_type=f32
    )


def times(left, right):
    return jnp.dot(left, right, preferred_element_type=f32)


def norm_scale(values):
    return lax.rsqrt(jnp.mean(values * values, axis=-1, keepdims=True) + epsilon)


def norm_backward(values, inverse, gain, normed_grad):
    weighted = normed_grad * gain
    gain_grad = jnp.sum(normed_grad * values * inverse, axis=0)
    cubed = inverse * inverse * inverse
    values_grad = inverse * weighted - values * cubed * jnp.mean(
        weighted * values, axis=-1, keepdims=True
    )
    return (gain_grad, values_grad)


def silu_parts(gate_act):
    logistic = jax.nn.sigmoid(gate_act)
    return (gate_act * logistic, logistic * (1.0 + gate_act * (1.0 - logistic)))


class Grid:
    def __init__(self, wide, ep):
        self.ny, self.nx, self.ep = wide // NZ, ep // NC, ep
        w, e = lax.axis_index("wide"), lax.axis_index("ep")
        self.z, self.y, self.x, self.c = w // self.ny, w % self.ny, e // NC, e % NC
        self.zm = self.z % ZP

    def pairs(self, move):
        made = []
        for z in range(NZ):
            for y in range(self.ny):
                for x in range(self.nx):
                    for c in range(NC):
                        tz, ty, tx, tc = move(z, y, x, c)
                        made.append(
                            (
                                (z * self.ny + y) * self.ep + x * NC + c,
                                (tz * self.ny + ty) * self.ep + tx * NC + tc,
                            )
                        )
        return made

    def send(self, value, axis, step):
        moves = {
            "c": lambda z, y, x, c: (z, y, x, (c + step) % NC),
            "x": lambda z, y, x, c: (z, y, (x + step) % self.nx, c),
            "y": lambda z, y, x, c: (z, (y + step) % self.ny, x, c),
            "z": lambda z, y, x, c: ((z + step) % NZ, y, x, c),
            "p": lambda z, y, x, c: (z // ZP * ZP + (z % ZP + step) % ZP, y, x, c),
        }
        return lax.ppermute(value, BOTH, self.pairs(moves[axis]))

    def size(self, axis):
        return {"c": NC, "x": self.nx, "y": self.ny, "z": NZ, "p": ZP}[axis]

    def place(self, axis):
        return {"c": self.c, "x": self.x, "y": self.y, "z": self.z, "p": self.zm}[axis]

    def gather(self, value, axis, at):
        parts = [value] + [
            self.send(value, axis, -d) for d in range(1, self.size(axis))
        ]
        return jnp.stack(parts, axis=at)

    def scatter(self, value, axis, at):
        total = lax.index_in_dim(value, 0, at, keepdims=False).astype(f32)
        for d in range(1, self.size(axis)):
            part = lax.index_in_dim(value, d, at, keepdims=False)
            total = total + self.send(part, axis, d).astype(f32)
        return total.astype(value.dtype)

    def scatter_absolute(self, value, axis, at):
        n, me = self.size(axis), self.place(axis)
        take = lambda i: lax.dynamic_index_in_dim(value, i, at, keepdims=False)
        total = take(me).astype(f32)
        for d in range(1, n):
            total = total + self.send(take((me + d) % n), axis, d).astype(f32)
        return total.astype(value.dtype)


class Sender:
    def __init__(self, sems):
        self.sems, self.started = sems, []

    def __call__(self, src, dst, sem, target):
        copy = pltpu.make_async_remote_copy(
            src_ref=src,
            dst_ref=dst,
            send_sem=self.sems.at[len(self.started)],
            recv_sem=sem,
            device_id=target,
            device_id_type=pl.DeviceIdType.MESH,
        )
        copy.start()
        self.started.append(copy)

    def finish(self):
        for copy in self.started:
            copy.wait_send()


def arrived(dst, sem):
    pltpu.make_async_copy(dst, dst, sem).wait()


def greet(targets):
    barrier = pltpu.get_barrier_semaphore()
    for target in targets:
        pl.semaphore_signal(
            barrier, inc=1, device_id=target, device_id_type=pl.DeviceIdType.MESH
        )
    pl.semaphore_wait(barrier, len(targets))


def around(grid, zp):
    steps = [(a, b, e) for a in range(zp) for b in range(grid.nx) for e in range(NC)]
    return steps[1:]


def stepped(grid, zp, a, b, e):
    z = grid.z // zp * zp + (grid.z % zp + a) % zp
    return (
        z * grid.ny + grid.y,
        (grid.x + b) % grid.nx * NC + (grid.c + e) % NC,
    )


def gather_kernel(
    grid_of,
    w_ref,
    rows_ref,
    cot_ref,
    ints_ref,
    w_all,
    rows_all,
    cot_all,
    ints_all,
    plane_sem,
    core_sem,
    rows_sem,
    cot_sem,
    ints_sem,
    send_sem,
    local_sem,
    z_in,
    z_out,
    x_out,
    y_out,
    c_out,
):
    grid = grid_of()
    z, y, x, c, nx, ny = grid.z, grid.y, grid.x, grid.c, grid.nx, grid.ny

    def device(tz, ty, tx, tc):
        return (tz * ny + ty, tx * NC + tc)

    def block(dz, dy, dx, tc):
        place = (z + NZ - dz) % NZ * ny + (y + ny - dy) % ny
        return w_all.at[place * (nx * NC) + (x + nx - dx) % nx * NC + tc]

    shift_z = lambda d: (z + d) % NZ
    shift_y = lambda d: (y + d) % ny
    shift_x = lambda d: (x + d) % nx
    back = lambda d: (nx - d) % nx
    other = (c + 1) % NC
    to = functools.partial(stepped, grid, ZP)
    greet(
        [device(shift_z(d), y, x, c) for d in range(1, NZ)]
        + [device(z, shift_y(d), x, c) for d in range(1, ny)]
        + [to(*s) for s in around(grid, ZP)]
    )
    send = Sender(send_sem)
    locals_ = [
        (w_ref, block(0, 0, 0, c)),
        (rows_ref, rows_all.at[0, 0]),
        (cot_ref, cot_all.at[0, 0, 0]),
        (ints_ref, ints_all.at[0, 0, 0]),
    ]
    locals_ = [
        pltpu.make_async_copy(src, dst, local_sem.at[k])
        for k, (src, dst) in enumerate(locals_)
    ]
    for copy in locals_:
        copy.start()
    def start(src, dst, out_sem, in_sem, target):
        pltpu.make_async_remote_copy(
            src_ref=src,
            dst_ref=dst,
            send_sem=out_sem,
            recv_sem=in_sem,
            device_id=target,
            device_id_type=pl.DeviceIdType.MESH,
        ).start()

    def each_source(act, least=0, most=NZ - 1):
        for d in range(least, most + 1):
            for way in range(2):
                there = z - d >= 0 if way == 0 else z + d <= NZ - 1
                pl.when(there)(
                    functools.partial(act, way, d, d if way == 0 else (NZ - d) % NZ)
                )

    def pass_on(way, d, dz):
        here = block(dz, 0, 0, c)
        src = here if d else w_ref
        if d:
            arrived(here, z_in.at[way, d])
        if d < NZ - 1:

            @pl.when(z < NZ - 1 if way == 0 else z > 0)
            def _():
                start(
                    src,
                    here,
                    z_out.at[way, d],
                    z_in.at[way, d + 1],
                    device(z + 1 if way == 0 else z - 1, y, x, c),
                )

        if d or way == 0:
            for b in range(1, nx):
                start(src, here, x_out.at[dz, b], plane_sem.at[dz, 0, b], device(z, y, shift_x(b), c))
            for b in range(1, ny):
                start(src, here, y_out.at[dz, 0, b], plane_sem.at[dz, b, 0], device(z, shift_y(b), x, c))
            start(src, here, c_out.at[dz, 0], core_sem.at[dz, 0, 0], device(z, y, x, other))

    def turn(way, d, dz):
        if d == 0 and way == 1:
            return
        for dx in range(1, nx):
            here = block(dz, 0, dx, c)
            arrived(here, plane_sem.at[dz, 0, dx])
            for b in range(1, ny):
                start(here, here, y_out.at[dz, dx, b], plane_sem.at[dz, b, dx], device(z, shift_y(b), x, c))
            start(here, here, c_out.at[dz, dx], core_sem.at[dz, 0, dx], device(z, y, x, other))

    for a, b, e in around(grid, ZP):
        mirror = ((ZP - a) % ZP, back(b), e)
        send(ints_ref, ints_all.at[mirror], ints_sem.at[mirror], to(a, b, e))
    each_source(pass_on, 0, 0)
    for d in range(1, NZ):
        each_source(pass_on, d, d)
        if d == NZ - 1:
            for a in range(1, ZP):
                send(cot_ref, cot_all.at[ZP - a, 0, 0], cot_sem.at[ZP - a, 0, 0, 0], to(a, 0, 0))
            for b in range(1, nx):
                send(cot_ref, cot_all.at[0, back(b), 0], cot_sem.at[0, back(b), 0, 0], to(0, b, 0))
                send(rows_ref, rows_all.at[back(b), 0], rows_sem.at[back(b), 0], to(0, b, 0))
        each_source(turn, d - 1, d - 1)
    each_source(turn, NZ - 1, NZ - 1)
    send(cot_ref, cot_all.at[0, 0, 1], cot_sem.at[0, 0, 1, 0], to(0, 0, 1))
    send(rows_ref, rows_all.at[0, 1], rows_sem.at[0, 1], to(0, 0, 1))
    for d in range(1, nx):
        here = rows_all.at[d, 0]
        arrived(here, rows_sem.at[d, 0])
        send(here, rows_all.at[d, 1], rows_sem.at[d, 1], to(0, 0, 1))
    width = cot_ref.shape[1]
    halves = [
        (slice(None), pl.ds(0, width // 2)),
        (slice(None), pl.ds(width // 2, width // 2)),
    ]
    for a in range(1, ZP):
        here = cot_all.at[a, 0, 0]
        arrived(here, cot_sem.at[a, 0, 0, 0])
        for b in range(1, nx):
            send(here.at[halves[0]], cot_all.at[a, back(b), 0].at[halves[0]], cot_sem.at[a, back(b), 0, 0], to(0, b, 0))
        send(here, cot_all.at[a, 0, 1], cot_sem.at[a, 0, 1, 0], to(0, 0, 1))
    for b in range(1, nx):
        here = cot_all.at[0, b, 0]
        arrived(here, cot_sem.at[0, b, 0, 0])
        for a in range(1, ZP):
            send(here.at[halves[1]], cot_all.at[ZP - a, b, 0].at[halves[1]], cot_sem.at[ZP - a, b, 0, 1], to(a, 0, 0))
        send(here, cot_all.at[0, b, 1], cot_sem.at[0, b, 1, 0], to(0, 0, 1))
    for dz in range(NZ):
        for dy in range(1, ny):
            for dx in range(nx):
                here = block(dz, dy, dx, c)
                arrived(here, plane_sem.at[dz, dy, dx])
                send(here, here, core_sem.at[dz, dy, dx], device(z, y, x, other))
    for a in range(1, ZP):
        for b in range(1, nx):
            here = cot_all.at[a, b, 0]
            for part in range(2):
                arrived(here.at[halves[part]], cot_sem.at[a, b, 0, part])
            send(here, cot_all.at[a, b, 1], cot_sem.at[a, b, 1, 0], to(0, 0, 1))
    for dx in range(nx):
        arrived(rows_all.at[dx, 1], rows_sem.at[dx, 1])
        for a in range(ZP):
            arrived(cot_all.at[a, dx, 1], cot_sem.at[a, dx, 1, 0])
    for a, b, e in around(grid, ZP):
        arrived(ints_all.at[a, b, e], ints_sem.at[a, b, e])
    for dz in range(NZ):
        for dy in range(ny):
            for dx in range(nx):
                arrived(block(dz, dy, dx, other), core_sem.at[dz, dy, dx])
    for copy in locals_:
        copy.wait()
    send.finish()

    def sent(way, d, dz):
        if d < NZ - 1:

            @pl.when(z < NZ - 1 if way == 0 else z > 0)
            def _():
                arrived(w_ref, z_out.at[way, d])

    each_source(sent)
    for dz in range(NZ):
        for b in range(1, nx):
            arrived(w_ref, x_out.at[dz, b])
        for dx in range(nx):
            for b in range(1, ny):
                arrived(w_ref, y_out.at[dz, dx, b])
            arrived(w_ref, c_out.at[dz, dx])


def gather_first(grid_of, w, rows, cot, ints):
    grid = grid_of()
    nx, ny = grid.nx, grid.ny
    places = NZ * ny * nx * NC
    octet = ZP * nx * NC
    sends = (NZ - 1) + NZ * (nx + ny) + 2 * nx + octet * 4 + NZ * nx * ny * (ny + 1)
    anywhere = pl.BlockSpec(memory_space=pl.ANY)
    dma = pltpu.SemaphoreType.DMA
    return pl.pallas_call(
        functools.partial(gather_kernel, grid_of),
        out_shape=(
            jax.ShapeDtypeStruct((places,) + w.shape, w.dtype),
            jax.ShapeDtypeStruct((nx, NC) + rows.shape, rows.dtype),
            jax.ShapeDtypeStruct((ZP, nx, NC) + cot.shape, cot.dtype),
            jax.ShapeDtypeStruct((ZP, nx, NC) + ints.shape, ints.dtype),
        ),
        in_specs=[anywhere] * 4,
        out_specs=(anywhere,) * 4,
        scratch_shapes=[
            dma((NZ, ny, nx)),
            dma((NZ, ny, nx)),
            dma((nx, NC)),
            dma((ZP, nx, NC, 2)),
            dma((ZP, nx, NC)),
            dma((sends,)),
            dma((4,)),
            dma((2, NZ)),
            dma((2, NZ)),
            dma((NZ, nx)),
            dma((NZ, nx, ny)),
            dma((NZ, nx)),
        ],
        compiler_params=pltpu.CompilerParams(collective_id=0, has_side_effects=True),
    )(w, rows, cot, ints)


def shared_compute(n2, cot, w_in, w_down, out, back, dg, du, dd, h, ag, au):
    hidden, width = w_down.shape
    strip = 256
    for low in range(0, hidden, strip):
        cut = slice(low, min(low + strip, hidden))
        up_cut = slice(hidden + cut.start, hidden + cut.stop)
        gate_act = times(n2[...], w_in[:, cut])
        up_act = times(n2[...], w_in[:, up_cut])
        hidden_grad = times_transposed(cot[...], w_down[cut])
        activated, slope = silu_parts(gate_act)
        h[:, cut] = (activated * up_act).astype(bf16)
        ag[:, cut] = (hidden_grad * up_act * slope).astype(bf16)
        au[:, cut] = (hidden_grad * activated).astype(bf16)
    turned = h[...].T
    for low in range(0, width, strip):
        cut = slice(low, low + strip)
        out[:, cut] = times(h[...], w_down[:, cut])
        back[:, cut] = times_transposed(ag[...], w_in[cut, :hidden]) + times_transposed(
            au[...], w_in[cut, hidden:]
        )
        rows = n2[:, cut].T
        dg[cut] = times(rows, ag[...]).astype(bf16)
        du[cut] = times(rows, au[...]).astype(bf16)
        dd[:, cut] = times(turned, cot[:, cut]).astype(bf16)


def exchange_kernel(grid_of, zp, cut, src, out, plane_sem, core_sem, local_sem, send_sem):
    grid = grid_of()
    nx = grid.nx
    send = Sender(send_sem)
    to = functools.partial(stepped, grid, zp)
    greet([to(*s) for s in around(grid, zp)])
    back = lambda d: (nx - d) % nx
    for a in range(1, zp):
        send(src, out.at[zp - a, 0, 0], plane_sem.at[zp - a, 0, 0], to(a, 0, 0))
    for b in range(1, nx):
        send(src, out.at[0, back(b), 0], plane_sem.at[0, back(b), 0], to(0, b, 0))
    send(src, out.at[0, 0, 1], core_sem.at[0, 0], to(0, 0, 1))
    keep = pltpu.make_async_copy(src, out.at[0, 0, 0], local_sem)
    keep.start()
    h0 = (slice(None), pl.ds(0, cut))
    h1 = (slice(None), pl.ds(cut, src.shape[1] - cut))
    for a in range(1, zp):
        here = out.at[a, 0, 0]
        arrived(here, plane_sem.at[a, 0, 0])
        for b in range(1, nx):
            send(here.at[h0], out.at[a, back(b), 0].at[h0], plane_sem.at[a, back(b), 0], to(0, b, 0))
        send(here, out.at[a, 0, 1], core_sem.at[a, 0], to(0, 0, 1))
    for b in range(1, nx):
        here = out.at[0, b, 0]
        arrived(here, plane_sem.at[0, b, 0])
        for a in range(1, zp):
            send(here.at[h1], out.at[zp - a, b, 0].at[h1], plane_sem.at[zp - a, b, 1], to(a, 0, 0))
        send(here, out.at[0, b, 1], core_sem.at[0, b], to(0, 0, 1))
    for a in range(1, zp):
        for b in range(1, nx):
            here = out.at[a, b, 0]
            arrived(here.at[h0], plane_sem.at[a, b, 0])
            arrived(here.at[h1], plane_sem.at[a, b, 1])
            send(here, out.at[a, b, 1], core_sem.at[a, b], to(0, 0, 1))
    for a in range(zp):
        for b in range(nx):
            arrived(out.at[a, b, 1], core_sem.at[a, b])
    keep.wait()
    send.finish()


def exchange(grid_of, zp, number, rows):
    grid = grid_of()
    nx = grid.nx
    sends = zp * nx * 2 + zp * nx * nx * 2
    anywhere = pl.BlockSpec(memory_space=pl.ANY)
    dma = pltpu.SemaphoreType.DMA
    return pl.pallas_call(
        functools.partial(exchange_kernel, grid_of, zp, rows.shape[1] // 256 * 128),
        out_shape=jax.ShapeDtypeStruct((zp, nx, NC) + rows.shape, rows.dtype),
        in_specs=[anywhere],
        out_specs=anywhere,
        scratch_shapes=[dma((zp, nx, 2)), dma((zp, nx)), dma, dma((sends,))],
        compiler_params=pltpu.CompilerParams(
            collective_id=number, has_side_effects=True
        ),
    )(rows)


def add_into(dst, src, rows):
    for k in range(dst.shape[0]):

        @pl.loop(0, dst.shape[1], step=rows)
        def _(i):
            at = pl.ds(pl.multiple_of(i, rows), rows)
            dst[k, at] = (dst[k, at].astype(f32) + src[k, at].astype(f32)).astype(
                dst.dtype
            )


def sum_kernel(grid_of, zp, cut, small, jobs, parts, *refs):
    grid = grid_of()
    nx = grid.nx
    if small:
        pieces, refs = refs[0], refs[1:]
        shared_ins, refs = refs[:4], refs[4:]
    job_ins, refs = refs[: len(jobs)], refs[len(jobs) :]
    out, refs = refs[0], refs[1:]
    if small:
        pieces_out, refs = refs[0], refs[1:]
        shared_outs, refs = refs[:5], refs[5:]
    job_outs, refs = refs[: len(jobs)], refs[len(jobs) :]
    refs, (job_send, job_recv) = refs[:-2], refs[-2:]
    if small:
        shared_held, load_sem, refs = refs[-8:-1], refs[-1], refs[:-8]
        loads = [
            pltpu.make_async_copy(a, b, load_sem.at[k])
            for k, (a, b) in enumerate(zip(shared_ins, shared_held))
        ]
    each = functools.partial(each_job, grid, jobs, job_ins, job_outs, job_send, job_recv)
    own, got_c, turn_x, turn_p, got_p, got_x = refs[:6]
    local_sem, c_sem, turn_sem, p_sem, x_sem, small_sem, send_sem = refs[6:]
    send = Sender(send_sem)
    to = functools.partial(stepped, grid, zp)
    greet([to(*s) for s in around(grid, zp)] + job_targets(grid, jobs))
    width = parts.shape[-1]
    h0, h1 = pl.ds(0, cut), pl.ds(cut, width - cut)
    order = (
        [(a, b) for a in range(1, zp) for b in range(1, nx)]
        + [(a, 0) for a in range(1, zp)]
        + [(0, b) for b in range(1, nx)]
        + [(0, 0)]
    )
    for a, b in order:
        send(parts.at[:, a, b, 1], got_c.at[:, a, b], c_sem.at[a, b], to(0, 0, 1))
        pltpu.make_async_copy(
            parts.at[:, a, b, 0], own.at[:, a, b], local_sem.at[a, b]
        ).start()
    if small:
        for a, b, e in around(grid, zp):
            mirror = ((zp - a) % zp, (nx - b) % nx, e)
            send(
                pieces.at[a, b, e],
                pieces_out.at[mirror],
                small_sem.at[mirror],
                to(a, b, e),
            )
        pltpu.make_async_copy(
            pieces.at[0, 0, 0], pieces_out.at[0, 0, 0], small_sem.at[0, 0, 0]
        ).start()
    each(lambda copy: copy.start())
    if small:
        for load in loads:
            load.start()
    rows = 32

    def ready(a, b):
        arrived(got_c.at[:, a, b], c_sem.at[a, b])
        pltpu.make_async_copy(
            parts.at[:, a, b, 0], own.at[:, a, b], local_sem.at[a, b]
        ).wait()
        add_into(own.at[:, a, b], got_c.at[:, a, b], rows)

    for a in range(1, zp):
        for b in range(1, nx):
            ready(a, b)
            send(own.at[:, a, b, :, h0], turn_x.at[:, a - 1, b - 1], turn_sem.at[a - 1, b - 1, 0], to(0, b, 0))
            send(own.at[:, a, b, :, h1], turn_p.at[:, a - 1, b - 1], turn_sem.at[a - 1, b - 1, 1], to(a, 0, 0))
    for a in range(1, zp):
        ready(a, 0)
    for b in range(1, nx):
        ready(0, b)
    for a in range(1, zp):
        for b in range(1, nx):
            arrived(turn_x.at[:, a - 1, b - 1], turn_sem.at[a - 1, b - 1, 0])
            add_into(own.at[:, a, 0, :, h0], turn_x.at[:, a - 1, b - 1], rows)
        send(own.at[:, a, 0], got_p.at[:, a - 1], p_sem.at[a - 1], to(a, 0, 0))
    for b in range(1, nx):
        for a in range(1, zp):
            arrived(turn_p.at[:, a - 1, b - 1], turn_sem.at[a - 1, b - 1, 1])
            add_into(own.at[:, 0, b, :, h1], turn_p.at[:, a - 1, b - 1], rows)
        send(own.at[:, 0, b], got_x.at[:, b - 1], x_sem.at[b - 1], to(0, b, 0))
    ready(0, 0)
    if small:
        for load in loads:
            load.wait()
        shared_compute(*shared_held[:4], *shared_outs, *shared_held[4:])
    for a in range(1, zp):
        arrived(got_p.at[:, a - 1], p_sem.at[a - 1])
        add_into(own.at[:, 0, 0], got_p.at[:, a - 1], rows)
    for b in range(1, nx):
        arrived(got_x.at[:, b - 1], x_sem.at[b - 1])
        add_into(own.at[:, 0, 0], got_x.at[:, b - 1], rows)
    result = pltpu.make_async_copy(own.at[:, 0, 0], out, local_sem.at[0, 0])
    result.start()
    if small:
        for a, b, e in [(0, 0, 0)] + around(grid, zp):
            arrived(pieces_out.at[a, b, e], small_sem.at[a, b, e])
    result.wait()
    each(lambda copy: copy.wait())
    send.finish()


def sum_around(grid_of, zp, number, parts, pieces=None, shared=(), jobs=(), job_arrays=()):
    grid = grid_of()
    nx = grid.nx
    payloads, rows, width = parts.shape[0], parts.shape[-2], parts.shape[-1]
    cut = width // 640 * 512
    anywhere = pl.BlockSpec(memory_space=pl.ANY)
    dma = pltpu.SemaphoreType.DMA
    small = pieces is not None
    out_shape = [jax.ShapeDtypeStruct((payloads, rows, width), parts.dtype)]
    args = [parts]
    if small:
        out_shape.append(jax.ShapeDtypeStruct(pieces.shape, pieces.dtype))
        args += [pieces, *shared]
        tokens, hidden = shared[0].shape[0], shared[3].shape[0]
        out_shape += [jax.ShapeDtypeStruct((tokens, width), f32)] * 2
        out_shape += [jax.ShapeDtypeStruct((width, hidden), bf16)] * 2
        out_shape.append(jax.ShapeDtypeStruct((hidden, width), bf16))
    plain = len(out_shape)
    out_shape += job_shapes(grid, jobs, job_arrays)
    args += list(job_arrays)
    turns = (max(zp - 1, 1), max(nx - 1, 1))
    vmem = lambda shape: pltpu.VMEM(shape, parts.dtype)
    made = pl.pallas_call(
        functools.partial(sum_kernel, grid_of, zp, cut, small, jobs),
        out_shape=tuple(out_shape),
        in_specs=[anywhere] * len(args),
        out_specs=tuple(
            pl.BlockSpec(memory_space=pltpu.VMEM) if 2 <= n < plain else anywhere
            for n in range(len(out_shape))
        ),
        scratch_shapes=[
            vmem((payloads, zp, nx, rows, width)),
            vmem((payloads, zp, nx, rows, width)),
            vmem((payloads,) + turns + (rows, cut)),
            vmem((payloads,) + turns + (rows, width - cut)),
            vmem((payloads, turns[0], rows, width)),
            vmem((payloads, turns[1], rows, width)),
            dma((zp, nx)),
            dma((zp, nx)),
            dma(turns + (2,)),
            dma((turns[0],)),
            dma((turns[1],)),
            dma((zp, nx, NC)),
            dma((zp * nx * 6 + 8,)),
        ]
        + (
            [pltpu.VMEM(v.shape, bf16) for v in shared]
            + [pltpu.VMEM((tokens, hidden), bf16)] * 3
            + [dma((4,))]
            if small
            else []
        )
        + job_sems(grid, jobs),
        compiler_params=pltpu.CompilerParams(
            collective_id=number,
            has_side_effects=True,
            vmem_limit_bytes=56 * 2**20,
        ),
    )(*args)
    return made[:plain], made[plain:]


def attention_kernel(q_ref, k_ref, v_ref, bias_ref, out_ref):
    scores = times_transposed(q_ref[...], k_ref[...]) * HD ** (-0.5) + bias_ref[...]
    weights = jnp.exp(scores - jnp.max(scores, axis=1, keepdims=True))
    probs = weights * (1.0 / jnp.sum(weights, axis=1, keepdims=True))
    out_ref[...] = times(probs.astype(bf16), v_ref[...]).astype(bf16)


def attention_forward(queries, keys, values, bias):
    rows, width = queries.shape
    length = keys.shape[0]
    by_head = lambda n: pl.BlockSpec((n, HD), lambda h: (0, h))
    return pl.pallas_call(
        attention_kernel,
        grid=(width // HD,),
        out_shape=jax.ShapeDtypeStruct((rows, width), bf16),
        in_specs=[
            by_head(rows),
            by_head(length),
            by_head(length),
            pl.BlockSpec((rows, length), lambda h: (0, 0)),
        ],
        out_specs=by_head(rows),
        compiler_params=pltpu.CompilerParams(vmem_limit_bytes=40 * 2**20),
        cost_estimate=pl.CostEstimate(
            flops=4 * rows * length * width,
            bytes_accessed=4 * (rows + length) * width + 4 * rows * length,
            transcendentals=rows * length * width // HD,
        ),
    )(queries, keys, values, bias)


def attention_back_kernel(grid_of, jobs, q_ref, k_ref, v_ref, g_ref, bias_ref, *refs):
    grid = grid_of()
    count = len(jobs)
    dq_ref, parts_ref = refs[count : count + 2]
    job_send, job_recv = refs[-2:]
    each = functools.partial(
        each_job, grid, jobs, refs[:count], refs[count + 2 : -2], job_send, job_recv
    )
    if jobs:

        @pl.when(pl.program_id(0) == 0)
        def _():
            greet(job_targets(grid, jobs))
            each(lambda copy: copy.start())

    q, k, g = q_ref[...], k_ref[...], g_ref[...]
    scores = times_transposed(k, q) * HD ** (-0.5) + bias_ref[...]
    weights = jnp.exp(scores - jnp.max(scores, axis=0, keepdims=True))
    probs = weights * (1.0 / jnp.sum(weights, axis=0, keepdims=True))
    prob_grad = times_transposed(v_ref[...], g)
    centre = jnp.sum(probs * prob_grad, axis=0, keepdims=True)
    score_grad = (probs * (prob_grad - centre)).astype(bf16)
    parts_ref[0] = times(probs.astype(bf16), g).astype(bf16)
    parts_ref[1] = (times(score_grad, q) * HD ** (-0.5)).astype(bf16)
    dq_ref[...] = (contract_rows(score_grad, k) * HD ** (-0.5)).astype(bf16)
    if jobs:

        @pl.when(pl.program_id(0) == pl.num_programs(0) - 1)
        def _():
            each(lambda copy: copy.wait())


def attention_backward(grid_of, number, queries, keys, values, grads, bias, jobs, job_arrays):
    grid = grid_of()
    rows, width = queries.shape
    length = keys.shape[0]
    by_head = lambda n: pl.BlockSpec((n, HD), lambda h: (0, h))
    anywhere = pl.BlockSpec(memory_space=pl.ANY)
    made = pl.pallas_call(
        functools.partial(attention_back_kernel, grid_of, jobs),
        grid=(width // HD,),
        out_shape=tuple(
            [
                jax.ShapeDtypeStruct((rows, width), bf16),
                jax.ShapeDtypeStruct((2, length, width), bf16),
            ]
            + job_shapes(grid, jobs, job_arrays)
        ),
        in_specs=[
            by_head(rows),
            by_head(length),
            by_head(length),
            by_head(rows),
            pl.BlockSpec((length, rows), lambda h: (0, 0)),
        ]
        + [anywhere] * len(jobs),
        out_specs=(by_head(rows), pl.BlockSpec((2, length, HD), lambda h: (0, 0, h)))
        + (anywhere,) * len(jobs),
        scratch_shapes=job_sems(grid, jobs),
        compiler_params=pltpu.CompilerParams(
            vmem_limit_bytes=40 * 2**20,
            **(dict(collective_id=number, has_side_effects=True) if jobs else {}),
        ),
        cost_estimate=pl.CostEstimate(
            flops=10 * rows * length * width,
            bytes_accessed=6 * rows * width + 8 * length * width + 4 * rows * length,
            transcendentals=rows * length * width // HD,
        ),
    )(queries, keys, values, grads, bias, *job_arrays)
    return made[0], made[1], made[2:]


ROW_SOURCES = 2


def expert_kernel(grid_of, capacity, steps, jobs, carry, *refs):
    grid = grid_of()
    count = len(jobs)
    take = lambda n: (refs[:n], refs[n:])
    (rows_ref, cot_ref, rank_row_ref, rank_col_ref, gate_ref, wg_ref, wu_ref, wd_ref), refs = take(8)
    before, refs = take(1 if carry else 0)
    job_ins, refs = take(count)
    (parts_ref, prob_ref, dg_ref, du_ref, dd_ref), refs = take(5)
    job_outs, refs = take(count)
    (x_keep, s_keep, c_keep, h_keep, ag_keep, au_keep, ht_keep), refs = take(7)
    each = functools.partial(each_job, grid, jobs, job_ins, job_outs, *refs)
    step = pl.program_id(0)
    width, hidden = x_keep.shape[1], h_keep.shape[1]
    tokens = rows_ref.shape[1]
    size = ROW_SOURCES * capacity
    strip = 256
    if jobs:

        @pl.when(step == 0)
        def _():
            greet(job_targets(grid, jobs))
            each(lambda copy: copy.start())

    @pl.when(step < steps)
    def _():
        at = pl.ds(pl.multiple_of(step * size, 32), size)
        picks, columns, gates = [], [], []
        for s in range(ROW_SOURCES):
            slots = lax.broadcasted_iota(jnp.int32, (capacity, tokens), 0)
            hit = slots == rank_row_ref[s]
            gate = jnp.sum(jnp.where(hit, gate_ref[s], 0.0), axis=1, keepdims=True)
            pick = hit.astype(f32).astype(bf16)
            picks.append(hit)
            gates.append(gate)
            across = lax.broadcasted_iota(jnp.int32, (tokens, capacity), 1)
            columns.append((across == rank_col_ref[s]).astype(f32).astype(bf16))
            to = pl.ds(pl.multiple_of(step * size + s * capacity, 16), capacity)
            x_keep[to] = times(pick, rows_ref[s]).astype(bf16)
            cot = times(pick, cot_ref[s])
            c_keep[pl.ds(s * capacity, capacity)] = cot.astype(bf16)
            s_keep[to] = (gate * cot).astype(bf16)
        x, slot = x_keep[at], s_keep[at]
        for low in range(0, hidden, strip):
            cut = slice(low, min(low + strip, hidden))
            gate_act = times(x, wg_ref[0, :, cut])
            up_act = times(x, wu_ref[0, :, cut])
            hidden_grad = times_transposed(slot, wd_ref[0, cut])
            activated, slope = silu_parts(gate_act)
            h_keep[at, cut] = (activated * up_act).astype(bf16)
            ag_keep[at, cut] = (hidden_grad * up_act * slope).astype(bf16)
            au_keep[at, cut] = (hidden_grad * activated).astype(bf16)
        h, ag, au = h_keep[at], ag_keep[at], au_keep[at]
        probs = jnp.zeros((size, 1), f32)
        for low in range(0, width, strip):
            cut = slice(low, low + strip)
            made = times(h, wd_ref[0, :, cut]).astype(bf16).astype(f32)
            probs += jnp.sum(made * c_keep[:, cut].astype(f32), axis=1, keepdims=True)
            back = (
                times_transposed(ag, wg_ref[0, cut]) + times_transposed(au, wu_ref[0, cut])
            ).astype(bf16)
            for s in range(ROW_SOURCES):
                mine = slice(s * capacity, (s + 1) * capacity)
                row = times(columns[s], back[mine])
                out = times(columns[s], (gates[s] * made[mine]).astype(bf16))
                if carry:
                    row += before[0][0, s, :, cut].astype(f32)
                    out += before[0][1, s, :, cut].astype(f32)
                parts_ref[0, s, :, cut] = row.astype(bf16)
                parts_ref[1, s, :, cut] = out.astype(bf16)
        for s in range(ROW_SOURCES):
            mine = slice(s * capacity, (s + 1) * capacity)
            prob_ref[s] = jnp.sum(
                jnp.where(picks[s], probs[mine], 0.0), axis=0, keepdims=True
            )

    @pl.when(step == steps)
    def _():
        ht_keep[...] = h_keep[...].T

    @pl.when(step >= steps)
    def _():
        cut = pl.ds(pl.multiple_of((step - steps) * strip, strip), strip)
        turned = x_keep[:, cut].T
        dg_ref[...] = times(turned, ag_keep[...]).astype(bf16)
        du_ref[...] = times(turned, au_keep[...]).astype(bf16)
        dd_ref[...] = times(ht_keep[...], s_keep[:, cut]).astype(bf16)

    if jobs:

        @pl.when(step == pl.num_programs(0) - 1)
        def _():
            each(lambda copy: copy.wait())


def run_expert(grid_of, number, expert, rows, cot, ranks, gates, weights, capacity, before, jobs, job_arrays):
    grid = grid_of()
    sources, tokens = ranks.shape
    width, hidden = weights[0].shape[1:]
    mine = weights[0].shape[0] // ZP
    steps = sources // ROW_SOURCES
    strip = 256
    strips = width // strip
    total = sources * capacity
    turn = lambda s: jnp.minimum(s, steps - 1)
    later = lambda s: jnp.maximum(s - steps, 0)
    block = pl.BlockSpec
    by_source = lambda *rest: block(
        (ROW_SOURCES,) + rest, lambda s: (turn(s),) + (0,) * len(rest)
    )
    held = lambda *rest: block(
        (1,) + rest,
        lambda s: (lax.axis_index("wide") // grid.ny % ZP * mine + expert, 0, 0),
    )
    parts = block((2, ROW_SOURCES, tokens, width), lambda s: (0, turn(s), 0, 0))
    anywhere = block(memory_space=pl.ANY)
    carry = before is not None
    made = pl.pallas_call(
        functools.partial(expert_kernel, grid_of, capacity, steps, jobs, carry),
        grid=(steps + strips,),
        in_specs=[
            by_source(tokens, width),
            by_source(tokens, width),
            by_source(1, tokens),
            by_source(tokens, 1),
            by_source(1, tokens),
            held(width, hidden),
            held(width, hidden),
            held(hidden, width),
        ]
        + [parts] * carry
        + [anywhere] * len(jobs),
        out_specs=[
            parts,
            by_source(1, tokens),
            block((strip, hidden), lambda s: (later(s), 0)),
            block((strip, hidden), lambda s: (later(s), 0)),
            block((hidden, strip), lambda s: (0, later(s))),
        ]
        + [anywhere] * len(jobs),
        scratch_shapes=[
            pltpu.VMEM((total, width), bf16),
            pltpu.VMEM((total, width), bf16),
            pltpu.VMEM((ROW_SOURCES * capacity, width), bf16),
            pltpu.VMEM((total, hidden), bf16),
            pltpu.VMEM((total, hidden), bf16),
            pltpu.VMEM((total, hidden), bf16),
            pltpu.VMEM((hidden, total), bf16),
        ]
        + job_sems(grid, jobs),
        out_shape=[
            jax.ShapeDtypeStruct((2, sources, tokens, width), bf16),
            jax.ShapeDtypeStruct((sources, 1, tokens), f32),
            jax.ShapeDtypeStruct((width, hidden), bf16),
            jax.ShapeDtypeStruct((width, hidden), bf16),
            jax.ShapeDtypeStruct((hidden, width), bf16),
        ]
        + job_shapes(grid, jobs, job_arrays),
        compiler_params=pltpu.CompilerParams(
            vmem_limit_bytes=58 * 2**20,
            **(dict(collective_id=number, has_side_effects=True) if jobs else {}),
        ),
        cost_estimate=pl.CostEstimate(
            flops=total * width * hidden * 18,
            bytes_accessed=width * hidden * 12 + 16 * sources * tokens * width,
            transcendentals=total * hidden,
        ),
    )(
        rows,
        cot,
        ranks[:, None, :],
        ranks[:, :, None],
        gates[:, None, :],
        *weights,
        *([before] if carry else []),
        *job_arrays,
    )
    return made[:5], made[5:]


def jobs_count(grid, jobs):
    return sum({"y": grid.ny, "z": NZ}[axis] - 1 for axis in jobs)


def job_targets(grid, jobs):
    axes = set(jobs)
    place = lambda z, y: (z * grid.ny + y, grid.x * NC + grid.c)
    made = []
    if "y" in axes:
        made += [place(grid.z, (grid.y + d) % grid.ny) for d in range(1, grid.ny)]
    if "z" in axes:
        made += [place((grid.z + d) % NZ, grid.y) for d in range(1, NZ)]
    return made


def each_job(grid, jobs, ins, outs, send_sem, recv_sem, act):
    at = 0
    for axis, src, out in zip(jobs, ins, outs):
        for d in range(1, {"y": grid.ny, "z": NZ}[axis]):
            if axis == "y":
                to = (grid.y + d) % grid.ny
                piece, target = src.at[:, to], (grid.z * grid.ny + to)
            else:
                to = (grid.z + d) % NZ
                piece, target = src.at[to], (to * grid.ny + grid.y)
            act(
                pltpu.make_async_remote_copy(
                    src_ref=piece,
                    dst_ref=out.at[d - 1],
                    send_sem=send_sem.at[at],
                    recv_sem=recv_sem.at[at],
                    device_id=(target, grid.x * NC + grid.c),
                    device_id_type=pl.DeviceIdType.MESH,
                )
            )
            at += 1


def job_shapes(grid, jobs, arrays):
    made = []
    for axis, v in zip(jobs, arrays):
        shape = (grid.ny - 1, NZ) + v.shape[2:] if axis == "y" else (NZ - 1,) + v.shape[1:]
        made.append(jax.ShapeDtypeStruct(shape, v.dtype))
    return made


def job_sems(grid, jobs):
    count = max(jobs_count(grid, jobs), 1)
    return [pltpu.SemaphoreType.DMA((count,)), pltpu.SemaphoreType.DMA((count,))]


def dense_kernel(grid_of, orders, jobs, items, *refs):
    grid = grid_of()
    z, y, x, c, nx, ny = grid.z, grid.y, grid.x, grid.c, grid.nx, grid.ny
    count, more = len(orders), len(jobs)
    wholes = items[-1][0] + 1
    take = lambda n: (refs[:n], refs[n:])
    ins, refs = take(wholes)
    job_ins, refs = take(more)
    outs, refs = take(wholes)
    job_outs, refs = take(more)
    strip = lambda v, low, wide: v.at[(slice(None),) * (len(v.shape) - 1) + (pl.ds(low, wide),)]
    ins = [strip(ins[k], low, wide) for k, low, wide in items]
    outs = [strip(outs[k], low, wide) for k, low, wide in items]
    held, refs = take(count)
    got_c, refs = take(count)
    got_one, refs = take(count)
    got_two, refs = take(count)
    got_z, refs = take(count)
    local_sem, c_sem, one_sem, two_sem, z_sem, out_sem, send_sem, job_send, job_recv = refs
    device = lambda tz, ty, tx, tc: (tz * ny + ty, tx * NC + tc)
    other = (c + 1) % NC
    greet(
        [device(z, y, x, other)]
        + [device(z, y, (x + d) % nx, c) for d in range(1, nx)]
        + [device(z, (y + d) % ny, x, c) for d in range(1, ny)]
        + [device((z + d) % NZ, y, x, c) for d in range(1, NZ)]
    )
    send = Sender(send_sem)
    loads = []

    def begin(k):
        send(ins[k].at[:, :, :, other], got_c[k], c_sem.at[k], device(z, y, x, other))
        load = pltpu.make_async_copy(ins[k].at[:, :, :, c], held[k], local_sem.at[k])
        load.start()
        loads.append(load)

    for k in range(min(3, count)):
        begin(k)
    each_job(grid, jobs, job_ins, job_outs, job_send, job_recv, lambda copy: copy.start())

    def add(dst, src):
        lead = dst.shape[:-2]
        total = 1
        for n in lead:
            total *= n

        @pl.loop(0, total)
        def _(i):
            index = []
            for n in reversed(lead):
                index.insert(0, i % n)
                i = i // n
            index = tuple(index)
            dst[index] = (dst[index].astype(f32) + src[index].astype(f32)).astype(dst.dtype)

    def first(k):
        if k + 3 < count:
            begin(k + 3)
        loads[k].wait()
        arrived(got_c[k], c_sem.at[k])
        add(held[k], got_c[k])
        if orders[k] == "xy":
            for d in range(1, nx):
                to = (x + d) % nx
                send(held[k].at[:, :, to], got_one[k].at[d - 1], one_sem.at[k, d - 1], device(z, y, to, c))
        else:
            for d in range(1, ny):
                to = (y + d) % ny
                send(held[k].at[:, to], got_one[k].at[d - 1], one_sem.at[k, d - 1], device(z, to, x, c))

    def second(k):
        mine = held[k].at[:, :, x] if orders[k] == "xy" else held[k].at[:, y]
        for d in range(1, nx if orders[k] == "xy" else ny):
            arrived(got_one[k].at[d - 1], one_sem.at[k, d - 1])
            add(mine, got_one[k].at[d - 1])
        if orders[k] == "xy":
            for d in range(1, ny):
                to = (y + d) % ny
                send(held[k].at[:, to, x], got_two[k].at[d - 1], two_sem.at[k, d - 1], device(z, to, x, c))
        else:
            for d in range(1, nx):
                to = (x + d) % nx
                send(held[k].at[:, y, to], got_two[k].at[d - 1], two_sem.at[k, d - 1], device(z, y, to, c))

    results = []

    def third(k):
        mine = held[k].at[:, y, x]
        for d in range(1, ny if orders[k] == "xy" else nx):
            arrived(got_two[k].at[d - 1], two_sem.at[k, d - 1])
            add(mine, got_two[k].at[d - 1])
        near = z // ZP * ZP + (z + 1) % ZP
        for n in range(NZ // ZP):
            to = (z + 1) % ZP + n * ZP
            send(held[k].at[to, y, x], got_z[k].at[n], z_sem.at[k, n], device(near, y, x, c))

    def fourth(k):
        for n in range(NZ // ZP):
            arrived(got_z[k].at[n], z_sem.at[k, n])
            at = (z % ZP + n * ZP, y, x)
            held[k][at] = (held[k][at].astype(f32) + got_z[k][n].astype(f32)).astype(held[k].dtype)
        for n in range(1, NZ // ZP):
            to = (z + n * ZP) % NZ
            send(held[k].at[to, y, x], outs[k].at[n], z_sem.at[k, NZ // ZP + n - 1], device(to, y, x, c))
        result = pltpu.make_async_copy(held[k].at[z, y, x], outs[k].at[0], out_sem.at[k])
        result.start()
        results.append(result)

    for t in range(count + 6):
        for stage, late in ((first, 0), (second, 2), (third, 4), (fourth, 6)):
            if 0 <= t - late < count:
                stage(t - late)
    for k in range(count):
        for n in range(1, NZ // ZP):
            arrived(outs[k].at[n], z_sem.at[k, NZ // ZP + n - 1])
        results[k].wait()
    each_job(grid, jobs, job_ins, job_outs, job_send, job_recv, lambda copy: copy.wait())
    send.finish()


def reduce_dense(grid_of, number, arrays, jobs, job_arrays):
    grid = grid_of()
    nx, ny = grid.nx, grid.ny
    items = []
    for k, v in enumerate(arrays):
        wide = v.shape[5]
        low = wide // 2 if wide % 256 == 0 else wide
        items += [(k, at, low) for at in range(0, wide, low)]
    orders = ["xy" if n % 2 == 0 else "yx" for n in range(len(items))]
    count = len(items)
    anywhere = pl.BlockSpec(memory_space=pl.ANY)
    dma = pltpu.SemaphoreType.DMA
    block = [(arrays[k].shape[4], wide) for k, _, wide in items]
    kind = [arrays[k].dtype for k, _, _ in items]
    far = max(nx, ny)
    held = [pltpu.VMEM((NZ, ny, nx) + b, t) for b, t in zip(block, kind)]
    one = [
        pltpu.VMEM((nx - 1, NZ, ny) + b if o == "xy" else (ny - 1, NZ, nx) + b, t)
        for b, t, o in zip(block, kind, orders)
    ]
    two = [
        pltpu.VMEM(((ny if o == "xy" else nx) - 1, NZ) + b, t)
        for b, t, o in zip(block, kind, orders)
    ]
    made = pl.pallas_call(
        functools.partial(dense_kernel, grid_of, orders, jobs, items),
        out_shape=tuple(
            [jax.ShapeDtypeStruct((NZ // ZP,) + v.shape[4:], v.dtype) for v in arrays]
            + job_shapes(grid, jobs, job_arrays)
        ),
        in_specs=[anywhere] * (len(arrays) + len(jobs)),
        out_specs=(anywhere,) * (len(arrays) + len(jobs)),
        scratch_shapes=held
        + held
        + one
        + two
        + [pltpu.VMEM((NZ // ZP,) + b, t) for b, t in zip(block, kind)]
        + [
            dma((count,)),
            dma((count,)),
            dma((count, far)),
            dma((count, far)),
            dma((count, NZ - 1)),
            dma((count,)),
            dma((count * (1 + nx + ny + NZ),)),
        ]
        + job_sems(grid, jobs),
        compiler_params=pltpu.CompilerParams(
            collective_id=number,
            has_side_effects=True,
            vmem_limit_bytes=60 * 2**20,
        ),
    )(*arrays, *job_arrays)
    return made[: len(arrays)], made[len(arrays) :]


def finish_kernel(grid_of, mine, dense, *refs):
    grid = grid_of()
    kinds = 3
    names = mine * kinds
    own, far = refs[:names], refs[names : 2 * names]
    terms = refs[2 * names : 2 * names + dense]
    outs = refs[2 * names + dense :]
    for n in range(names):
        i, kind = n // kinds, n % kinds
        sums = [own[n][0].astype(f32), None]
        for d in range(1, NZ):
            got = far[n][d - 1].astype(f32)
            sums[d % ZP] = got if sums[d % ZP] is None else sums[d % ZP] + got
        outs[kind][grid.zm, i] = sums[0]
        outs[kind][1 - grid.zm, i] = sums[1]
    for n in range(dense):
        total = terms[n][0].astype(f32)
        for d in range(1, terms[n].shape[0]):
            total = total + terms[n][d].astype(f32)
        outs[kinds + n][...] = total


def finish(grid_of, mine, columns, far, terms):
    grid = grid_of()
    whole = lambda v: pl.BlockSpec(v.shape, lambda _: (0,) * len(v.shape))
    out_shape = [
        jax.ShapeDtypeStruct((ZP, mine) + columns[k].shape[1:], f32) for k in range(3)
    ] + [jax.ShapeDtypeStruct(v.shape[1:], f32) for v in terms]
    return pl.pallas_call(
        functools.partial(finish_kernel, grid_of, mine, len(terms)),
        grid=(1,),
        out_shape=out_shape,
        in_specs=[
            pl.BlockSpec(
                (1,) + v.shape[1:],
                lambda _: (lax.axis_index("wide") // grid.ny, 0, 0),
            )
            for v in columns
        ]
        + [whole(v) for v in far]
        + [whole(v) for v in terms],
        out_specs=[whole(v) for v in out_shape],
        compiler_params=pltpu.CompilerParams(vmem_limit_bytes=62 * 2**20),
    )(*columns, *far, *terms)


def attention_bias(segment, labels_all, query_places, key_places):
    same_doc = segment[:, None] == labels_all[None, :]
    allowed = same_doc & (query_places[:, None] >= key_places[None, :])
    return jnp.where(allowed, 0.0, masked_value).astype(f32)


def body(
    wide,
    ep,
    activations,
    segment,
    routes,
    gain_attention,
    query_weight,
    key_weight,
    value_weight,
    output_weight,
    gain_experts,
    router_weight,
    shared_gate,
    shared_up,
    shared_down,
    expert_gate,
    expert_up,
    expert_down,
    cotangent,
):
    grid_of = functools.partial(Grid, wide, ep)
    grid = grid_of()
    nx, ny = grid.nx, grid.ny
    tok_rows, width = activations.shape
    heads = width // HD
    top_count = routes.shape[1]
    experts = router_weight.shape[1]
    local_experts = expert_gate.shape[0]
    mine = local_experts // ZP
    hidden_width = expert_gate.shape[2]
    sources = ZP * nx * NC
    capacity = min((tok_rows * top_count * 10 // (7 * experts) + 7) // 8 * 8, tok_rows)

    bundle = jnp.concatenate(
        [
            query_weight,
            key_weight,
            value_weight,
            output_weight,
            router_weight,
            gain_attention[:, None],
            gain_experts[:, None],
            jnp.zeros((gain_experts.shape[0], 128 - experts - 2), bf16),
        ],
        axis=1,
    )
    integers = jnp.concatenate([routes.T, segment[None, :]], axis=0)
    bundle_all, group_rows, cot_all, integers_all = gather_first(
        grid_of, bundle, activations, cotangent, integers
    )
    group_rows = group_rows.reshape(-1, width)
    integers_all = integers_all.reshape(sources, top_count + 1, tok_rows)
    bundle_all = bundle_all.reshape(width, bundle.shape[1])
    w_query, w_key, w_value, w_out = (
        bundle_all[:, i * width : (i + 1) * width] for i in range(4)
    )
    small_all = bundle_all[:, 4 * width :]
    gather_all = lambda v: lax.all_gather(v, BOTH, axis=0, tiled=True)
    shared_in, shared_out_in, integers_all = lax.optimization_barrier(
        (
            jnp.concatenate([shared_gate, shared_up], axis=1),
            shared_down,
            integers_all,
        )
    )
    s_both = gather_all(shared_in)
    s_down = gather_all(shared_out_in)
    w_router = small_all[:, :experts]
    gain_one = small_all[:, experts].astype(f32)
    gain_two = small_all[:, experts + 1].astype(f32)

    inputs = activations.astype(f32)
    inverse_one = norm_scale(inputs)
    group_inputs = group_rows.astype(f32)
    normed_group = (group_inputs * norm_scale(group_inputs) * gain_one).astype(bf16)
    normed_one = normed_group[:tok_rows]
    queries = times(normed_one, w_query).astype(bf16)
    keys_all = times(normed_group, w_key).astype(bf16)
    values_all = times(normed_group, w_value).astype(bf16)
    labels_all = integers_all[: nx * NC, top_count].reshape(-1)
    steps = jnp.arange(tok_rows, dtype=jnp.int32)
    block_places = (
        (grid.x + jnp.arange(nx, dtype=jnp.int32)[:, None]) % nx * NC
        + (grid.c + jnp.arange(NC, dtype=jnp.int32)[None, :]) % NC
    ).reshape(-1)
    key_places = (block_places[:, None] * tok_rows + steps[None, :]).reshape(-1)
    query_places = (grid.x * NC + grid.c) * tok_rows + steps
    bias = attention_bias(segment, labels_all, query_places, key_places)
    attended = attention_forward(queries, keys_all, values_all, bias)
    middle = inputs + times(attended, w_out)
    inverse_two = norm_scale(middle)
    normed_two = (middle * inverse_two * gain_two).astype(bf16)

    rows_all = exchange(grid_of, ZP, 1, normed_two)
    rows_all = rows_all.reshape(sources, tok_rows, width)
    cot_all = cot_all.reshape(sources, tok_rows, width)
    router_probs_all = jax.nn.softmax(
        times(rows_all.reshape(-1, width), w_router).reshape(sources, tok_rows, experts),
        axis=-1,
    )
    router_probs = router_probs_all[0]
    first_expert = (grid.x * NC + grid.c) * local_experts + grid.zm * mine
    routes_all = integers_all[:, :top_count]
    numbers = first_expert + jnp.arange(mine, dtype=jnp.int32)
    marks = jnp.any(
        routes_all[None] == numbers[:, None, None, None], axis=2
    )
    earlier = (steps[:, None] < steps[None, :]).astype(bf16)
    ranks = jnp.einsum(
        "irt,tu->iru", marks.astype(bf16), earlier, preferred_element_type=f32
    ).astype(jnp.int32)
    ranks = jnp.where(marks, ranks, -1)
    gates_mine = jnp.moveaxis(
        lax.dynamic_slice_in_dim(router_probs_all, first_expert, mine, axis=2), 2, 0
    )
    def by_wide(v):
        return v.reshape(NZ, ny, v.shape[0] // wide, v.shape[1])

    names = [(i, k) for i in range(mine) for k in range(3)]
    grads, along_y, along_z = {}, {}, {}

    def jobs_of(which_y, which_z):
        tags = tuple("y" for _ in which_y) + tuple("z" for _ in which_z)
        return tags, [grads[n] for n in which_y] + [column[n] for n in which_z]

    def landed(which_y, which_z, moved):
        along_y.update(zip(which_y, moved))
        along_z.update(zip(which_z, moved[len(which_y) :]))

    def summed(name):
        total = lax.dynamic_index_in_dim(grads[name], grid.y, 1, keepdims=False).astype(f32)
        for d in range(ny - 1):
            total = total + along_y[name][d].astype(f32)
        return total.astype(bf16)

    column = {}
    both_parts = None
    prob_parts = []
    for i in range(mine):
        behind = (names[3 * i - 3 : 3 * i - 1], []) if i else ([], [])
        (both_parts, probs_here, *made), moved = run_expert(
            grid_of,
            5 + i,
            i,
            rows_all,
            cot_all,
            ranks[i],
            gates_mine[i],
            (expert_gate, expert_up, expert_down),
            capacity,
            both_parts,
            *jobs_of(*behind),
        )
        landed(*behind, moved)
        prob_parts.append(probs_here[:, 0])
        grads.update({(i, k): by_wide(v) for k, v in enumerate(made)})
    column.update({name: summed(name) for name in along_y})
    behind = (names[2:4], names[:1])
    (
        sums,
        sent,
        shared_out,
        shared_back,
        shared_gate_grad,
        shared_up_grad,
        shared_down_grad,
    ), moved = sum_around(
        grid_of,
        ZP,
        2,
        both_parts.reshape(2, ZP, nx, NC, tok_rows, width),
        jnp.stack(prob_parts, axis=1).reshape(ZP, nx, NC, mine, tok_rows),
        (normed_two, cotangent, s_both, s_down),
        *jobs_of(*behind),
    )
    landed(*behind, moved)
    column.update({name: summed(name) for name in behind[0]})
    routed_grad = sums[0].astype(f32)
    routed = sums[1].astype(f32)
    dz = (grid.zm + jnp.arange(ZP, dtype=jnp.int32)) % ZP
    owner = block_places.reshape(1, nx, NC, 1) * local_experts
    owner = owner + dz[:, None, None, None] * mine + jnp.arange(mine, dtype=jnp.int32)
    same = owner.reshape(-1)[None, :] == jnp.arange(experts, dtype=jnp.int32)[:, None]
    prob_grad = jnp.sum(
        jnp.where(same[:, :, None], sent.reshape(1, experts, tok_rows), 0.0), axis=1
    ).T

    out_grad = cotangent.astype(f32)
    block_out = (middle + shared_out + routed).astype(bf16)

    logit_grad = router_probs * (
        prob_grad - jnp.sum(router_probs * prob_grad, axis=-1, keepdims=True)
    )
    router_grad = lax.dot_general(
        normed_two.astype(f32),
        logit_grad,
        (((0,), (0,)), ((), ())),
        precision=lax.Precision.HIGHEST,
        preferred_element_type=f32,
    )
    normed_two_grad = (
        shared_back
        + routed_grad
        + lax.dot_general(
            logit_grad,
            w_router.astype(f32),
            (((1,), (1,)), ((), ())),
            precision=lax.Precision.HIGHEST,
            preferred_element_type=f32,
        )
    )
    gain_two_grad, middle_part = norm_backward(
        middle, inverse_two, gain_two, normed_two_grad
    )
    middle_grad = out_grad + middle_part
    branch_grad = middle_grad.astype(bf16)
    output_weight_grad = contract_rows(attended, branch_grad)
    attended_grad = times_transposed(branch_grad, w_out).astype(bf16)

    behind = (names[4:5], names[1:2])
    query_act_grad, parts, moved = attention_backward(
        grid_of,
        1 + 8,
        queries,
        keys_all,
        values_all,
        attended_grad,
        bias.T,
        *jobs_of(*behind),
    )
    landed(*behind, moved)
    behind = (names[5:], names[2:4])
    ((value_key,), moved) = sum_around(
        grid_of,
        1,
        3,
        parts.reshape(2, 1, nx, NC, tok_rows, width),
        None,
        (),
        *jobs_of(*behind),
    )
    value_act_grad, key_act_grad = value_key
    landed(*behind, moved)
    column.update({name: summed(name) for name in names[4:]})
    query_w_grad = contract_rows(normed_one, query_act_grad)
    key_w_grad = contract_rows(normed_one, key_act_grad)
    value_w_grad = contract_rows(normed_one, value_act_grad)
    normed_one_grad = (
        times_transposed(query_act_grad, w_query)
        + times_transposed(key_act_grad, w_key)
        + times_transposed(value_act_grad, w_value)
    )
    gain_one_grad, input_part = norm_backward(
        inputs, inverse_one, gain_one, normed_one_grad
    )
    input_grad = middle_grad + input_part

    def by_place(v):
        return v.reshape((NZ, ny, nx, NC, v.shape[0] // (wide * ep)) + v.shape[1:])

    counts = jnp.sum(
        (routes[:, :, None] == jnp.arange(experts, dtype=jnp.int32)).astype(f32),
        axis=(0, 1),
    )
    share = gain_attention.shape[0]
    count_block = jnp.pad(
        jnp.tile(counts.reshape(1, ep, 1, local_experts), (wide, 1, 1, 1)),
        ((0, 0), (0, 0), (0, 0), (0, 128 - local_experts)),
    )
    extras = jnp.concatenate(
        [
            router_grad,
            gain_one_grad[:, None],
            gain_two_grad[:, None],
            jnp.zeros((width, 128 - experts - 2), f32),
        ],
        axis=1,
    ).reshape(wide, ep, share, 128)
    extras = jnp.concatenate(
        [extras, count_block, jnp.zeros((wide, ep, 7, 128), f32)], axis=2
    )
    dense = [
        output_weight_grad,
        shared_down_grad,
        shared_gate_grad,
        shared_up_grad,
        query_w_grad,
        key_w_grad,
        value_w_grad,
    ]
    terms, moved = reduce_dense(
        grid_of,
        4,
        [by_place(v.astype(bf16)) for v in dense]
        + [extras.reshape(NZ, ny, nx, NC, share + 8, 128)],
        *jobs_of([], names[4:]),
    )
    landed([], names[4:], moved)
    (
        expert_gate_grad,
        expert_up_grad,
        expert_down_grad,
        output_weight_sum,
        shared_down_sum,
        shared_gate_sum,
        shared_up_sum,
        query_sum,
        key_sum,
        value_sum,
        extra_sum,
    ) = finish(
        grid_of, mine, [column[n] for n in names], [along_z[n] for n in names], terms
    )
    expert_gate_grad, expert_up_grad, expert_down_grad = (
        v.reshape((local_experts,) + v.shape[2:])
        for v in (expert_gate_grad, expert_up_grad, expert_down_grad)
    )
    return (
        block_out,
        input_grad,
        extra_sum[:share, experts],
        query_sum,
        key_sum,
        value_sum,
        output_weight_sum,
        extra_sum[:share, experts + 1],
        extra_sum[:share, :experts],
        shared_gate_sum,
        shared_up_sum,
        shared_down_sum,
        expert_gate_grad,
        expert_up_grad,
        expert_down_grad,
        extra_sum[share, :local_experts].astype(jnp.int32),
    )


def solution(mesh):
    split = P(BOTH, None)
    line = P(BOTH)
    held = P("ep", None, None)
    out_held = P("ep", "wide", None)
    in_specs = (
        (split, line, split, line)
        + (split,) * 4
        + (line,)
        + (split,) * 4
        + (held,) * 3
        + (split,)
    )
    out_specs = (
        (split, split, line)
        + (split,) * 4
        + (line,)
        + (split,) * 4
        + (out_held,) * 3
        + (P("ep"),)
    )
    return jax.shard_map(
        functools.partial(body, mesh.shape["wide"], mesh.shape["ep"]),
        mesh=mesh,
        in_specs=in_specs,
        out_specs=out_specs,
        check_vma=False,
    )
```

```python
import functools

import jax
import jax.numpy as jnp
from jax import lax
from jax.experimental import pallas as pl
from jax.experimental.pallas import tpu as pltpu
from jax.sharding import PartitionSpec as P

HD = 128
NC = 2
NZ = 4
ZP = 2
epsilon = 1e-06
masked_value = -1e30
BOTH = ("wide", "ep")
f32 = jnp.float32
bf16 = jnp.bfloat16


def contract_rows(left, right):
    return lax.dot_general(
        left, right, (((0,), (0,)), ((), ())), preferred_element_type=f32
    )


def times_transposed(left, right):
    return lax.dot_general(
        left, right, (((1,), (1,)), ((), ())), preferred_element_type=f32
    )


def times(left, right):
    return jnp.dot(left, right, preferred_element_type=f32)


def norm_scale(values):
    return lax.rsqrt(jnp.mean(values * values, axis=-1, keepdims=True) + epsilon)


def norm_backward(values, inverse, gain, normed_grad):
    weighted = normed_grad * gain
    gain_grad = jnp.sum(normed_grad * values * inverse, axis=0)
    cubed = inverse * inverse * inverse
    values_grad = inverse * weighted - values * cubed * jnp.mean(
        weighted * values, axis=-1, keepdims=True
    )
    return (gain_grad, values_grad)


def silu_parts(gate_act):
    logistic = 0.5 * jnp.tanh(0.5 * gate_act) + 0.5
    return (gate_act * logistic, logistic * (1.0 + gate_act * (1.0 - logistic)))


class Grid:
    def __init__(self, wide, ep):
        self.ny, self.nx, self.ep = wide // NZ, ep // NC, ep
        w, e = lax.axis_index("wide"), lax.axis_index("ep")
        self.z, self.y, self.x, self.c = w // self.ny, w % self.ny, e // NC, e % NC
        self.zm = self.z % ZP

    def pairs(self, move):
        made = []
        for z in range(NZ):
            for y in range(self.ny):
                for x in range(self.nx):
                    for c in range(NC):
                        tz, ty, tx, tc = move(z, y, x, c)
                        made.append(
                            (
                                (z * self.ny + y) * self.ep + x * NC + c,
                                (tz * self.ny + ty) * self.ep + tx * NC + tc,
                            )
                        )
        return made

    def send(self, value, axis, step):
        moves = {
            "c": lambda z, y, x, c: (z, y, x, (c + step) % NC),
            "x": lambda z, y, x, c: (z, y, (x + step) % self.nx, c),
            "y": lambda z, y, x, c: (z, (y + step) % self.ny, x, c),
            "z": lambda z, y, x, c: ((z + step) % NZ, y, x, c),
            "p": lambda z, y, x, c: (z // ZP * ZP + (z % ZP + step) % ZP, y, x, c),
        }
        return lax.ppermute(value, BOTH, self.pairs(moves[axis]))

    def size(self, axis):
        return {"c": NC, "x": self.nx, "y": self.ny, "z": NZ, "p": ZP}[axis]

    def place(self, axis):
        return {"c": self.c, "x": self.x, "y": self.y, "z": self.z, "p": self.zm}[axis]

    def gather(self, value, axis, at):
        parts = [value] + [
            self.send(value, axis, -d) for d in range(1, self.size(axis))
        ]
        return jnp.stack(parts, axis=at)

    def scatter(self, value, axis, at):
        total = lax.index_in_dim(value, 0, at, keepdims=False).astype(f32)
        for d in range(1, self.size(axis)):
            part = lax.index_in_dim(value, d, at, keepdims=False)
            total = total + self.send(part, axis, d).astype(f32)
        return total.astype(value.dtype)

    def scatter_absolute(self, value, axis, at):
        n, me = self.size(axis), self.place(axis)
        take = lambda i: lax.dynamic_index_in_dim(value, i, at, keepdims=False)
        total = take(me).astype(f32)
        for d in range(1, n):
            total = total + self.send(take((me + d) % n), axis, d).astype(f32)
        return total.astype(value.dtype)


class Sender:
    def __init__(self, sems):
        self.sems, self.started = sems, []

    def __call__(self, src, dst, sem, target):
        copy = pltpu.make_async_remote_copy(
            src_ref=src,
            dst_ref=dst,
            send_sem=self.sems.at[len(self.started)],
            recv_sem=sem,
            device_id=target,
            device_id_type=pl.DeviceIdType.MESH,
        )
        copy.start()
        self.started.append(copy)

    def finish(self):
        for copy in self.started:
            copy.wait_send()


def arrived(dst, sem):
    pltpu.make_async_copy(dst, dst, sem).wait()


def greet(targets):
    barrier = pltpu.get_barrier_semaphore()
    for target in targets:
        pl.semaphore_signal(
            barrier, inc=1, device_id=target, device_id_type=pl.DeviceIdType.MESH
        )
    pl.semaphore_wait(barrier, len(targets))


def around(grid, zp):
    steps = [(a, b, e) for a in range(zp) for b in range(grid.nx) for e in range(NC)]
    return steps[1:]


def stepped(grid, zp, a, b, e):
    z = grid.z // zp * zp + (grid.z % zp + a) % zp
    return (
        z * grid.ny + grid.y,
        (grid.x + b) % grid.nx * NC + (grid.c + e) % NC,
    )


def gather_kernel(
    grid_of,
    w_ref,
    rows_ref,
    cot_ref,
    ints_ref,
    w_all,
    rows_all,
    cot_all,
    ints_all,
    plane_sem,
    core_sem,
    rows_sem,
    cot_sem,
    ints_sem,
    send_sem,
    local_sem,
    z_in,
    z_out,
    x_out,
    y_out,
    c_out,
):
    grid = grid_of()
    z, y, x, c, nx, ny = grid.z, grid.y, grid.x, grid.c, grid.nx, grid.ny

    def device(tz, ty, tx, tc):
        return (tz * ny + ty, tx * NC + tc)

    def block(dz, dy, dx, tc):
        place = (z + NZ - dz) % NZ * ny + (y + ny - dy) % ny
        return w_all.at[place * (nx * NC) + (x + nx - dx) % nx * NC + tc]

    shift_z = lambda d: (z + d) % NZ
    shift_y = lambda d: (y + d) % ny
    shift_x = lambda d: (x + d) % nx
    back = lambda d: (nx - d) % nx
    other = (c + 1) % NC
    to = functools.partial(stepped, grid, ZP)
    greet(
        [device(shift_z(d), y, x, c) for d in range(1, NZ)]
        + [device(z, shift_y(d), x, c) for d in range(1, ny)]
        + [to(*s) for s in around(grid, ZP)]
    )
    send = Sender(send_sem)
    locals_ = [
        (w_ref, block(0, 0, 0, c)),
        (rows_ref, rows_all.at[0, 0]),
        (cot_ref, cot_all.at[0, 0, 0]),
        (ints_ref, ints_all.at[0, 0, 0]),
    ]
    locals_ = [
        pltpu.make_async_copy(src, dst, local_sem.at[k])
        for k, (src, dst) in enumerate(locals_)
    ]
    for copy in locals_:
        copy.start()
    def start(src, dst, out_sem, in_sem, target):
        pltpu.make_async_remote_copy(
            src_ref=src,
            dst_ref=dst,
            send_sem=out_sem,
            recv_sem=in_sem,
            device_id=target,
            device_id_type=pl.DeviceIdType.MESH,
        ).start()

    def each_source(act, least=0, most=NZ - 1):
        for d in range(least, most + 1):
            for way in range(2):
                there = z - d >= 0 if way == 0 else z + d <= NZ - 1
                pl.when(there)(
                    functools.partial(act, way, d, d if way == 0 else (NZ - d) % NZ)
                )

    def pass_on(way, d, dz):
        here = block(dz, 0, 0, c)
        src = here if d else w_ref
        if d:
            arrived(here, z_in.at[way, d])
        if d < NZ - 1:

            @pl.when(z < NZ - 1 if way == 0 else z > 0)
            def _():
                start(
                    src,
                    here,
                    z_out.at[way, d],
                    z_in.at[way, d + 1],
                    device(z + 1 if way == 0 else z - 1, y, x, c),
                )

        if d or way == 0:
            for b in range(1, nx):
                start(src, here, x_out.at[dz, b], plane_sem.at[dz, 0, b], device(z, y, shift_x(b), c))
            for b in range(1, ny):
                start(src, here, y_out.at[dz, 0, b], plane_sem.at[dz, b, 0], device(z, shift_y(b), x, c))
            start(src, here, c_out.at[dz, 0], core_sem.at[dz, 0, 0], device(z, y, x, other))

    def turn(way, d, dz):
        if d == 0 and way == 1:
            return
        for dx in range(1, nx):
            here = block(dz, 0, dx, c)
            arrived(here, plane_sem.at[dz, 0, dx])
            for b in range(1, ny):
                start(here, here, y_out.at[dz, dx, b], plane_sem.at[dz, b, dx], device(z, shift_y(b), x, c))
            start(here, here, c_out.at[dz, dx], core_sem.at[dz, 0, dx], device(z, y, x, other))

    for a, b, e in around(grid, ZP):
        mirror = ((ZP - a) % ZP, back(b), e)
        send(ints_ref, ints_all.at[mirror], ints_sem.at[mirror], to(a, b, e))
    each_source(pass_on, 0, 0)
    for d in range(1, NZ):
        each_source(pass_on, d, d)
        if d == NZ - 1:
            for a in range(1, ZP):
                send(cot_ref, cot_all.at[ZP - a, 0, 0], cot_sem.at[ZP - a, 0, 0, 0], to(a, 0, 0))
            for b in range(1, nx):
                send(cot_ref, cot_all.at[0, back(b), 0], cot_sem.at[0, back(b), 0, 0], to(0, b, 0))
                send(rows_ref, rows_all.at[back(b), 0], rows_sem.at[back(b), 0], to(0, b, 0))
        each_source(turn, d - 1, d - 1)
    each_source(turn, NZ - 1, NZ - 1)
    send(cot_ref, cot_all.at[0, 0, 1], cot_sem.at[0, 0, 1, 0], to(0, 0, 1))
    send(rows_ref, rows_all.at[0, 1], rows_sem.at[0, 1], to(0, 0, 1))
    for d in range(1, nx):
        here = rows_all.at[d, 0]
        arrived(here, rows_sem.at[d, 0])
        send(here, rows_all.at[d, 1], rows_sem.at[d, 1], to(0, 0, 1))
    width = cot_ref.shape[1]
    halves = [
        (slice(None), pl.ds(0, width // 2)),
        (slice(None), pl.ds(width // 2, width // 2)),
    ]
    for a in range(1, ZP):
        here = cot_all.at[a, 0, 0]
        arrived(here, cot_sem.at[a, 0, 0, 0])
        for b in range(1, nx):
            send(here.at[halves[0]], cot_all.at[a, back(b), 0].at[halves[0]], cot_sem.at[a, back(b), 0, 0], to(0, b, 0))
        send(here, cot_all.at[a, 0, 1], cot_sem.at[a, 0, 1, 0], to(0, 0, 1))
    for b in range(1, nx):
        here = cot_all.at[0, b, 0]
        arrived(here, cot_sem.at[0, b, 0, 0])
        for a in range(1, ZP):
            send(here.at[halves[1]], cot_all.at[ZP - a, b, 0].at[halves[1]], cot_sem.at[ZP - a, b, 0, 1], to(a, 0, 0))
        send(here, cot_all.at[0, b, 1], cot_sem.at[0, b, 1, 0], to(0, 0, 1))
    for dz in range(NZ):
        for dy in range(1, ny):
            for dx in range(nx):
                here = block(dz, dy, dx, c)
                arrived(here, plane_sem.at[dz, dy, dx])
                send(here, here, core_sem.at[dz, dy, dx], device(z, y, x, other))
    for a in range(1, ZP):
        for b in range(1, nx):
            here = cot_all.at[a, b, 0]
            for part in range(2):
                arrived(here.at[halves[part]], cot_sem.at[a, b, 0, part])
            send(here, cot_all.at[a, b, 1], cot_sem.at[a, b, 1, 0], to(0, 0, 1))
    for dx in range(nx):
        arrived(rows_all.at[dx, 1], rows_sem.at[dx, 1])
        for a in range(ZP):
            arrived(cot_all.at[a, dx, 1], cot_sem.at[a, dx, 1, 0])
    for a, b, e in around(grid, ZP):
        arrived(ints_all.at[a, b, e], ints_sem.at[a, b, e])
    for dz in range(NZ):
        for dy in range(ny):
            for dx in range(nx):
                arrived(block(dz, dy, dx, other), core_sem.at[dz, dy, dx])
    for copy in locals_:
        copy.wait()
    send.finish()

    def sent(way, d, dz):
        if d < NZ - 1:

            @pl.when(z < NZ - 1 if way == 0 else z > 0)
            def _():
                arrived(w_ref, z_out.at[way, d])

    each_source(sent)
    for dz in range(NZ):
        for b in range(1, nx):
            arrived(w_ref, x_out.at[dz, b])
        for dx in range(nx):
            for b in range(1, ny):
                arrived(w_ref, y_out.at[dz, dx, b])
            arrived(w_ref, c_out.at[dz, dx])


def gather_first(grid_of, w, rows, cot, ints):
    grid = grid_of()
    nx, ny = grid.nx, grid.ny
    places = NZ * ny * nx * NC
    octet = ZP * nx * NC
    sends = (NZ - 1) + NZ * (nx + ny) + 2 * nx + octet * 4 + NZ * nx * ny * (ny + 1)
    anywhere = pl.BlockSpec(memory_space=pl.ANY)
    dma = pltpu.SemaphoreType.DMA
    return pl.pallas_call(
        functools.partial(gather_kernel, grid_of),
        out_shape=(
            jax.ShapeDtypeStruct((places,) + w.shape, w.dtype),
            jax.ShapeDtypeStruct((nx, NC) + rows.shape, rows.dtype),
            jax.ShapeDtypeStruct((ZP, nx, NC) + cot.shape, cot.dtype),
            jax.ShapeDtypeStruct((ZP, nx, NC) + ints.shape, ints.dtype),
        ),
        in_specs=[anywhere] * 4,
        out_specs=(anywhere,) * 4,
        scratch_shapes=[
            dma((NZ, ny, nx)),
            dma((NZ, ny, nx)),
            dma((nx, NC)),
            dma((ZP, nx, NC, 2)),
            dma((ZP, nx, NC)),
            dma((sends,)),
            dma((4,)),
            dma((2, NZ)),
            dma((2, NZ)),
            dma((NZ, nx)),
            dma((NZ, nx, ny)),
            dma((NZ, nx)),
        ],
        compiler_params=pltpu.CompilerParams(collective_id=0, has_side_effects=True),
    )(w, rows, cot, ints)


def shared_compute(n2, cot, w_in, w_down, out, back, dg, du, dd, h, ag, au):
    hidden, width = w_down.shape
    strip = 256
    for low in range(0, hidden, strip):
        cut = slice(low, min(low + strip, hidden))
        up_cut = slice(hidden + cut.start, hidden + cut.stop)
        gate_act = times(n2[...], w_in[:, cut])
        up_act = times(n2[...], w_in[:, up_cut])
        hidden_grad = times_transposed(cot[...], w_down[cut])
        activated, slope = silu_parts(gate_act)
        h[:, cut] = (activated * up_act).astype(bf16)
        ag[:, cut] = (hidden_grad * up_act * slope).astype(bf16)
        au[:, cut] = (hidden_grad * activated).astype(bf16)
    turned = h[...].T
    for low in range(0, width, strip):
        cut = slice(low, low + strip)
        out[:, cut] = times(h[...], w_down[:, cut])
        back[:, cut] = times_transposed(ag[...], w_in[cut, :hidden]) + times_transposed(
            au[...], w_in[cut, hidden:]
        )
        rows = n2[:, cut].T
        dg[cut] = times(rows, ag[...]).astype(bf16)
        du[cut] = times(rows, au[...]).astype(bf16)
        dd[:, cut] = times(turned, cot[:, cut]).astype(bf16)


def exchange_kernel(grid_of, zp, cut, src, out, plane_sem, core_sem, local_sem, send_sem):
    grid = grid_of()
    nx = grid.nx
    send = Sender(send_sem)
    to = functools.partial(stepped, grid, zp)
    greet([to(*s) for s in around(grid, zp)])
    back = lambda d: (nx - d) % nx
    for a in range(1, zp):
        send(src, out.at[zp - a, 0, 0], plane_sem.at[zp - a, 0, 0], to(a, 0, 0))
    for b in range(1, nx):
        send(src, out.at[0, back(b), 0], plane_sem.at[0, back(b), 0], to(0, b, 0))
    send(src, out.at[0, 0, 1], core_sem.at[0, 0], to(0, 0, 1))
    keep = pltpu.make_async_copy(src, out.at[0, 0, 0], local_sem)
    keep.start()
    h0 = (slice(None), pl.ds(0, cut))
    h1 = (slice(None), pl.ds(cut, src.shape[1] - cut))
    for a in range(1, zp):
        here = out.at[a, 0, 0]
        arrived(here, plane_sem.at[a, 0, 0])
        for b in range(1, nx):
            send(here.at[h0], out.at[a, back(b), 0].at[h0], plane_sem.at[a, back(b), 0], to(0, b, 0))
        send(here, out.at[a, 0, 1], core_sem.at[a, 0], to(0, 0, 1))
    for b in range(1, nx):
        here = out.at[0, b, 0]
        arrived(here, plane_sem.at[0, b, 0])
        for a in range(1, zp):
            send(here.at[h1], out.at[zp - a, b, 0].at[h1], plane_sem.at[zp - a, b, 1], to(a, 0, 0))
        send(here, out.at[0, b, 1], core_sem.at[0, b], to(0, 0, 1))
    for a in range(1, zp):
        for b in range(1, nx):
            here = out.at[a, b, 0]
            arrived(here.at[h0], plane_sem.at[a, b, 0])
            arrived(here.at[h1], plane_sem.at[a, b, 1])
            send(here, out.at[a, b, 1], core_sem.at[a, b], to(0, 0, 1))
    for a in range(zp):
        for b in range(nx):
            arrived(out.at[a, b, 1], core_sem.at[a, b])
    keep.wait()
    send.finish()


def exchange(grid_of, zp, number, rows):
    grid = grid_of()
    nx = grid.nx
    sends = zp * nx * 2 + zp * nx * nx * 2
    anywhere = pl.BlockSpec(memory_space=pl.ANY)
    dma = pltpu.SemaphoreType.DMA
    return pl.pallas_call(
        functools.partial(exchange_kernel, grid_of, zp, rows.shape[1] // 256 * 128),
        out_shape=jax.ShapeDtypeStruct((zp, nx, NC) + rows.shape, rows.dtype),
        in_specs=[anywhere],
        out_specs=anywhere,
        scratch_shapes=[dma((zp, nx, 2)), dma((zp, nx)), dma, dma((sends,))],
        compiler_params=pltpu.CompilerParams(
            collective_id=number, has_side_effects=True
        ),
    )(rows)


def add_into(dst, src, rows):
    for k in range(dst.shape[0]):

        @pl.loop(0, dst.shape[1], step=rows)
        def _(i):
            at = pl.ds(pl.multiple_of(i, rows), rows)
            dst[k, at] = (dst[k, at].astype(f32) + src[k, at].astype(f32)).astype(
                dst.dtype
            )


def sum_kernel(grid_of, zp, cut, small, jobs, parts, *refs):
    grid = grid_of()
    nx = grid.nx
    if small:
        pieces, refs = refs[0], refs[1:]
        shared_ins, refs = refs[:4], refs[4:]
    job_ins, refs = refs[: len(jobs)], refs[len(jobs) :]
    out, refs = refs[0], refs[1:]
    if small:
        pieces_out, refs = refs[0], refs[1:]
        shared_outs, refs = refs[:5], refs[5:]
    job_outs, refs = refs[: len(jobs)], refs[len(jobs) :]
    refs, (job_send, job_recv) = refs[:-2], refs[-2:]
    if small:
        shared_held, load_sem, refs = refs[-8:-1], refs[-1], refs[:-8]
        loads = [
            pltpu.make_async_copy(a, b, load_sem.at[k])
            for k, (a, b) in enumerate(zip(shared_ins, shared_held))
        ]
    each = functools.partial(each_job, grid, jobs, job_ins, job_outs, job_send, job_recv)
    own, got_c, turn_x, turn_p, got_p, got_x = refs[:6]
    local_sem, c_sem, turn_sem, p_sem, x_sem, small_sem, send_sem = refs[6:]
    send = Sender(send_sem)
    to = functools.partial(stepped, grid, zp)
    greet([to(*s) for s in around(grid, zp)] + job_targets(grid, jobs))
    width = parts.shape[-1]
    h0, h1 = pl.ds(0, cut), pl.ds(cut, width - cut)
    order = (
        [(a, b) for a in range(1, zp) for b in range(1, nx)]
        + [(a, 0) for a in range(1, zp)]
        + [(0, b) for b in range(1, nx)]
        + [(0, 0)]
    )
    for a, b in order:
        send(parts.at[:, a, b, 1], got_c.at[:, a, b], c_sem.at[a, b], to(0, 0, 1))
        pltpu.make_async_copy(
            parts.at[:, a, b, 0], own.at[:, a, b], local_sem.at[a, b]
        ).start()
    if small:
        for a, b, e in around(grid, zp):
            mirror = ((zp - a) % zp, (nx - b) % nx, e)
            send(
                pieces.at[a, b, e],
                pieces_out.at[mirror],
                small_sem.at[mirror],
                to(a, b, e),
            )
        pltpu.make_async_copy(
            pieces.at[0, 0, 0], pieces_out.at[0, 0, 0], small_sem.at[0, 0, 0]
        ).start()
    each(lambda copy: copy.start())
    if small:
        for load in loads:
            load.start()
    rows = 32

    def ready(a, b):
        arrived(got_c.at[:, a, b], c_sem.at[a, b])
        pltpu.make_async_copy(
            parts.at[:, a, b, 0], own.at[:, a, b], local_sem.at[a, b]
        ).wait()
        add_into(own.at[:, a, b], got_c.at[:, a, b], rows)

    for a in range(1, zp):
        for b in range(1, nx):
            ready(a, b)
            send(own.at[:, a, b, :, h0], turn_x.at[:, a - 1, b - 1], turn_sem.at[a - 1, b - 1, 0], to(0, b, 0))
            send(own.at[:, a, b, :, h1], turn_p.at[:, a - 1, b - 1], turn_sem.at[a - 1, b - 1, 1], to(a, 0, 0))
    for a in range(1, zp):
        ready(a, 0)
    for b in range(1, nx):
        ready(0, b)
    for a in range(1, zp):
        for b in range(1, nx):
            arrived(turn_x.at[:, a - 1, b - 1], turn_sem.at[a - 1, b - 1, 0])
            add_into(own.at[:, a, 0, :, h0], turn_x.at[:, a - 1, b - 1], rows)
        send(own.at[:, a, 0], got_p.at[:, a - 1], p_sem.at[a - 1], to(a, 0, 0))
    for b in range(1, nx):
        for a in range(1, zp):
            arrived(turn_p.at[:, a - 1, b - 1], turn_sem.at[a - 1, b - 1, 1])
            add_into(own.at[:, 0, b, :, h1], turn_p.at[:, a - 1, b - 1], rows)
        send(own.at[:, 0, b], got_x.at[:, b - 1], x_sem.at[b - 1], to(0, b, 0))
    ready(0, 0)
    if small:
        for load in loads:
            load.wait()
        shared_compute(*shared_held[:4], *shared_outs, *shared_held[4:])
    for a in range(1, zp):
        arrived(got_p.at[:, a - 1], p_sem.at[a - 1])
        add_into(own.at[:, 0, 0], got_p.at[:, a - 1], rows)
    for b in range(1, nx):
        arrived(got_x.at[:, b - 1], x_sem.at[b - 1])
        add_into(own.at[:, 0, 0], got_x.at[:, b - 1], rows)
    result = pltpu.make_async_copy(own.at[:, 0, 0], out, local_sem.at[0, 0])
    result.start()
    if small:
        for a, b, e in [(0, 0, 0)] + around(grid, zp):
            arrived(pieces_out.at[a, b, e], small_sem.at[a, b, e])
    result.wait()
    each(lambda copy: copy.wait())
    send.finish()


def sum_around(grid_of, zp, number, parts, pieces=None, shared=(), jobs=(), job_arrays=()):
    grid = grid_of()
    nx = grid.nx
    payloads, rows, width = parts.shape[0], parts.shape[-2], parts.shape[-1]
    cut = width // 640 * 512
    anywhere = pl.BlockSpec(memory_space=pl.ANY)
    dma = pltpu.SemaphoreType.DMA
    small = pieces is not None
    out_shape = [jax.ShapeDtypeStruct((payloads, rows, width), parts.dtype)]
    args = [parts]
    if small:
        out_shape.append(jax.ShapeDtypeStruct(pieces.shape, pieces.dtype))
        args += [pieces, *shared]
        tokens, hidden = shared[0].shape[0], shared[3].shape[0]
        out_shape += [jax.ShapeDtypeStruct((tokens, width), f32)] * 2
        out_shape += [jax.ShapeDtypeStruct((width, hidden), bf16)] * 2
        out_shape.append(jax.ShapeDtypeStruct((hidden, width), bf16))
    plain = len(out_shape)
    out_shape += job_shapes(grid, jobs, job_arrays)
    args += list(job_arrays)
    turns = (max(zp - 1, 1), max(nx - 1, 1))
    vmem = lambda shape: pltpu.VMEM(shape, parts.dtype)
    made = pl.pallas_call(
        functools.partial(sum_kernel, grid_of, zp, cut, small, jobs),
        out_shape=tuple(out_shape),
        in_specs=[anywhere] * len(args),
        out_specs=tuple(
            pl.BlockSpec(memory_space=pltpu.VMEM) if 2 <= n < plain else anywhere
            for n in range(len(out_shape))
        ),
        scratch_shapes=[
            vmem((payloads, zp, nx, rows, width)),
            vmem((payloads, zp, nx, rows, width)),
            vmem((payloads,) + turns + (rows, cut)),
            vmem((payloads,) + turns + (rows, width - cut)),
            vmem((payloads, turns[0], rows, width)),
            vmem((payloads, turns[1], rows, width)),
            dma((zp, nx)),
            dma((zp, nx)),
            dma(turns + (2,)),
            dma((turns[0],)),
            dma((turns[1],)),
            dma((zp, nx, NC)),
            dma((zp * nx * 6 + 8,)),
        ]
        + (
            [pltpu.VMEM(v.shape, bf16) for v in shared]
            + [pltpu.VMEM((tokens, hidden), bf16)] * 3
            + [dma((4,))]
            if small
            else []
        )
        + job_sems(grid, jobs),
        compiler_params=pltpu.CompilerParams(
            collective_id=number,
            has_side_effects=True,
            vmem_limit_bytes=56 * 2**20,
        ),
    )(*args)
    return made[:plain], made[plain:]


def project_kernel(rows_ref, wq_ref, wk_ref, wv_ref, q_ref, k_ref, v_ref):
    rows = rows_ref[...]
    q_ref[...] = times(rows[: q_ref.shape[0]], wq_ref[...]).astype(bf16)
    k_ref[...] = times(rows, wk_ref[...]).astype(bf16)
    v_ref[...] = times(rows, wv_ref[...]).astype(bf16)


def project(rows, weights, tokens):
    length, width = rows.shape
    strip = 256
    strips = width // strip
    block = pl.BlockSpec
    weight = lambda k: block((width, strip), lambda s: (0, k * strips + s))
    return pl.pallas_call(
        project_kernel,
        grid=(strips,),
        in_specs=[block((length, width), lambda s: (0, 0)), weight(0), weight(1), weight(2)],
        out_specs=[
            block((tokens, strip), lambda s: (0, s)),
            block((length, strip), lambda s: (0, s)),
            block((length, strip), lambda s: (0, s)),
        ],
        out_shape=[
            jax.ShapeDtypeStruct((n, width), bf16) for n in (tokens, length, length)
        ],
        compiler_params=pltpu.CompilerParams(vmem_limit_bytes=48 * 2**20),
        cost_estimate=pl.CostEstimate(
            flops=2 * (tokens + 2 * length) * width * width,
            bytes_accessed=6 * width * width + 6 * length * width,
            transcendentals=0,
        ),
    )(rows, weights, weights, weights)


def project_back_kernel(rows_ref, gq_ref, gvk_ref, w_ref, dq_ref, dk_ref, dv_ref, back_ref):
    turned = rows_ref[...].T
    width = gq_ref.shape[1]
    total = None
    for k, (grad, out) in enumerate(
        ((gq_ref[...], dq_ref), (gvk_ref[1], dk_ref), (gvk_ref[0], dv_ref))
    ):
        out[...] = times(turned, grad).astype(bf16)
        part = times_transposed(grad, w_ref[:, k * width : (k + 1) * width])
        total = part if total is None else total + part
    back_ref[...] = total


def project_back(rows, gq, gvk, weights):
    tokens, width = rows.shape
    strip = 256
    block = pl.BlockSpec
    return pl.pallas_call(
        project_back_kernel,
        grid=(width // strip,),
        in_specs=[
            block((tokens, strip), lambda s: (0, s)),
            block((tokens, width), lambda s: (0, 0)),
            block((2, tokens, width), lambda s: (0, 0, 0)),
            block((strip, 3 * width), lambda s: (s, 0)),
        ],
        out_specs=[block((strip, width), lambda s: (s, 0))] * 3
        + [block((tokens, strip), lambda s: (0, s))],
        out_shape=[jax.ShapeDtypeStruct((width, width), bf16)] * 3
        + [jax.ShapeDtypeStruct((tokens, width), f32)],
        compiler_params=pltpu.CompilerParams(vmem_limit_bytes=48 * 2**20),
        cost_estimate=pl.CostEstimate(
            flops=12 * tokens * width * width,
            bytes_accessed=12 * width * width + 12 * tokens * width,
            transcendentals=0,
        ),
    )(rows, gq, gvk, weights)


def attention_kernel(q_ref, k_ref, v_ref, bias_ref, out_ref):
    scores = times_transposed(q_ref[...], k_ref[...]) * HD ** (-0.5) + bias_ref[...]
    weights = jnp.exp(scores - jnp.max(scores, axis=1, keepdims=True))
    probs = weights * (1.0 / jnp.sum(weights, axis=1, keepdims=True))
    out_ref[...] = times(probs.astype(bf16), v_ref[...]).astype(bf16)


def attention_forward(queries, keys, values, bias):
    rows, width = queries.shape
    length = keys.shape[0]
    by_head = lambda n: pl.BlockSpec((n, HD), lambda h: (0, h))
    return pl.pallas_call(
        attention_kernel,
        grid=(width // HD,),
        out_shape=jax.ShapeDtypeStruct((rows, width), bf16),
        in_specs=[
            by_head(rows),
            by_head(length),
            by_head(length),
            pl.BlockSpec((rows, length), lambda h: (0, 0)),
        ],
        out_specs=by_head(rows),
        compiler_params=pltpu.CompilerParams(vmem_limit_bytes=40 * 2**20),
        cost_estimate=pl.CostEstimate(
            flops=4 * rows * length * width,
            bytes_accessed=4 * (rows + length) * width + 4 * rows * length,
            transcendentals=rows * length * width // HD,
        ),
    )(queries, keys, values, bias)


def attention_back_kernel(grid_of, jobs, q_ref, k_ref, v_ref, g_ref, bias_ref, *refs):
    grid = grid_of()
    count = len(jobs)
    dq_ref, parts_ref = refs[count : count + 2]
    job_send, job_recv = refs[-2:]
    each = functools.partial(
        each_job, grid, jobs, refs[:count], refs[count + 2 : -2], job_send, job_recv
    )
    if jobs:

        @pl.when(pl.program_id(0) == 0)
        def _():
            greet(job_targets(grid, jobs))
            each(lambda copy: copy.start())

    q, k, g = q_ref[...], k_ref[...], g_ref[...]
    scores = times_transposed(k, q) * HD ** (-0.5) + bias_ref[...]
    weights = jnp.exp(scores - jnp.max(scores, axis=0, keepdims=True))
    probs = weights * (1.0 / jnp.sum(weights, axis=0, keepdims=True))
    prob_grad = times_transposed(v_ref[...], g)
    centre = jnp.sum(probs * prob_grad, axis=0, keepdims=True)
    score_grad = (probs * (prob_grad - centre)).astype(bf16)
    parts_ref[0] = times(probs.astype(bf16), g).astype(bf16)
    parts_ref[1] = (times(score_grad, q) * HD ** (-0.5)).astype(bf16)
    dq_ref[...] = (contract_rows(score_grad, k) * HD ** (-0.5)).astype(bf16)
    if jobs:

        @pl.when(pl.program_id(0) == pl.num_programs(0) - 1)
        def _():
            each(lambda copy: copy.wait())


def attention_backward(grid_of, number, queries, keys, values, grads, bias, jobs, job_arrays):
    grid = grid_of()
    rows, width = queries.shape
    length = keys.shape[0]
    by_head = lambda n: pl.BlockSpec((n, HD), lambda h: (0, h))
    anywhere = pl.BlockSpec(memory_space=pl.ANY)
    made = pl.pallas_call(
        functools.partial(attention_back_kernel, grid_of, jobs),
        grid=(width // HD,),
        out_shape=tuple(
            [
                jax.ShapeDtypeStruct((rows, width), bf16),
                jax.ShapeDtypeStruct((2, length, width), bf16),
            ]
            + job_shapes(grid, jobs, job_arrays)
        ),
        in_specs=[
            by_head(rows),
            by_head(length),
            by_head(length),
            by_head(rows),
            pl.BlockSpec((length, rows), lambda h: (0, 0)),
        ]
        + [anywhere] * len(jobs),
        out_specs=(by_head(rows), pl.BlockSpec((2, length, HD), lambda h: (0, 0, h)))
        + (anywhere,) * len(jobs),
        scratch_shapes=job_sems(grid, jobs),
        compiler_params=pltpu.CompilerParams(
            vmem_limit_bytes=40 * 2**20,
            **(dict(collective_id=number, has_side_effects=True) if jobs else {}),
        ),
        cost_estimate=pl.CostEstimate(
            flops=10 * rows * length * width,
            bytes_accessed=6 * rows * width + 8 * length * width + 4 * rows * length,
            transcendentals=rows * length * width // HD,
        ),
    )(queries, keys, values, grads, bias, *job_arrays)
    return made[0], made[1], made[2:]


ROW_SOURCES = 2


def expert_kernel(grid_of, capacity, steps, jobs, carry, *refs):
    grid = grid_of()
    count = len(jobs)
    take = lambda n: (refs[:n], refs[n:])
    (rows_ref, cot_ref, rank_row_ref, rank_col_ref, gate_ref, wg_ref, wu_ref, wd_ref), refs = take(8)
    before, refs = take(1 if carry else 0)
    job_ins, refs = take(count)
    (parts_ref, prob_ref, dg_ref, du_ref, dd_ref), refs = take(5)
    job_outs, refs = take(count)
    (x_keep, s_keep, c_keep, h_keep, ag_keep, au_keep, ht_keep), refs = take(7)
    each = functools.partial(each_job, grid, jobs, job_ins, job_outs, *refs)
    step = pl.program_id(0)
    width, hidden = x_keep.shape[1], h_keep.shape[1]
    tokens = rows_ref.shape[1]
    size = ROW_SOURCES * capacity
    strip = 256
    if jobs:

        @pl.when(step == 0)
        def _():
            greet(job_targets(grid, jobs))
            each(lambda copy: copy.start())

    @pl.when(step < steps)
    def _():
        at = pl.ds(pl.multiple_of(step * size, 32), size)
        picks, columns, gates = [], [], []
        for s in range(ROW_SOURCES):
            slots = lax.broadcasted_iota(jnp.int32, (capacity, tokens), 0)
            hit = slots == rank_row_ref[s]
            gate = jnp.sum(jnp.where(hit, gate_ref[s], 0.0), axis=1, keepdims=True)
            pick = hit.astype(f32).astype(bf16)
            picks.append(hit)
            gates.append(gate)
            across = lax.broadcasted_iota(jnp.int32, (tokens, capacity), 1)
            columns.append((across == rank_col_ref[s]).astype(f32).astype(bf16))
            to = pl.ds(pl.multiple_of(step * size + s * capacity, 16), capacity)
            x_keep[to] = times(pick, rows_ref[s]).astype(bf16)
            cot = times(pick, cot_ref[s])
            c_keep[pl.ds(s * capacity, capacity)] = cot.astype(bf16)
            s_keep[to] = (gate * cot).astype(bf16)
        x, slot = x_keep[at], s_keep[at]
        for low in range(0, hidden, strip):
            cut = slice(low, min(low + strip, hidden))
            gate_act = times(x, wg_ref[0, :, cut])
            up_act = times(x, wu_ref[0, :, cut])
            hidden_grad = times_transposed(slot, wd_ref[0, cut])
            activated, slope = silu_parts(gate_act)
            h_keep[at, cut] = (activated * up_act).astype(bf16)
            ag_keep[at, cut] = (hidden_grad * up_act * slope).astype(bf16)
            au_keep[at, cut] = (hidden_grad * activated).astype(bf16)
        h, ag, au = h_keep[at], ag_keep[at], au_keep[at]
        probs = jnp.zeros((size, 1), f32)
        for low in range(0, width, strip):
            cut = slice(low, low + strip)
            made = times(h, wd_ref[0, :, cut]).astype(bf16).astype(f32)
            probs += jnp.sum(made * c_keep[:, cut].astype(f32), axis=1, keepdims=True)
            back = (
                times_transposed(ag, wg_ref[0, cut]) + times_transposed(au, wu_ref[0, cut])
            ).astype(bf16)
            for s in range(ROW_SOURCES):
                mine = slice(s * capacity, (s + 1) * capacity)
                row = times(columns[s], back[mine])
                out = times(columns[s], (gates[s] * made[mine]).astype(bf16))
                if carry:
                    row += before[0][0, s, :, cut].astype(f32)
                    out += before[0][1, s, :, cut].astype(f32)
                parts_ref[0, s, :, cut] = row.astype(bf16)
                parts_ref[1, s, :, cut] = out.astype(bf16)
        for s in range(ROW_SOURCES):
            mine = slice(s * capacity, (s + 1) * capacity)
            prob_ref[s] = jnp.sum(
                jnp.where(picks[s], probs[mine], 0.0), axis=0, keepdims=True
            )

    @pl.when(step == steps)
    def _():
        ht_keep[...] = h_keep[...].T

    @pl.when(step >= steps)
    def _():
        cut = pl.ds(pl.multiple_of((step - steps) * strip, strip), strip)
        turned = x_keep[:, cut].T
        dg_ref[...] = times(turned, ag_keep[...]).astype(bf16)
        du_ref[...] = times(turned, au_keep[...]).astype(bf16)
        dd_ref[...] = times(ht_keep[...], s_keep[:, cut]).astype(bf16)

    if jobs:

        @pl.when(step == pl.num_programs(0) - 1)
        def _():
            each(lambda copy: copy.wait())


def run_expert(grid_of, number, expert, rows, cot, ranks, gates, weights, capacity, before, jobs, job_arrays):
    grid = grid_of()
    sources, tokens = ranks.shape
    width, hidden = weights[0].shape[1:]
    mine = weights[0].shape[0] // ZP
    steps = sources // ROW_SOURCES
    strip = 256
    strips = width // strip
    total = sources * capacity
    turn = lambda s: jnp.minimum(s, steps - 1)
    later = lambda s: jnp.maximum(s - steps, 0)
    block = pl.BlockSpec
    by_source = lambda *rest: block(
        (ROW_SOURCES,) + rest, lambda s: (turn(s),) + (0,) * len(rest)
    )
    held = lambda *rest: block(
        (1,) + rest,
        lambda s: (lax.axis_index("wide") // grid.ny % ZP * mine + expert, 0, 0),
    )
    parts = block((2, ROW_SOURCES, tokens, width), lambda s: (0, turn(s), 0, 0))
    anywhere = block(memory_space=pl.ANY)
    carry = before is not None
    made = pl.pallas_call(
        functools.partial(expert_kernel, grid_of, capacity, steps, jobs, carry),
        grid=(steps + strips,),
        in_specs=[
            by_source(tokens, width),
            by_source(tokens, width),
            by_source(1, tokens),
            by_source(tokens, 1),
            by_source(1, tokens),
            held(width, hidden),
            held(width, hidden),
            held(hidden, width),
        ]
        + [parts] * carry
        + [anywhere] * len(jobs),
        out_specs=[
            parts,
            by_source(1, tokens),
            block((strip, hidden), lambda s: (later(s), 0)),
            block((strip, hidden), lambda s: (later(s), 0)),
            block((hidden, strip), lambda s: (0, later(s))),
        ]
        + [anywhere] * len(jobs),
        scratch_shapes=[
            pltpu.VMEM((total, width), bf16),
            pltpu.VMEM((total, width), bf16),
            pltpu.VMEM((ROW_SOURCES * capacity, width), bf16),
            pltpu.VMEM((total, hidden), bf16),
            pltpu.VMEM((total, hidden), bf16),
            pltpu.VMEM((total, hidden), bf16),
            pltpu.VMEM((hidden, total), bf16),
        ]
        + job_sems(grid, jobs),
        out_shape=[
            jax.ShapeDtypeStruct((2, sources, tokens, width), bf16),
            jax.ShapeDtypeStruct((sources, 1, tokens), f32),
            jax.ShapeDtypeStruct((width, hidden), bf16),
            jax.ShapeDtypeStruct((width, hidden), bf16),
            jax.ShapeDtypeStruct((hidden, width), bf16),
        ]
        + job_shapes(grid, jobs, job_arrays),
        compiler_params=pltpu.CompilerParams(
            vmem_limit_bytes=58 * 2**20,
            **(dict(collective_id=number, has_side_effects=True) if jobs else {}),
        ),
        cost_estimate=pl.CostEstimate(
            flops=total * width * hidden * 18,
            bytes_accessed=width * hidden * 12 + 16 * sources * tokens * width,
            transcendentals=total * hidden,
        ),
    )(
        rows,
        cot,
        ranks[:, None, :],
        ranks[:, :, None],
        gates[:, None, :],
        *weights,
        *([before] if carry else []),
        *job_arrays,
    )
    return made[:5], made[5:]


def jobs_count(grid, jobs):
    return sum({"y": grid.ny, "z": NZ}[axis] - 1 for axis in jobs)


def job_targets(grid, jobs):
    axes = set(jobs)
    place = lambda z, y: (z * grid.ny + y, grid.x * NC + grid.c)
    made = []
    if "y" in axes:
        made += [place(grid.z, (grid.y + d) % grid.ny) for d in range(1, grid.ny)]
    if "z" in axes:
        made += [place((grid.z + d) % NZ, grid.y) for d in range(1, NZ)]
    return made


def each_job(grid, jobs, ins, outs, send_sem, recv_sem, act):
    at = 0
    for axis, src, out in zip(jobs, ins, outs):
        for d in range(1, {"y": grid.ny, "z": NZ}[axis]):
            if axis == "y":
                to = (grid.y + d) % grid.ny
                piece, target = src.at[:, to], (grid.z * grid.ny + to)
            else:
                to = (grid.z + d) % NZ
                piece, target = src.at[to], (to * grid.ny + grid.y)
            act(
                pltpu.make_async_remote_copy(
                    src_ref=piece,
                    dst_ref=out.at[d - 1],
                    send_sem=send_sem.at[at],
                    recv_sem=recv_sem.at[at],
                    device_id=(target, grid.x * NC + grid.c),
                    device_id_type=pl.DeviceIdType.MESH,
                )
            )
            at += 1


def job_shapes(grid, jobs, arrays):
    made = []
    for axis, v in zip(jobs, arrays):
        shape = (grid.ny - 1, NZ) + v.shape[2:] if axis == "y" else (NZ - 1,) + v.shape[1:]
        made.append(jax.ShapeDtypeStruct(shape, v.dtype))
    return made


def job_sems(grid, jobs):
    count = max(jobs_count(grid, jobs), 1)
    return [pltpu.SemaphoreType.DMA((count,)), pltpu.SemaphoreType.DMA((count,))]


def dense_kernel(grid_of, orders, jobs, items, *refs):
    grid = grid_of()
    z, y, x, c, nx, ny = grid.z, grid.y, grid.x, grid.c, grid.nx, grid.ny
    count, more = len(orders), len(jobs)
    wholes = items[-1][0] + 1
    take = lambda n: (refs[:n], refs[n:])
    ins, refs = take(wholes)
    job_ins, refs = take(more)
    outs, refs = take(wholes)
    job_outs, refs = take(more)
    strip = lambda v, low, wide: v.at[(slice(None),) * (len(v.shape) - 1) + (pl.ds(low, wide),)]
    ins = [strip(ins[k], low, wide) for k, low, wide in items]
    outs = [strip(outs[k], low, wide) for k, low, wide in items]
    held, refs = take(count)
    got_c, refs = take(count)
    got_one, refs = take(count)
    got_two, refs = take(count)
    got_z, refs = take(count)
    local_sem, c_sem, one_sem, two_sem, z_sem, out_sem, send_sem, job_send, job_recv = refs
    device = lambda tz, ty, tx, tc: (tz * ny + ty, tx * NC + tc)
    other = (c + 1) % NC
    greet(
        [device(z, y, x, other)]
        + [device(z, y, (x + d) % nx, c) for d in range(1, nx)]
        + [device(z, (y + d) % ny, x, c) for d in range(1, ny)]
        + [device((z + d) % NZ, y, x, c) for d in range(1, NZ)]
    )
    send = Sender(send_sem)
    loads = []

    def begin(k):
        send(ins[k].at[:, :, :, other], got_c[k], c_sem.at[k], device(z, y, x, other))
        load = pltpu.make_async_copy(ins[k].at[:, :, :, c], held[k], local_sem.at[k])
        load.start()
        loads.append(load)

    for k in range(min(3, count)):
        begin(k)
    each_job(grid, jobs, job_ins, job_outs, job_send, job_recv, lambda copy: copy.start())

    def add(dst, src):
        lead = dst.shape[:-2]
        total = 1
        for n in lead:
            total *= n

        @pl.loop(0, total)
        def _(i):
            index = []
            for n in reversed(lead):
                index.insert(0, i % n)
                i = i // n
            index = tuple(index)
            dst[index] = (dst[index].astype(f32) + src[index].astype(f32)).astype(dst.dtype)

    def first(k):
        if k + 3 < count:
            begin(k + 3)
        loads[k].wait()
        arrived(got_c[k], c_sem.at[k])
        add(held[k], got_c[k])
        if orders[k] == "xy":
            for d in range(1, nx):
                to = (x + d) % nx
                send(held[k].at[:, :, to], got_one[k].at[d - 1], one_sem.at[k, d - 1], device(z, y, to, c))
        else:
            for d in range(1, ny):
                to = (y + d) % ny
                send(held[k].at[:, to], got_one[k].at[d - 1], one_sem.at[k, d - 1], device(z, to, x, c))

    def second(k):
        mine = held[k].at[:, :, x] if orders[k] == "xy" else held[k].at[:, y]
        for d in range(1, nx if orders[k] == "xy" else ny):
            arrived(got_one[k].at[d - 1], one_sem.at[k, d - 1])
            add(mine, got_one[k].at[d - 1])
        if orders[k] == "xy":
            for d in range(1, ny):
                to = (y + d) % ny
                send(held[k].at[:, to, x], got_two[k].at[d - 1], two_sem.at[k, d - 1], device(z, to, x, c))
        else:
            for d in range(1, nx):
                to = (x + d) % nx
                send(held[k].at[:, y, to], got_two[k].at[d - 1], two_sem.at[k, d - 1], device(z, y, to, c))

    results = []

    def third(k):
        mine = held[k].at[:, y, x]
        for d in range(1, ny if orders[k] == "xy" else nx):
            arrived(got_two[k].at[d - 1], two_sem.at[k, d - 1])
            add(mine, got_two[k].at[d - 1])
        near = z // ZP * ZP + (z + 1) % ZP
        for n in range(NZ // ZP):
            to = (z + 1) % ZP + n * ZP
            send(held[k].at[to, y, x], got_z[k].at[n], z_sem.at[k, n], device(near, y, x, c))

    def fourth(k):
        for n in range(NZ // ZP):
            arrived(got_z[k].at[n], z_sem.at[k, n])
            at = (z % ZP + n * ZP, y, x)
            held[k][at] = (held[k][at].astype(f32) + got_z[k][n].astype(f32)).astype(held[k].dtype)
        for n in range(1, NZ // ZP):
            to = (z + n * ZP) % NZ
            send(held[k].at[to, y, x], outs[k].at[n], z_sem.at[k, NZ // ZP + n - 1], device(to, y, x, c))
        result = pltpu.make_async_copy(held[k].at[z, y, x], outs[k].at[0], out_sem.at[k])
        result.start()
        results.append(result)

    for t in range(count + 6):
        for stage, late in ((first, 0), (second, 2), (third, 4), (fourth, 6)):
            if 0 <= t - late < count:
                stage(t - late)
    for k in range(count):
        for n in range(1, NZ // ZP):
            arrived(outs[k].at[n], z_sem.at[k, NZ // ZP + n - 1])
        results[k].wait()
    each_job(grid, jobs, job_ins, job_outs, job_send, job_recv, lambda copy: copy.wait())
    send.finish()


def reduce_dense(grid_of, number, arrays, jobs, job_arrays):
    grid = grid_of()
    nx, ny = grid.nx, grid.ny
    items = []
    for k, v in enumerate(arrays):
        wide = v.shape[5]
        low = wide // 2 if wide % 256 == 0 else wide
        items += [(k, at, low) for at in range(0, wide, low)]
    orders = ["xy" if n % 2 == 0 else "yx" for n in range(len(items))]
    count = len(items)
    anywhere = pl.BlockSpec(memory_space=pl.ANY)
    dma = pltpu.SemaphoreType.DMA
    block = [(arrays[k].shape[4], wide) for k, _, wide in items]
    kind = [arrays[k].dtype for k, _, _ in items]
    far = max(nx, ny)
    held = [pltpu.VMEM((NZ, ny, nx) + b, t) for b, t in zip(block, kind)]
    one = [
        pltpu.VMEM((nx - 1, NZ, ny) + b if o == "xy" else (ny - 1, NZ, nx) + b, t)
        for b, t, o in zip(block, kind, orders)
    ]
    two = [
        pltpu.VMEM(((ny if o == "xy" else nx) - 1, NZ) + b, t)
        for b, t, o in zip(block, kind, orders)
    ]
    made = pl.pallas_call(
        functools.partial(dense_kernel, grid_of, orders, jobs, items),
        out_shape=tuple(
            [jax.ShapeDtypeStruct((NZ // ZP,) + v.shape[4:], v.dtype) for v in arrays]
            + job_shapes(grid, jobs, job_arrays)
        ),
        in_specs=[anywhere] * (len(arrays) + len(jobs)),
        out_specs=(anywhere,) * (len(arrays) + len(jobs)),
        scratch_shapes=held
        + held
        + one
        + two
        + [pltpu.VMEM((NZ // ZP,) + b, t) for b, t in zip(block, kind)]
        + [
            dma((count,)),
            dma((count,)),
            dma((count, far)),
            dma((count, far)),
            dma((count, NZ - 1)),
            dma((count,)),
            dma((count * (1 + nx + ny + NZ),)),
        ]
        + job_sems(grid, jobs),
        compiler_params=pltpu.CompilerParams(
            collective_id=number,
            has_side_effects=True,
            vmem_limit_bytes=60 * 2**20,
        ),
    )(*arrays, *job_arrays)
    return made[: len(arrays)], made[len(arrays) :]


def finish_kernel(grid_of, mine, dense, *refs):
    grid = grid_of()
    kinds = 3
    names = mine * kinds
    own, far = refs[:names], refs[names : 2 * names]
    terms = refs[2 * names : 2 * names + dense]
    outs = refs[2 * names + dense :]
    for n in range(names):
        i, kind = n // kinds, n % kinds
        sums = [own[n][0].astype(f32), None]
        for d in range(1, NZ):
            got = far[n][d - 1].astype(f32)
            sums[d % ZP] = got if sums[d % ZP] is None else sums[d % ZP] + got
        outs[kind][grid.zm, i] = sums[0]
        outs[kind][1 - grid.zm, i] = sums[1]
    for n in range(dense):
        total = terms[n][0].astype(f32)
        for d in range(1, terms[n].shape[0]):
            total = total + terms[n][d].astype(f32)
        outs[kinds + n][...] = total


def finish(grid_of, mine, columns, far, terms):
    grid = grid_of()
    whole = lambda v: pl.BlockSpec(v.shape, lambda _: (0,) * len(v.shape))
    out_shape = [
        jax.ShapeDtypeStruct((ZP, mine) + columns[k].shape[1:], f32) for k in range(3)
    ] + [jax.ShapeDtypeStruct(v.shape[1:], f32) for v in terms]
    return pl.pallas_call(
        functools.partial(finish_kernel, grid_of, mine, len(terms)),
        grid=(1,),
        out_shape=out_shape,
        in_specs=[
            pl.BlockSpec(
                (1,) + v.shape[1:],
                lambda _: (lax.axis_index("wide") // grid.ny, 0, 0),
            )
            for v in columns
        ]
        + [whole(v) for v in far]
        + [whole(v) for v in terms],
        out_specs=[whole(v) for v in out_shape],
        compiler_params=pltpu.CompilerParams(vmem_limit_bytes=62 * 2**20),
    )(*columns, *far, *terms)


def attention_bias(segment, labels_all, query_places, key_places):
    same_doc = segment[:, None] == labels_all[None, :]
    allowed = same_doc & (query_places[:, None] >= key_places[None, :])
    return jnp.where(allowed, 0.0, masked_value).astype(f32)


def body(
    wide,
    ep,
    activations,
    segment,
    routes,
    gain_attention,
    query_weight,
    key_weight,
    value_weight,
    output_weight,
    gain_experts,
    router_weight,
    shared_gate,
    shared_up,
    shared_down,
    expert_gate,
    expert_up,
    expert_down,
    cotangent,
):
    grid_of = functools.partial(Grid, wide, ep)
    grid = grid_of()
    nx, ny = grid.nx, grid.ny
    tok_rows, width = activations.shape
    heads = width // HD
    top_count = routes.shape[1]
    experts = router_weight.shape[1]
    local_experts = expert_gate.shape[0]
    mine = local_experts // ZP
    hidden_width = expert_gate.shape[2]
    sources = ZP * nx * NC
    capacity = min((tok_rows * top_count * 10 // (7 * experts) + 7) // 8 * 8, tok_rows)

    bundle = jnp.concatenate(
        [
            query_weight,
            key_weight,
            value_weight,
            output_weight,
            router_weight,
            gain_attention[:, None],
            gain_experts[:, None],
            jnp.zeros((gain_experts.shape[0], 128 - experts - 2), bf16),
        ],
        axis=1,
    )
    integers = jnp.concatenate([routes.T, segment[None, :]], axis=0)
    bundle_all, group_rows, cot_all, integers_all = gather_first(
        grid_of, bundle, activations, cotangent, integers
    )
    group_rows = group_rows.reshape(-1, width)
    integers_all = integers_all.reshape(sources, top_count + 1, tok_rows)
    bundle_all = bundle_all.reshape(width, bundle.shape[1])
    w_out = bundle_all[:, 3 * width : 4 * width]
    small_all = bundle_all[:, 4 * width :]
    gather_all = lambda v: lax.all_gather(v, BOTH, axis=0, tiled=True)
    shared_in, shared_out_in, integers_all = lax.optimization_barrier(
        (
            jnp.concatenate([shared_gate, shared_up], axis=1),
            shared_down,
            integers_all,
        )
    )
    s_both = gather_all(shared_in)
    s_down = gather_all(shared_out_in)
    w_router = small_all[:, :experts]
    gain_one = small_all[:, experts].astype(f32)
    gain_two = small_all[:, experts + 1].astype(f32)

    inputs = activations.astype(f32)
    inverse_one = norm_scale(inputs)
    group_inputs = group_rows.astype(f32)
    normed_group = (group_inputs * norm_scale(group_inputs) * gain_one).astype(bf16)
    normed_one = normed_group[:tok_rows]
    queries, keys_all, values_all = project(normed_group, bundle_all, tok_rows)
    labels_all = integers_all[: nx * NC, top_count].reshape(-1)
    steps = jnp.arange(tok_rows, dtype=jnp.int32)
    block_places = (
        (grid.x + jnp.arange(nx, dtype=jnp.int32)[:, None]) % nx * NC
        + (grid.c + jnp.arange(NC, dtype=jnp.int32)[None, :]) % NC
    ).reshape(-1)
    key_places = (block_places[:, None] * tok_rows + steps[None, :]).reshape(-1)
    query_places = (grid.x * NC + grid.c) * tok_rows + steps
    bias = attention_bias(segment, labels_all, query_places, key_places)
    attended = attention_forward(queries, keys_all, values_all, bias)
    middle = inputs + times(attended, w_out)
    inverse_two = norm_scale(middle)
    normed_two = (middle * inverse_two * gain_two).astype(bf16)

    rows_all = exchange(grid_of, ZP, 1, normed_two)
    rows_all = rows_all.reshape(sources, tok_rows, width)
    cot_all = cot_all.reshape(sources, tok_rows, width)
    router_probs_all = jax.nn.softmax(
        times(rows_all.reshape(-1, width), w_router).reshape(sources, tok_rows, experts),
        axis=-1,
    )
    router_probs = router_probs_all[0]
    first_expert = (grid.x * NC + grid.c) * local_experts + grid.zm * mine
    routes_all = integers_all[:, :top_count]
    numbers = first_expert + jnp.arange(mine, dtype=jnp.int32)
    marks = jnp.any(
        routes_all[None] == numbers[:, None, None, None], axis=2
    )
    earlier = (steps[:, None] < steps[None, :]).astype(bf16)
    ranks = jnp.einsum(
        "irt,tu->iru", marks.astype(bf16), earlier, preferred_element_type=f32
    ).astype(jnp.int32)
    ranks = jnp.where(marks, ranks, -1)
    gates_mine = jnp.moveaxis(
        lax.dynamic_slice_in_dim(router_probs_all, first_expert, mine, axis=2), 2, 0
    )
    def by_wide(v):
        return v.reshape(NZ, ny, v.shape[0] // wide, v.shape[1])

    names = [(i, k) for i in range(mine) for k in range(3)]
    grads, along_y, along_z = {}, {}, {}

    def jobs_of(which_y, which_z):
        tags = tuple("y" for _ in which_y) + tuple("z" for _ in which_z)
        return tags, [grads[n] for n in which_y] + [column[n] for n in which_z]

    def landed(which_y, which_z, moved):
        along_y.update(zip(which_y, moved))
        along_z.update(zip(which_z, moved[len(which_y) :]))

    def summed(name):
        total = lax.dynamic_index_in_dim(grads[name], grid.y, 1, keepdims=False).astype(f32)
        for d in range(ny - 1):
            total = total + along_y[name][d].astype(f32)
        return total.astype(bf16)

    column = {}
    both_parts = None
    prob_parts = []
    for i in range(mine):
        behind = (names[:1], []) if i else ([], [])
        (both_parts, probs_here, *made), moved = run_expert(
            grid_of,
            5 + i,
            i,
            rows_all,
            cot_all,
            ranks[i],
            gates_mine[i],
            (expert_gate, expert_up, expert_down),
            capacity,
            both_parts,
            *jobs_of(*behind),
        )
        landed(*behind, moved)
        prob_parts.append(probs_here[:, 0])
        grads.update({(i, k): by_wide(v) for k, v in enumerate(made)})
    column.update({name: summed(name) for name in along_y})
    behind = (names[1:3], names[:1])
    (
        sums,
        sent,
        shared_out,
        shared_back,
        shared_gate_grad,
        shared_up_grad,
        shared_down_grad,
    ), moved = sum_around(
        grid_of,
        ZP,
        2,
        both_parts.reshape(2, ZP, nx, NC, tok_rows, width),
        jnp.stack(prob_parts, axis=1).reshape(ZP, nx, NC, mine, tok_rows),
        (normed_two, cotangent, s_both, s_down),
        *jobs_of(*behind),
    )
    landed(*behind, moved)
    column.update({name: summed(name) for name in behind[0]})
    routed_grad = sums[0].astype(f32)
    routed = sums[1].astype(f32)
    dz = (grid.zm + jnp.arange(ZP, dtype=jnp.int32)) % ZP
    owner = block_places.reshape(1, nx, NC, 1) * local_experts
    owner = owner + dz[:, None, None, None] * mine + jnp.arange(mine, dtype=jnp.int32)
    same = owner.reshape(-1)[None, :] == jnp.arange(experts, dtype=jnp.int32)[:, None]
    prob_grad = jnp.sum(
        jnp.where(same[:, :, None], sent.reshape(1, experts, tok_rows), 0.0), axis=1
    ).T

    out_grad = cotangent.astype(f32)
    block_out = (middle + shared_out + routed).astype(bf16)

    logit_grad = router_probs * (
        prob_grad - jnp.sum(router_probs * prob_grad, axis=-1, keepdims=True)
    )
    router_grad = lax.dot_general(
        normed_two.astype(f32),
        logit_grad,
        (((0,), (0,)), ((), ())),
        precision=lax.Precision.HIGHEST,
        preferred_element_type=f32,
    )
    normed_two_grad = (
        shared_back
        + routed_grad
        + lax.dot_general(
            logit_grad,
            w_router.astype(f32),
            (((1,), (1,)), ((), ())),
            precision=lax.Precision.HIGHEST,
            preferred_element_type=f32,
        )
    )
    gain_two_grad, middle_part = norm_backward(
        middle, inverse_two, gain_two, normed_two_grad
    )
    middle_grad = out_grad + middle_part
    branch_grad = middle_grad.astype(bf16)
    output_weight_grad = contract_rows(attended, branch_grad)
    attended_grad = times_transposed(branch_grad, w_out).astype(bf16)

    behind = (names[3:4], names[1:2])
    query_act_grad, parts, moved = attention_backward(
        grid_of,
        1 + 8,
        queries,
        keys_all,
        values_all,
        attended_grad,
        bias.T,
        *jobs_of(*behind),
    )
    landed(*behind, moved)
    behind = (names[4:], names[2:4])
    column.update({name: summed(name) for name in names[3:4]})
    ((value_key,), moved) = sum_around(
        grid_of,
        1,
        3,
        parts.reshape(2, 1, nx, NC, tok_rows, width),
        None,
        (),
        *jobs_of(*behind),
    )
    landed(*behind, moved)
    column.update({name: summed(name) for name in names[4:]})
    query_w_grad, key_w_grad, value_w_grad, normed_one_grad = project_back(
        normed_one, query_act_grad, value_key, bundle_all
    )
    gain_one_grad, input_part = norm_backward(
        inputs, inverse_one, gain_one, normed_one_grad
    )
    input_grad = middle_grad + input_part

    def by_place(v):
        return v.reshape((NZ, ny, nx, NC, v.shape[0] // (wide * ep)) + v.shape[1:])

    counts = jnp.sum(
        (routes[:, :, None] == jnp.arange(experts, dtype=jnp.int32)).astype(f32),
        axis=(0, 1),
    )
    share = gain_attention.shape[0]
    count_block = jnp.pad(
        jnp.tile(counts.reshape(1, ep, 1, local_experts), (wide, 1, 1, 1)),
        ((0, 0), (0, 0), (0, 0), (0, 128 - local_experts)),
    )
    extras = jnp.concatenate(
        [
            router_grad,
            gain_one_grad[:, None],
            gain_two_grad[:, None],
            jnp.zeros((width, 128 - experts - 2), f32),
        ],
        axis=1,
    ).reshape(wide, ep, share, 128)
    extras = jnp.concatenate(
        [extras, count_block, jnp.zeros((wide, ep, 7, 128), f32)], axis=2
    )
    dense = [
        output_weight_grad,
        shared_down_grad,
        shared_gate_grad,
        shared_up_grad,
        query_w_grad,
        key_w_grad,
        value_w_grad,
    ]
    terms, moved = reduce_dense(
        grid_of,
        4,
        [by_place(v.astype(bf16)) for v in dense]
        + [extras.reshape(NZ, ny, nx, NC, share + 8, 128)],
        *jobs_of([], names[4:]),
    )
    landed([], names[4:], moved)
    (
        expert_gate_grad,
        expert_up_grad,
        expert_down_grad,
        output_weight_sum,
        shared_down_sum,
        shared_gate_sum,
        shared_up_sum,
        query_sum,
        key_sum,
        value_sum,
        extra_sum,
    ) = finish(
        grid_of, mine, [column[n] for n in names], [along_z[n] for n in names], terms
    )
    expert_gate_grad, expert_up_grad, expert_down_grad = (
        v.reshape((local_experts,) + v.shape[2:])
        for v in (expert_gate_grad, expert_up_grad, expert_down_grad)
    )
    return (
        block_out,
        input_grad,
        extra_sum[:share, experts],
        query_sum,
        key_sum,
        value_sum,
        output_weight_sum,
        extra_sum[:share, experts + 1],
        extra_sum[:share, :experts],
        shared_gate_sum,
        shared_up_sum,
        shared_down_sum,
        expert_gate_grad,
        expert_up_grad,
        expert_down_grad,
        extra_sum[share, :local_experts].astype(jnp.int32),
    )


def solution(mesh):
    split = P(BOTH, None)
    line = P(BOTH)
    held = P("ep", None, None)
    out_held = P("ep", "wide", None)
    in_specs = (
        (split, line, split, line)
        + (split,) * 4
        + (line,)
        + (split,) * 4
        + (held,) * 3
        + (split,)
    )
    out_specs = (
        (split, split, line)
        + (split,) * 4
        + (line,)
        + (split,) * 4
        + (out_held,) * 3
        + (P("ep"),)
    )
    return jax.shard_map(
        functools.partial(body, mesh.shape["wide"], mesh.shape["ep"]),
        mesh=mesh,
        in_specs=in_specs,
        out_specs=out_specs,
        check_vma=False,
    )
```

```python
import functools

import jax
import jax.numpy as jnp
from jax import lax
from jax.experimental import pallas as pl
from jax.experimental.pallas import tpu as pltpu
from jax.sharding import PartitionSpec as P

HD = 128
NC = 2
NZ = 4
ZP = 2
epsilon = 1e-06
masked_value = -1e30
BOTH = ("wide", "ep")
f32 = jnp.float32
bf16 = jnp.bfloat16


def contract_rows(left, right):
    return lax.dot_general(
        left, right, (((0,), (0,)), ((), ())), preferred_element_type=f32
    )


def times_transposed(left, right):
    return lax.dot_general(
        left, right, (((1,), (1,)), ((), ())), preferred_element_type=f32
    )


def times(left, right):
    return jnp.dot(left, right, preferred_element_type=f32)


def norm_scale(values):
    return lax.rsqrt(jnp.mean(values * values, axis=-1, keepdims=True) + epsilon)


def norm_backward(values, inverse, gain, normed_grad):
    weighted = normed_grad * gain
    gain_grad = jnp.sum(normed_grad * values * inverse, axis=0)
    cubed = inverse * inverse * inverse
    values_grad = inverse * weighted - values * cubed * jnp.mean(
        weighted * values, axis=-1, keepdims=True
    )
    return (gain_grad, values_grad)


def silu_parts(gate_act):
    logistic = 0.5 * jnp.tanh(0.5 * gate_act) + 0.5
    return (gate_act * logistic, logistic * (1.0 + gate_act * (1.0 - logistic)))


class Grid:
    def __init__(self, wide, ep):
        self.ny, self.nx, self.ep = wide // NZ, ep // NC, ep
        w, e = lax.axis_index("wide"), lax.axis_index("ep")
        self.z, self.y, self.x, self.c = w // self.ny, w % self.ny, e // NC, e % NC
        self.zm = self.z % ZP

    def pairs(self, move):
        made = []
        for z in range(NZ):
            for y in range(self.ny):
                for x in range(self.nx):
                    for c in range(NC):
                        tz, ty, tx, tc = move(z, y, x, c)
                        made.append(
                            (
                                (z * self.ny + y) * self.ep + x * NC + c,
                                (tz * self.ny + ty) * self.ep + tx * NC + tc,
                            )
                        )
        return made

    def send(self, value, axis, step):
        moves = {
            "c": lambda z, y, x, c: (z, y, x, (c + step) % NC),
            "x": lambda z, y, x, c: (z, y, (x + step) % self.nx, c),
            "y": lambda z, y, x, c: (z, (y + step) % self.ny, x, c),
            "z": lambda z, y, x, c: ((z + step) % NZ, y, x, c),
            "p": lambda z, y, x, c: (z // ZP * ZP + (z % ZP + step) % ZP, y, x, c),
        }
        return lax.ppermute(value, BOTH, self.pairs(moves[axis]))

    def size(self, axis):
        return {"c": NC, "x": self.nx, "y": self.ny, "z": NZ, "p": ZP}[axis]

    def place(self, axis):
        return {"c": self.c, "x": self.x, "y": self.y, "z": self.z, "p": self.zm}[axis]

    def gather(self, value, axis, at):
        parts = [value] + [
            self.send(value, axis, -d) for d in range(1, self.size(axis))
        ]
        return jnp.stack(parts, axis=at)

    def scatter(self, value, axis, at):
        total = lax.index_in_dim(value, 0, at, keepdims=False).astype(f32)
        for d in range(1, self.size(axis)):
            part = lax.index_in_dim(value, d, at, keepdims=False)
            total = total + self.send(part, axis, d).astype(f32)
        return total.astype(value.dtype)

    def scatter_absolute(self, value, axis, at):
        n, me = self.size(axis), self.place(axis)
        take = lambda i: lax.dynamic_index_in_dim(value, i, at, keepdims=False)
        total = take(me).astype(f32)
        for d in range(1, n):
            total = total + self.send(take((me + d) % n), axis, d).astype(f32)
        return total.astype(value.dtype)


class Sender:
    def __init__(self, sems):
        self.sems, self.started = sems, []

    def __call__(self, src, dst, sem, target):
        copy = pltpu.make_async_remote_copy(
            src_ref=src,
            dst_ref=dst,
            send_sem=self.sems.at[len(self.started)],
            recv_sem=sem,
            device_id=target,
            device_id_type=pl.DeviceIdType.MESH,
        )
        copy.start()
        self.started.append(copy)

    def finish(self):
        for copy in self.started:
            copy.wait_send()


def arrived(dst, sem):
    pltpu.make_async_copy(dst, dst, sem).wait()


def greet(targets):
    barrier = pltpu.get_barrier_semaphore()
    for target in targets:
        pl.semaphore_signal(
            barrier, inc=1, device_id=target, device_id_type=pl.DeviceIdType.MESH
        )
    pl.semaphore_wait(barrier, len(targets))


def around(grid, zp):
    steps = [(a, b, e) for a in range(zp) for b in range(grid.nx) for e in range(NC)]
    return steps[1:]


def stepped(grid, zp, a, b, e):
    z = grid.z // zp * zp + (grid.z % zp + a) % zp
    return (
        z * grid.ny + grid.y,
        (grid.x + b) % grid.nx * NC + (grid.c + e) % NC,
    )


def gather_kernel(
    grid_of,
    w_ref,
    rows_ref,
    cot_ref,
    ints_ref,
    w_all,
    rows_all,
    cot_all,
    ints_all,
    plane_sem,
    core_sem,
    rows_sem,
    cot_sem,
    ints_sem,
    send_sem,
    local_sem,
    z_in,
    z_out,
    x_out,
    y_out,
    c_out,
):
    grid = grid_of()
    z, y, x, c, nx, ny = grid.z, grid.y, grid.x, grid.c, grid.nx, grid.ny

    def device(tz, ty, tx, tc):
        return (tz * ny + ty, tx * NC + tc)

    def block(dz, dy, dx, tc):
        place = (z + NZ - dz) % NZ * ny + (y + ny - dy) % ny
        return w_all.at[place * (nx * NC) + (x + nx - dx) % nx * NC + tc]

    shift_z = lambda d: (z + d) % NZ
    shift_y = lambda d: (y + d) % ny
    shift_x = lambda d: (x + d) % nx
    back = lambda d: (nx - d) % nx
    other = (c + 1) % NC
    to = functools.partial(stepped, grid, ZP)
    greet(
        [device(shift_z(d), y, x, c) for d in range(1, NZ)]
        + [device(z, shift_y(d), x, c) for d in range(1, ny)]
        + [to(*s) for s in around(grid, ZP)]
    )
    send = Sender(send_sem)
    locals_ = [
        (w_ref, block(0, 0, 0, c)),
        (rows_ref, rows_all.at[0, 0]),
        (cot_ref, cot_all.at[0, 0, 0]),
        (ints_ref, ints_all.at[0, 0, 0]),
    ]
    locals_ = [
        pltpu.make_async_copy(src, dst, local_sem.at[k])
        for k, (src, dst) in enumerate(locals_)
    ]
    for copy in locals_:
        copy.start()
    def start(src, dst, out_sem, in_sem, target):
        pltpu.make_async_remote_copy(
            src_ref=src,
            dst_ref=dst,
            send_sem=out_sem,
            recv_sem=in_sem,
            device_id=target,
            device_id_type=pl.DeviceIdType.MESH,
        ).start()

    def each_source(act, least=0, most=NZ - 1):
        for d in range(least, most + 1):
            for way in range(2):
                there = z - d >= 0 if way == 0 else z + d <= NZ - 1
                pl.when(there)(
                    functools.partial(act, way, d, d if way == 0 else (NZ - d) % NZ)
                )

    def pass_on(way, d, dz):
        here = block(dz, 0, 0, c)
        src = here if d else w_ref
        if d:
            arrived(here, z_in.at[way, d])
        if d < NZ - 1:

            @pl.when(z < NZ - 1 if way == 0 else z > 0)
            def _():
                start(
                    src,
                    here,
                    z_out.at[way, d],
                    z_in.at[way, d + 1],
                    device(z + 1 if way == 0 else z - 1, y, x, c),
                )

        if d or way == 0:
            for b in range(1, nx):
                start(src, here, x_out.at[dz, b], plane_sem.at[dz, 0, b], device(z, y, shift_x(b), c))
            for b in range(1, ny):
                start(src, here, y_out.at[dz, 0, b], plane_sem.at[dz, b, 0], device(z, shift_y(b), x, c))
            start(src, here, c_out.at[dz, 0], core_sem.at[dz, 0, 0], device(z, y, x, other))

    def turn(way, d, dz):
        if d == 0 and way == 1:
            return
        for dx in range(1, nx):
            here = block(dz, 0, dx, c)
            arrived(here, plane_sem.at[dz, 0, dx])
            for b in range(1, ny):
                start(here, here, y_out.at[dz, dx, b], plane_sem.at[dz, b, dx], device(z, shift_y(b), x, c))
            start(here, here, c_out.at[dz, dx], core_sem.at[dz, 0, dx], device(z, y, x, other))

    for a, b, e in around(grid, ZP):
        mirror = ((ZP - a) % ZP, back(b), e)
        send(ints_ref, ints_all.at[mirror], ints_sem.at[mirror], to(a, b, e))
    each_source(pass_on, 0, 0)
    for d in range(1, NZ):
        each_source(pass_on, d, d)
        if d == NZ - 1:
            for a in range(1, ZP):
                send(cot_ref, cot_all.at[ZP - a, 0, 0], cot_sem.at[ZP - a, 0, 0, 0], to(a, 0, 0))
            for b in range(1, nx):
                send(cot_ref, cot_all.at[0, back(b), 0], cot_sem.at[0, back(b), 0, 0], to(0, b, 0))
                send(rows_ref, rows_all.at[back(b), 0], rows_sem.at[back(b), 0], to(0, b, 0))
        each_source(turn, d - 1, d - 1)
    each_source(turn, NZ - 1, NZ - 1)
    send(cot_ref, cot_all.at[0, 0, 1], cot_sem.at[0, 0, 1, 0], to(0, 0, 1))
    send(rows_ref, rows_all.at[0, 1], rows_sem.at[0, 1], to(0, 0, 1))
    for d in range(1, nx):
        here = rows_all.at[d, 0]
        arrived(here, rows_sem.at[d, 0])
        send(here, rows_all.at[d, 1], rows_sem.at[d, 1], to(0, 0, 1))
    width = cot_ref.shape[1]
    halves = [
        (slice(None), pl.ds(0, width // 2)),
        (slice(None), pl.ds(width // 2, width // 2)),
    ]
    for a in range(1, ZP):
        here = cot_all.at[a, 0, 0]
        arrived(here, cot_sem.at[a, 0, 0, 0])
        for b in range(1, nx):
            send(here.at[halves[0]], cot_all.at[a, back(b), 0].at[halves[0]], cot_sem.at[a, back(b), 0, 0], to(0, b, 0))
        send(here, cot_all.at[a, 0, 1], cot_sem.at[a, 0, 1, 0], to(0, 0, 1))
    for b in range(1, nx):
        here = cot_all.at[0, b, 0]
        arrived(here, cot_sem.at[0, b, 0, 0])
        for a in range(1, ZP):
            send(here.at[halves[1]], cot_all.at[ZP - a, b, 0].at[halves[1]], cot_sem.at[ZP - a, b, 0, 1], to(a, 0, 0))
        send(here, cot_all.at[0, b, 1], cot_sem.at[0, b, 1, 0], to(0, 0, 1))
    for dz in range(NZ):
        for dy in range(1, ny):
            for dx in range(nx):
                here = block(dz, dy, dx, c)
                arrived(here, plane_sem.at[dz, dy, dx])
                send(here, here, core_sem.at[dz, dy, dx], device(z, y, x, other))
    for a in range(1, ZP):
        for b in range(1, nx):
            here = cot_all.at[a, b, 0]
            for part in range(2):
                arrived(here.at[halves[part]], cot_sem.at[a, b, 0, part])
            send(here, cot_all.at[a, b, 1], cot_sem.at[a, b, 1, 0], to(0, 0, 1))
    for dx in range(nx):
        arrived(rows_all.at[dx, 1], rows_sem.at[dx, 1])
        for a in range(ZP):
            arrived(cot_all.at[a, dx, 1], cot_sem.at[a, dx, 1, 0])
    for a, b, e in around(grid, ZP):
        arrived(ints_all.at[a, b, e], ints_sem.at[a, b, e])
    for dz in range(NZ):
        for dy in range(ny):
            for dx in range(nx):
                arrived(block(dz, dy, dx, other), core_sem.at[dz, dy, dx])
    for copy in locals_:
        copy.wait()
    send.finish()

    def sent(way, d, dz):
        if d < NZ - 1:

            @pl.when(z < NZ - 1 if way == 0 else z > 0)
            def _():
                arrived(w_ref, z_out.at[way, d])

    each_source(sent)
    for dz in range(NZ):
        for b in range(1, nx):
            arrived(w_ref, x_out.at[dz, b])
        for dx in range(nx):
            for b in range(1, ny):
                arrived(w_ref, y_out.at[dz, dx, b])
            arrived(w_ref, c_out.at[dz, dx])


def gather_first(grid_of, w, rows, cot, ints):
    grid = grid_of()
    nx, ny = grid.nx, grid.ny
    places = NZ * ny * nx * NC
    octet = ZP * nx * NC
    sends = (NZ - 1) + NZ * (nx + ny) + 2 * nx + octet * 4 + NZ * nx * ny * (ny + 1)
    anywhere = pl.BlockSpec(memory_space=pl.ANY)
    dma = pltpu.SemaphoreType.DMA
    return pl.pallas_call(
        functools.partial(gather_kernel, grid_of),
        out_shape=(
            jax.ShapeDtypeStruct((places,) + w.shape, w.dtype),
            jax.ShapeDtypeStruct((nx, NC) + rows.shape, rows.dtype),
            jax.ShapeDtypeStruct((ZP, nx, NC) + cot.shape, cot.dtype),
            jax.ShapeDtypeStruct((ZP, nx, NC) + ints.shape, ints.dtype),
        ),
        in_specs=[anywhere] * 4,
        out_specs=(anywhere,) * 4,
        scratch_shapes=[
            dma((NZ, ny, nx)),
            dma((NZ, ny, nx)),
            dma((nx, NC)),
            dma((ZP, nx, NC, 2)),
            dma((ZP, nx, NC)),
            dma((sends,)),
            dma((4,)),
            dma((2, NZ)),
            dma((2, NZ)),
            dma((NZ, nx)),
            dma((NZ, nx, ny)),
            dma((NZ, nx)),
        ],
        compiler_params=pltpu.CompilerParams(collective_id=0, has_side_effects=True),
    )(w, rows, cot, ints)


def shared_compute(n2, cot, w_in, w_down, out, back, dg, du, dd, h, ag, au):
    hidden, width = w_down.shape
    strip = 256
    for low in range(0, hidden, strip):
        cut = slice(low, min(low + strip, hidden))
        up_cut = slice(hidden + cut.start, hidden + cut.stop)
        gate_act = times(n2[...], w_in[:, cut])
        up_act = times(n2[...], w_in[:, up_cut])
        hidden_grad = times_transposed(cot[...], w_down[cut])
        activated, slope = silu_parts(gate_act)
        h[:, cut] = (activated * up_act).astype(bf16)
        ag[:, cut] = (hidden_grad * up_act * slope).astype(bf16)
        au[:, cut] = (hidden_grad * activated).astype(bf16)
    turned = h[...].T
    for low in range(0, width, strip):
        cut = slice(low, low + strip)
        out[:, cut] = times(h[...], w_down[:, cut])
        back[:, cut] = times_transposed(ag[...], w_in[cut, :hidden]) + times_transposed(
            au[...], w_in[cut, hidden:]
        )
        rows = n2[:, cut].T
        dg[cut] = times(rows, ag[...]).astype(bf16)
        du[cut] = times(rows, au[...]).astype(bf16)
        dd[:, cut] = times(turned, cot[:, cut]).astype(bf16)


def exchange_kernel(grid_of, zp, cut, src, out, plane_sem, core_sem, local_sem, send_sem):
    grid = grid_of()
    nx = grid.nx
    send = Sender(send_sem)
    to = functools.partial(stepped, grid, zp)
    greet([to(*s) for s in around(grid, zp)])
    back = lambda d: (nx - d) % nx
    for a in range(1, zp):
        send(src, out.at[zp - a, 0, 0], plane_sem.at[zp - a, 0, 0], to(a, 0, 0))
    for b in range(1, nx):
        send(src, out.at[0, back(b), 0], plane_sem.at[0, back(b), 0], to(0, b, 0))
    send(src, out.at[0, 0, 1], core_sem.at[0, 0], to(0, 0, 1))
    keep = pltpu.make_async_copy(src, out.at[0, 0, 0], local_sem)
    keep.start()
    h0 = (slice(None), pl.ds(0, cut))
    h1 = (slice(None), pl.ds(cut, src.shape[1] - cut))
    for a in range(1, zp):
        here = out.at[a, 0, 0]
        arrived(here, plane_sem.at[a, 0, 0])
        for b in range(1, nx):
            send(here.at[h0], out.at[a, back(b), 0].at[h0], plane_sem.at[a, back(b), 0], to(0, b, 0))
        send(here, out.at[a, 0, 1], core_sem.at[a, 0], to(0, 0, 1))
    for b in range(1, nx):
        here = out.at[0, b, 0]
        arrived(here, plane_sem.at[0, b, 0])
        for a in range(1, zp):
            send(here.at[h1], out.at[zp - a, b, 0].at[h1], plane_sem.at[zp - a, b, 1], to(a, 0, 0))
        send(here, out.at[0, b, 1], core_sem.at[0, b], to(0, 0, 1))
    for a in range(1, zp):
        for b in range(1, nx):
            here = out.at[a, b, 0]
            arrived(here.at[h0], plane_sem.at[a, b, 0])
            arrived(here.at[h1], plane_sem.at[a, b, 1])
            send(here, out.at[a, b, 1], core_sem.at[a, b], to(0, 0, 1))
    for a in range(zp):
        for b in range(nx):
            arrived(out.at[a, b, 1], core_sem.at[a, b])
    keep.wait()
    send.finish()


def exchange(grid_of, zp, number, rows):
    grid = grid_of()
    nx = grid.nx
    sends = zp * nx * 2 + zp * nx * nx * 2
    anywhere = pl.BlockSpec(memory_space=pl.ANY)
    dma = pltpu.SemaphoreType.DMA
    return pl.pallas_call(
        functools.partial(exchange_kernel, grid_of, zp, rows.shape[1] // 256 * 128),
        out_shape=jax.ShapeDtypeStruct((zp, nx, NC) + rows.shape, rows.dtype),
        in_specs=[anywhere],
        out_specs=anywhere,
        scratch_shapes=[dma((zp, nx, 2)), dma((zp, nx)), dma, dma((sends,))],
        compiler_params=pltpu.CompilerParams(
            collective_id=number, has_side_effects=True
        ),
    )(rows)


def add_into(dst, src, rows):
    for k in range(dst.shape[0]):

        @pl.loop(0, dst.shape[1], step=rows)
        def _(i):
            at = pl.ds(pl.multiple_of(i, rows), rows)
            dst[k, at] = (dst[k, at].astype(f32) + src[k, at].astype(f32)).astype(
                dst.dtype
            )


def sum_kernel(grid_of, zp, cut, small, jobs, parts, *refs):
    grid = grid_of()
    nx = grid.nx
    if small:
        pieces, refs = refs[0], refs[1:]
        shared_ins, refs = refs[:4], refs[4:]
    job_ins, refs = refs[: len(jobs)], refs[len(jobs) :]
    out, refs = refs[0], refs[1:]
    if small:
        pieces_out, refs = refs[0], refs[1:]
        shared_outs, refs = refs[:5], refs[5:]
    job_outs, refs = refs[: len(jobs)], refs[len(jobs) :]
    refs, (job_send, job_recv) = refs[:-2], refs[-2:]
    if small:
        shared_held, load_sem, refs = refs[-8:-1], refs[-1], refs[:-8]
        loads = [
            pltpu.make_async_copy(a, b, load_sem.at[k])
            for k, (a, b) in enumerate(zip(shared_ins, shared_held))
        ]
    each = functools.partial(each_job, grid, jobs, job_ins, job_outs, job_send, job_recv)
    own, got_c, turn_x, turn_p, got_p, got_x = refs[:6]
    local_sem, c_sem, turn_sem, p_sem, x_sem, small_sem, send_sem = refs[6:]
    send = Sender(send_sem)
    to = functools.partial(stepped, grid, zp)
    greet([to(*s) for s in around(grid, zp)] + job_targets(grid, jobs))
    width = parts.shape[-1]
    h0, h1 = pl.ds(0, cut), pl.ds(cut, width - cut)
    order = (
        [(a, b) for a in range(1, zp) for b in range(1, nx)]
        + [(a, 0) for a in range(1, zp)]
        + [(0, b) for b in range(1, nx)]
        + [(0, 0)]
    )
    for a, b in order:
        send(parts.at[:, a, b, 1], got_c.at[:, a, b], c_sem.at[a, b], to(0, 0, 1))
        pltpu.make_async_copy(
            parts.at[:, a, b, 0], own.at[:, a, b], local_sem.at[a, b]
        ).start()
    if small:
        for a, b, e in around(grid, zp):
            mirror = ((zp - a) % zp, (nx - b) % nx, e)
            send(
                pieces.at[a, b, e],
                pieces_out.at[mirror],
                small_sem.at[mirror],
                to(a, b, e),
            )
        pltpu.make_async_copy(
            pieces.at[0, 0, 0], pieces_out.at[0, 0, 0], small_sem.at[0, 0, 0]
        ).start()
    each(lambda copy: copy.start())
    if small:
        for load in loads:
            load.start()
    rows = 32

    def ready(a, b):
        arrived(got_c.at[:, a, b], c_sem.at[a, b])
        pltpu.make_async_copy(
            parts.at[:, a, b, 0], own.at[:, a, b], local_sem.at[a, b]
        ).wait()
        add_into(own.at[:, a, b], got_c.at[:, a, b], rows)

    for a in range(1, zp):
        for b in range(1, nx):
            ready(a, b)
            send(own.at[:, a, b, :, h0], turn_x.at[:, a - 1, b - 1], turn_sem.at[a - 1, b - 1, 0], to(0, b, 0))
            send(own.at[:, a, b, :, h1], turn_p.at[:, a - 1, b - 1], turn_sem.at[a - 1, b - 1, 1], to(a, 0, 0))
    for a in range(1, zp):
        ready(a, 0)
    for b in range(1, nx):
        ready(0, b)
    for a in range(1, zp):
        for b in range(1, nx):
            arrived(turn_x.at[:, a - 1, b - 1], turn_sem.at[a - 1, b - 1, 0])
            add_into(own.at[:, a, 0, :, h0], turn_x.at[:, a - 1, b - 1], rows)
        send(own.at[:, a, 0], got_p.at[:, a - 1], p_sem.at[a - 1], to(a, 0, 0))
    for b in range(1, nx):
        for a in range(1, zp):
            arrived(turn_p.at[:, a - 1, b - 1], turn_sem.at[a - 1, b - 1, 1])
            add_into(own.at[:, 0, b, :, h1], turn_p.at[:, a - 1, b - 1], rows)
        send(own.at[:, 0, b], got_x.at[:, b - 1], x_sem.at[b - 1], to(0, b, 0))
    ready(0, 0)
    if small:
        for load in loads:
            load.wait()
        shared_compute(*shared_held[:4], *shared_outs, *shared_held[4:])
    for a in range(1, zp):
        arrived(got_p.at[:, a - 1], p_sem.at[a - 1])
        add_into(own.at[:, 0, 0], got_p.at[:, a - 1], rows)
    for b in range(1, nx):
        arrived(got_x.at[:, b - 1], x_sem.at[b - 1])
        add_into(own.at[:, 0, 0], got_x.at[:, b - 1], rows)
    result = pltpu.make_async_copy(own.at[:, 0, 0], out, local_sem.at[0, 0])
    result.start()
    if small:
        for a, b, e in [(0, 0, 0)] + around(grid, zp):
            arrived(pieces_out.at[a, b, e], small_sem.at[a, b, e])
    result.wait()
    each(lambda copy: copy.wait())
    send.finish()


def sum_around(grid_of, zp, number, parts, pieces=None, shared=(), jobs=(), job_arrays=()):
    grid = grid_of()
    nx = grid.nx
    payloads, rows, width = parts.shape[0], parts.shape[-2], parts.shape[-1]
    cut = width // 640 * 512
    anywhere = pl.BlockSpec(memory_space=pl.ANY)
    dma = pltpu.SemaphoreType.DMA
    small = pieces is not None
    out_shape = [jax.ShapeDtypeStruct((payloads, rows, width), parts.dtype)]
    args = [parts]
    if small:
        out_shape.append(jax.ShapeDtypeStruct(pieces.shape, pieces.dtype))
        args += [pieces, *shared]
        tokens, hidden = shared[0].shape[0], shared[3].shape[0]
        out_shape += [jax.ShapeDtypeStruct((tokens, width), f32)] * 2
        out_shape += [jax.ShapeDtypeStruct((width, hidden), bf16)] * 2
        out_shape.append(jax.ShapeDtypeStruct((hidden, width), bf16))
    plain = len(out_shape)
    out_shape += job_shapes(grid, jobs, job_arrays)
    args += list(job_arrays)
    turns = (max(zp - 1, 1), max(nx - 1, 1))
    vmem = lambda shape: pltpu.VMEM(shape, parts.dtype)
    made = pl.pallas_call(
        functools.partial(sum_kernel, grid_of, zp, cut, small, jobs),
        out_shape=tuple(out_shape),
        in_specs=[anywhere] * len(args),
        out_specs=tuple(
            pl.BlockSpec(memory_space=pltpu.VMEM) if 2 <= n < plain else anywhere
            for n in range(len(out_shape))
        ),
        scratch_shapes=[
            vmem((payloads, zp, nx, rows, width)),
            vmem((payloads, zp, nx, rows, width)),
            vmem((payloads,) + turns + (rows, cut)),
            vmem((payloads,) + turns + (rows, width - cut)),
            vmem((payloads, turns[0], rows, width)),
            vmem((payloads, turns[1], rows, width)),
            dma((zp, nx)),
            dma((zp, nx)),
            dma(turns + (2,)),
            dma((turns[0],)),
            dma((turns[1],)),
            dma((zp, nx, NC)),
            dma((zp * nx * 6 + 8,)),
        ]
        + (
            [pltpu.VMEM(v.shape, bf16) for v in shared]
            + [pltpu.VMEM((tokens, hidden), bf16)] * 3
            + [dma((4,))]
            if small
            else []
        )
        + job_sems(grid, jobs),
        compiler_params=pltpu.CompilerParams(
            collective_id=number,
            has_side_effects=True,
            vmem_limit_bytes=56 * 2**20,
        ),
    )(*args)
    return made[:plain], made[plain:]


def project_kernel(rows_ref, wq_ref, wk_ref, wv_ref, q_ref, k_ref, v_ref):
    rows = rows_ref[...]
    q_ref[...] = times(rows[: q_ref.shape[0]], wq_ref[...]).astype(bf16)
    k_ref[...] = times(rows, wk_ref[...]).astype(bf16)
    v_ref[...] = times(rows, wv_ref[...]).astype(bf16)


def project(rows, weights, tokens):
    length, width = rows.shape
    strip = 256
    strips = width // strip
    block = pl.BlockSpec
    weight = lambda k: block((width, strip), lambda s: (0, k * strips + s))
    return pl.pallas_call(
        project_kernel,
        grid=(strips,),
        in_specs=[block((length, width), lambda s: (0, 0)), weight(0), weight(1), weight(2)],
        out_specs=[
            block((tokens, strip), lambda s: (0, s)),
            block((length, strip), lambda s: (0, s)),
            block((length, strip), lambda s: (0, s)),
        ],
        out_shape=[
            jax.ShapeDtypeStruct((n, width), bf16) for n in (tokens, length, length)
        ],
        compiler_params=pltpu.CompilerParams(vmem_limit_bytes=48 * 2**20),
        cost_estimate=pl.CostEstimate(
            flops=2 * (tokens + 2 * length) * width * width,
            bytes_accessed=6 * width * width + 6 * length * width,
            transcendentals=0,
        ),
    )(rows, weights, weights, weights)


def project_back_kernel(rows_ref, gq_ref, gvk_ref, w_ref, dq_ref, dk_ref, dv_ref, back_ref):
    turned = rows_ref[...].T
    width = gq_ref.shape[1]
    total = None
    for k, (grad, out) in enumerate(
        ((gq_ref[...], dq_ref), (gvk_ref[1], dk_ref), (gvk_ref[0], dv_ref))
    ):
        out[...] = times(turned, grad).astype(bf16)
        part = times_transposed(grad, w_ref[:, k * width : (k + 1) * width])
        total = part if total is None else total + part
    back_ref[...] = total


def project_back(rows, gq, gvk, weights):
    tokens, width = gq.shape
    strip = 256
    block = pl.BlockSpec
    return pl.pallas_call(
        project_back_kernel,
        grid=(width // strip,),
        in_specs=[
            block((tokens, strip), lambda s: (0, s)),
            block((tokens, width), lambda s: (0, 0)),
            block((2, tokens, width), lambda s: (0, 0, 0)),
            block((strip, 3 * width), lambda s: (s, 0)),
        ],
        out_specs=[block((strip, width), lambda s: (s, 0))] * 3
        + [block((tokens, strip), lambda s: (0, s))],
        out_shape=[jax.ShapeDtypeStruct((width, width), bf16)] * 3
        + [jax.ShapeDtypeStruct((tokens, width), f32)],
        compiler_params=pltpu.CompilerParams(vmem_limit_bytes=48 * 2**20),
        cost_estimate=pl.CostEstimate(
            flops=12 * tokens * width * width,
            bytes_accessed=12 * width * width + 12 * tokens * width,
            transcendentals=0,
        ),
    )(rows, gq, gvk, weights)


def attention_kernel(q_ref, k_ref, v_ref, bias_ref, out_ref):
    scores = times_transposed(q_ref[...], k_ref[...]) * HD ** (-0.5) + bias_ref[...]
    weights = jnp.exp(scores - jnp.max(scores, axis=1, keepdims=True))
    probs = weights * (1.0 / jnp.sum(weights, axis=1, keepdims=True))
    out_ref[...] = times(probs.astype(bf16), v_ref[...]).astype(bf16)


def attention_forward(queries, keys, values, bias):
    rows, width = queries.shape
    length = keys.shape[0]
    by_head = lambda n: pl.BlockSpec((n, HD), lambda h: (0, h))
    return pl.pallas_call(
        attention_kernel,
        grid=(width // HD,),
        out_shape=jax.ShapeDtypeStruct((rows, width), bf16),
        in_specs=[
            by_head(rows),
            by_head(length),
            by_head(length),
            pl.BlockSpec((rows, length), lambda h: (0, 0)),
        ],
        out_specs=by_head(rows),
        compiler_params=pltpu.CompilerParams(vmem_limit_bytes=40 * 2**20),
        cost_estimate=pl.CostEstimate(
            flops=4 * rows * length * width,
            bytes_accessed=4 * (rows + length) * width + 4 * rows * length,
            transcendentals=rows * length * width // HD,
        ),
    )(queries, keys, values, bias)


def attention_back_kernel(
    grid_of, jobs, q_ref, k_ref, v_ref, branch_ref, wo_ref, out_ref, bias_ref, *refs
):
    grid = grid_of()
    count = len(jobs)
    dq_ref, parts_ref, dwo_ref = refs[count : count + 3]
    job_send, job_recv = refs[-2:]
    each = functools.partial(
        each_job, grid, jobs, refs[:count], refs[count + 3 : -2], job_send, job_recv
    )
    if jobs:

        @pl.when(pl.program_id(0) == 0)
        def _():
            greet(job_targets(grid, jobs))
            each(lambda copy: copy.start())

    q, k, branch = q_ref[...], k_ref[...], branch_ref[...]
    g = times_transposed(branch, wo_ref[...]).astype(bf16)
    dwo_ref[...] = times(out_ref[...].T, branch).astype(bf16)
    scores = times_transposed(k, q) * HD ** (-0.5) + bias_ref[...]
    weights = jnp.exp(scores - jnp.max(scores, axis=0, keepdims=True))
    probs = weights * (1.0 / jnp.sum(weights, axis=0, keepdims=True))
    prob_grad = times_transposed(v_ref[...], g)
    centre = jnp.sum(probs * prob_grad, axis=0, keepdims=True)
    score_grad = (probs * (prob_grad - centre)).astype(bf16)
    parts_ref[0] = times(probs.astype(bf16), g).astype(bf16)
    parts_ref[1] = (times(score_grad, q) * HD ** (-0.5)).astype(bf16)
    dq_ref[...] = (contract_rows(score_grad, k) * HD ** (-0.5)).astype(bf16)
    if jobs:

        @pl.when(pl.program_id(0) == pl.num_programs(0) - 1)
        def _():
            each(lambda copy: copy.wait())


def attention_backward(
    grid_of, number, queries, keys, values, branch, weights, attended, bias, jobs, job_arrays
):
    grid = grid_of()
    rows, width = queries.shape
    length = keys.shape[0]
    by_head = lambda n: pl.BlockSpec((n, HD), lambda h: (0, h))
    whole = lambda *shape: pl.BlockSpec(shape, lambda h: (0, 0))
    anywhere = pl.BlockSpec(memory_space=pl.ANY)
    made = pl.pallas_call(
        functools.partial(attention_back_kernel, grid_of, jobs),
        grid=(width // HD,),
        out_shape=tuple(
            [
                jax.ShapeDtypeStruct((rows, width), bf16),
                jax.ShapeDtypeStruct((2, length, width), bf16),
                jax.ShapeDtypeStruct((width, width), bf16),
            ]
            + job_shapes(grid, jobs, job_arrays)
        ),
        in_specs=[
            by_head(rows),
            by_head(length),
            by_head(length),
            whole(rows, width),
            pl.BlockSpec((HD, width), lambda h: (h, 3)),
            by_head(rows),
            whole(length, rows),
        ]
        + [anywhere] * len(jobs),
        out_specs=(
            by_head(rows),
            pl.BlockSpec((2, length, HD), lambda h: (0, 0, h)),
            pl.BlockSpec((HD, width), lambda h: (h, 0)),
        )
        + (anywhere,) * len(jobs),
        scratch_shapes=job_sems(grid, jobs),
        compiler_params=pltpu.CompilerParams(
            vmem_limit_bytes=40 * 2**20,
            **(dict(collective_id=number, has_side_effects=True) if jobs else {}),
        ),
        cost_estimate=pl.CostEstimate(
            flops=10 * rows * length * width + 4 * rows * width * width,
            bytes_accessed=8 * rows * width + 8 * length * width + 4 * rows * length,
            transcendentals=rows * length * width // HD,
        ),
    )(queries, keys, values, branch, weights, attended, bias, *job_arrays)
    return made[0], made[1], made[2], made[3:]


ROW_SOURCES = 2


def expert_kernel(grid_of, capacity, steps, jobs, carry, *refs):
    grid = grid_of()
    count = len(jobs)
    take = lambda n: (refs[:n], refs[n:])
    (rows_ref, cot_ref, rank_row_ref, rank_col_ref, gate_ref, wg_ref, wu_ref, wd_ref), refs = take(8)
    before, refs = take(1 if carry else 0)
    job_ins, refs = take(count)
    (parts_ref, prob_ref, dg_ref, du_ref, dd_ref), refs = take(5)
    job_outs, refs = take(count)
    (x_keep, s_keep, c_keep, h_keep, ag_keep, au_keep, ht_keep), refs = take(7)
    each = functools.partial(each_job, grid, jobs, job_ins, job_outs, *refs)
    step = pl.program_id(0)
    width, hidden = x_keep.shape[1], h_keep.shape[1]
    tokens = rows_ref.shape[1]
    size = ROW_SOURCES * capacity
    strip = 256
    if jobs:

        @pl.when(step == 0)
        def _():
            greet(job_targets(grid, jobs))
            each(lambda copy: copy.start())

    @pl.when(step < steps)
    def _():
        at = pl.ds(pl.multiple_of(step * size, 32), size)
        picks, columns, gates = [], [], []
        for s in range(ROW_SOURCES):
            slots = lax.broadcasted_iota(jnp.int32, (capacity, tokens), 0)
            hit = slots == rank_row_ref[s]
            gate = jnp.sum(jnp.where(hit, gate_ref[s], 0.0), axis=1, keepdims=True)
            pick = hit.astype(f32).astype(bf16)
            picks.append(hit)
            gates.append(gate)
            across = lax.broadcasted_iota(jnp.int32, (tokens, capacity), 1)
            columns.append((across == rank_col_ref[s]).astype(f32).astype(bf16))
            to = pl.ds(pl.multiple_of(step * size + s * capacity, 16), capacity)
            x_keep[to] = times(pick, rows_ref[s]).astype(bf16)
            cot = times(pick, cot_ref[s])
            c_keep[pl.ds(s * capacity, capacity)] = cot.astype(bf16)
            s_keep[to] = (gate * cot).astype(bf16)
        x, slot = x_keep[at], s_keep[at]
        for low in range(0, hidden, strip):
            cut = slice(low, min(low + strip, hidden))
            gate_act = times(x, wg_ref[0, :, cut])
            up_act = times(x, wu_ref[0, :, cut])
            hidden_grad = times_transposed(slot, wd_ref[0, cut])
            activated, slope = silu_parts(gate_act)
            h_keep[at, cut] = (activated * up_act).astype(bf16)
            ag_keep[at, cut] = (hidden_grad * up_act * slope).astype(bf16)
            au_keep[at, cut] = (hidden_grad * activated).astype(bf16)
        h, ag, au = h_keep[at], ag_keep[at], au_keep[at]
        probs = jnp.zeros((size, 1), f32)
        for low in range(0, width, strip):
            cut = slice(low, low + strip)
            made = times(h, wd_ref[0, :, cut]).astype(bf16).astype(f32)
            probs += jnp.sum(made * c_keep[:, cut].astype(f32), axis=1, keepdims=True)
            back = (
                times_transposed(ag, wg_ref[0, cut]) + times_transposed(au, wu_ref[0, cut])
            ).astype(bf16)
            for s in range(ROW_SOURCES):
                mine = slice(s * capacity, (s + 1) * capacity)
                row = times(columns[s], back[mine])
                out = times(columns[s], (gates[s] * made[mine]).astype(bf16))
                if carry:
                    row += before[0][0, s, :, cut].astype(f32)
                    out += before[0][1, s, :, cut].astype(f32)
                parts_ref[0, s, :, cut] = row.astype(bf16)
                parts_ref[1, s, :, cut] = out.astype(bf16)
        for s in range(ROW_SOURCES):
            mine = slice(s * capacity, (s + 1) * capacity)
            prob_ref[s] = jnp.sum(
                jnp.where(picks[s], probs[mine], 0.0), axis=0, keepdims=True
            )

    @pl.when(step == steps)
    def _():
        ht_keep[...] = h_keep[...].T

    @pl.when(step >= steps)
    def _():
        cut = pl.ds(pl.multiple_of((step - steps) * strip, strip), strip)
        turned = x_keep[:, cut].T
        dg_ref[...] = times(turned, ag_keep[...]).astype(bf16)
        du_ref[...] = times(turned, au_keep[...]).astype(bf16)
        dd_ref[...] = times(ht_keep[...], s_keep[:, cut]).astype(bf16)

    if jobs:

        @pl.when(step == pl.num_programs(0) - 1)
        def _():
            each(lambda copy: copy.wait())


def run_expert(grid_of, number, expert, rows, cot, ranks, gates, weights, capacity, before, jobs, job_arrays):
    grid = grid_of()
    sources, tokens = ranks.shape
    width, hidden = weights[0].shape[1:]
    mine = weights[0].shape[0] // ZP
    steps = sources // ROW_SOURCES
    strip = 256
    strips = width // strip
    total = sources * capacity
    turn = lambda s: jnp.minimum(s, steps - 1)
    later = lambda s: jnp.maximum(s - steps, 0)
    block = pl.BlockSpec
    by_source = lambda *rest: block(
        (ROW_SOURCES,) + rest, lambda s: (turn(s),) + (0,) * len(rest)
    )
    held = lambda *rest: block(
        (1,) + rest,
        lambda s: (lax.axis_index("wide") // grid.ny % ZP * mine + expert, 0, 0),
    )
    parts = block((2, ROW_SOURCES, tokens, width), lambda s: (0, turn(s), 0, 0))
    anywhere = block(memory_space=pl.ANY)
    carry = before is not None
    made = pl.pallas_call(
        functools.partial(expert_kernel, grid_of, capacity, steps, jobs, carry),
        grid=(steps + strips,),
        in_specs=[
            by_source(tokens, width),
            by_source(tokens, width),
            by_source(1, tokens),
            by_source(tokens, 1),
            by_source(1, tokens),
            held(width, hidden),
            held(width, hidden),
            held(hidden, width),
        ]
        + [parts] * carry
        + [anywhere] * len(jobs),
        out_specs=[
            parts,
            by_source(1, tokens),
            block((strip, hidden), lambda s: (later(s), 0)),
            block((strip, hidden), lambda s: (later(s), 0)),
            block((hidden, strip), lambda s: (0, later(s))),
        ]
        + [anywhere] * len(jobs),
        scratch_shapes=[
            pltpu.VMEM((total, width), bf16),
            pltpu.VMEM((total, width), bf16),
            pltpu.VMEM((ROW_SOURCES * capacity, width), bf16),
            pltpu.VMEM((total, hidden), bf16),
            pltpu.VMEM((total, hidden), bf16),
            pltpu.VMEM((total, hidden), bf16),
            pltpu.VMEM((hidden, total), bf16),
        ]
        + job_sems(grid, jobs),
        out_shape=[
            jax.ShapeDtypeStruct((2, sources, tokens, width), bf16),
            jax.ShapeDtypeStruct((sources, 1, tokens), f32),
            jax.ShapeDtypeStruct((width, hidden), bf16),
            jax.ShapeDtypeStruct((width, hidden), bf16),
            jax.ShapeDtypeStruct((hidden, width), bf16),
        ]
        + job_shapes(grid, jobs, job_arrays),
        compiler_params=pltpu.CompilerParams(
            vmem_limit_bytes=58 * 2**20,
            **(dict(collective_id=number, has_side_effects=True) if jobs else {}),
        ),
        cost_estimate=pl.CostEstimate(
            flops=total * width * hidden * 18,
            bytes_accessed=width * hidden * 12 + 16 * sources * tokens * width,
            transcendentals=total * hidden,
        ),
    )(
        rows,
        cot,
        ranks[:, None, :],
        ranks[:, :, None],
        gates[:, None, :],
        *weights,
        *([before] if carry else []),
        *job_arrays,
    )
    return made[:5], made[5:]


def jobs_count(grid, jobs):
    return sum({"y": grid.ny, "z": NZ}[axis] - 1 for axis in jobs)


def job_targets(grid, jobs):
    axes = set(jobs)
    place = lambda z, y: (z * grid.ny + y, grid.x * NC + grid.c)
    made = []
    if "y" in axes:
        made += [place(grid.z, (grid.y + d) % grid.ny) for d in range(1, grid.ny)]
    if "z" in axes:
        made += [place((grid.z + d) % NZ, grid.y) for d in range(1, NZ)]
    return made


def each_job(grid, jobs, ins, outs, send_sem, recv_sem, act):
    at = 0
    for axis, src, out in zip(jobs, ins, outs):
        for d in range(1, {"y": grid.ny, "z": NZ}[axis]):
            if axis == "y":
                to = (grid.y + d) % grid.ny
                piece, target = src.at[:, to], (grid.z * grid.ny + to)
            else:
                to = (grid.z + d) % NZ
                piece, target = src.at[to], (to * grid.ny + grid.y)
            act(
                pltpu.make_async_remote_copy(
                    src_ref=piece,
                    dst_ref=out.at[d - 1],
                    send_sem=send_sem.at[at],
                    recv_sem=recv_sem.at[at],
                    device_id=(target, grid.x * NC + grid.c),
                    device_id_type=pl.DeviceIdType.MESH,
                )
            )
            at += 1


def job_shapes(grid, jobs, arrays):
    made = []
    for axis, v in zip(jobs, arrays):
        shape = (grid.ny - 1, NZ) + v.shape[2:] if axis == "y" else (NZ - 1,) + v.shape[1:]
        made.append(jax.ShapeDtypeStruct(shape, v.dtype))
    return made


def job_sems(grid, jobs):
    count = max(jobs_count(grid, jobs), 1)
    return [pltpu.SemaphoreType.DMA((count,)), pltpu.SemaphoreType.DMA((count,))]


def dense_kernel(grid_of, orders, jobs, items, *refs):
    grid = grid_of()
    z, y, x, c, nx, ny = grid.z, grid.y, grid.x, grid.c, grid.nx, grid.ny
    count, more = len(orders), len(jobs)
    wholes = items[-1][0] + 1
    take = lambda n: (refs[:n], refs[n:])
    ins, refs = take(wholes)
    job_ins, refs = take(more)
    outs, refs = take(wholes)
    job_outs, refs = take(more)
    strip = lambda v, low, wide: v.at[(slice(None),) * (len(v.shape) - 1) + (pl.ds(low, wide),)]
    ins = [strip(ins[k], low, wide) for k, low, wide in items]
    outs = [strip(outs[k], low, wide) for k, low, wide in items]
    held, refs = take(count)
    got_c, refs = take(count)
    got_one, refs = take(count)
    got_two, refs = take(count)
    got_z, refs = take(count)
    local_sem, c_sem, one_sem, two_sem, z_sem, out_sem, send_sem, job_send, job_recv = refs
    device = lambda tz, ty, tx, tc: (tz * ny + ty, tx * NC + tc)
    other = (c + 1) % NC
    greet(
        [device(z, y, x, other)]
        + [device(z, y, (x + d) % nx, c) for d in range(1, nx)]
        + [device(z, (y + d) % ny, x, c) for d in range(1, ny)]
        + [device((z + d) % NZ, y, x, c) for d in range(1, NZ)]
    )
    send = Sender(send_sem)
    loads = []

    def begin(k):
        send(ins[k].at[:, :, :, other], got_c[k], c_sem.at[k], device(z, y, x, other))
        load = pltpu.make_async_copy(ins[k].at[:, :, :, c], held[k], local_sem.at[k])
        load.start()
        loads.append(load)

    for k in range(min(3, count)):
        begin(k)
    each_job(grid, jobs, job_ins, job_outs, job_send, job_recv, lambda copy: copy.start())

    def add(dst, src):
        lead = dst.shape[:-2]
        total = 1
        for n in lead:
            total *= n

        @pl.loop(0, total)
        def _(i):
            index = []
            for n in reversed(lead):
                index.insert(0, i % n)
                i = i // n
            index = tuple(index)
            dst[index] = (dst[index].astype(f32) + src[index].astype(f32)).astype(dst.dtype)

    def first(k):
        if k + 3 < count:
            begin(k + 3)
        loads[k].wait()
        arrived(got_c[k], c_sem.at[k])
        add(held[k], got_c[k])
        if orders[k] == "xy":
            for d in range(1, nx):
                to = (x + d) % nx
                send(held[k].at[:, :, to], got_one[k].at[d - 1], one_sem.at[k, d - 1], device(z, y, to, c))
        else:
            for d in range(1, ny):
                to = (y + d) % ny
                send(held[k].at[:, to], got_one[k].at[d - 1], one_sem.at[k, d - 1], device(z, to, x, c))

    def second(k):
        mine = held[k].at[:, :, x] if orders[k] == "xy" else held[k].at[:, y]
        for d in range(1, nx if orders[k] == "xy" else ny):
            arrived(got_one[k].at[d - 1], one_sem.at[k, d - 1])
            add(mine, got_one[k].at[d - 1])
        if orders[k] == "xy":
            for d in range(1, ny):
                to = (y + d) % ny
                send(held[k].at[:, to, x], got_two[k].at[d - 1], two_sem.at[k, d - 1], device(z, to, x, c))
        else:
            for d in range(1, nx):
                to = (x + d) % nx
                send(held[k].at[:, y, to], got_two[k].at[d - 1], two_sem.at[k, d - 1], device(z, y, to, c))

    results = []

    def third(k):
        mine = held[k].at[:, y, x]
        for d in range(1, ny if orders[k] == "xy" else nx):
            arrived(got_two[k].at[d - 1], two_sem.at[k, d - 1])
            add(mine, got_two[k].at[d - 1])
        near = z // ZP * ZP + (z + 1) % ZP
        for n in range(NZ // ZP):
            to = (z + 1) % ZP + n * ZP
            send(held[k].at[to, y, x], got_z[k].at[n], z_sem.at[k, n], device(near, y, x, c))

    def fourth(k):
        for n in range(NZ // ZP):
            arrived(got_z[k].at[n], z_sem.at[k, n])
            at = (z % ZP + n * ZP, y, x)
            held[k][at] = (held[k][at].astype(f32) + got_z[k][n].astype(f32)).astype(held[k].dtype)
        for n in range(1, NZ // ZP):
            to = (z + n * ZP) % NZ
            send(held[k].at[to, y, x], outs[k].at[n], z_sem.at[k, NZ // ZP + n - 1], device(to, y, x, c))
        result = pltpu.make_async_copy(held[k].at[z, y, x], outs[k].at[0], out_sem.at[k])
        result.start()
        results.append(result)

    for t in range(count + 6):
        for stage, late in ((first, 0), (second, 2), (third, 4), (fourth, 6)):
            if 0 <= t - late < count:
                stage(t - late)
    for k in range(count):
        for n in range(1, NZ // ZP):
            arrived(outs[k].at[n], z_sem.at[k, NZ // ZP + n - 1])
        results[k].wait()
    each_job(grid, jobs, job_ins, job_outs, job_send, job_recv, lambda copy: copy.wait())
    send.finish()


def reduce_dense(grid_of, number, arrays, jobs, job_arrays):
    grid = grid_of()
    nx, ny = grid.nx, grid.ny
    items = []
    for k, v in enumerate(arrays):
        wide = v.shape[5]
        low = wide // 2 if wide % 256 == 0 else wide
        items += [(k, at, low) for at in range(0, wide, low)]
    orders = ["xy" if n % 2 == 0 else "yx" for n in range(len(items))]
    count = len(items)
    anywhere = pl.BlockSpec(memory_space=pl.ANY)
    dma = pltpu.SemaphoreType.DMA
    block = [(arrays[k].shape[4], wide) for k, _, wide in items]
    kind = [arrays[k].dtype for k, _, _ in items]
    far = max(nx, ny)
    held = [pltpu.VMEM((NZ, ny, nx) + b, t) for b, t in zip(block, kind)]
    one = [
        pltpu.VMEM((nx - 1, NZ, ny) + b if o == "xy" else (ny - 1, NZ, nx) + b, t)
        for b, t, o in zip(block, kind, orders)
    ]
    two = [
        pltpu.VMEM(((ny if o == "xy" else nx) - 1, NZ) + b, t)
        for b, t, o in zip(block, kind, orders)
    ]
    made = pl.pallas_call(
        functools.partial(dense_kernel, grid_of, orders, jobs, items),
        out_shape=tuple(
            [jax.ShapeDtypeStruct((NZ // ZP,) + v.shape[4:], v.dtype) for v in arrays]
            + job_shapes(grid, jobs, job_arrays)
        ),
        in_specs=[anywhere] * (len(arrays) + len(jobs)),
        out_specs=(anywhere,) * (len(arrays) + len(jobs)),
        scratch_shapes=held
        + held
        + one
        + two
        + [pltpu.VMEM((NZ // ZP,) + b, t) for b, t in zip(block, kind)]
        + [
            dma((count,)),
            dma((count,)),
            dma((count, far)),
            dma((count, far)),
            dma((count, NZ - 1)),
            dma((count,)),
            dma((count * (1 + nx + ny + NZ),)),
        ]
        + job_sems(grid, jobs),
        compiler_params=pltpu.CompilerParams(
            collective_id=number,
            has_side_effects=True,
            vmem_limit_bytes=60 * 2**20,
        ),
    )(*arrays, *job_arrays)
    return made[: len(arrays)], made[len(arrays) :]


def finish_kernel(grid_of, mine, dense, *refs):
    grid = grid_of()
    kinds = 3
    names = mine * kinds
    own, far = refs[:names], refs[names : 2 * names]
    terms = refs[2 * names : 2 * names + dense]
    outs = refs[2 * names + dense :]
    for n in range(names):
        i, kind = n // kinds, n % kinds
        sums = [own[n][0].astype(f32), None]
        for d in range(1, NZ):
            got = far[n][d - 1].astype(f32)
            sums[d % ZP] = got if sums[d % ZP] is None else sums[d % ZP] + got
        outs[kind][grid.zm, i] = sums[0]
        outs[kind][1 - grid.zm, i] = sums[1]
    for n in range(dense):
        total = terms[n][0].astype(f32)
        for d in range(1, terms[n].shape[0]):
            total = total + terms[n][d].astype(f32)
        outs[kinds + n][...] = total


def finish(grid_of, mine, columns, far, terms):
    grid = grid_of()
    whole = lambda v: pl.BlockSpec(v.shape, lambda _: (0,) * len(v.shape))
    out_shape = [
        jax.ShapeDtypeStruct((ZP, mine) + columns[k].shape[1:], f32) for k in range(3)
    ] + [jax.ShapeDtypeStruct(v.shape[1:], f32) for v in terms]
    return pl.pallas_call(
        functools.partial(finish_kernel, grid_of, mine, len(terms)),
        grid=(1,),
        out_shape=out_shape,
        in_specs=[
            pl.BlockSpec(
                (1,) + v.shape[1:],
                lambda _: (lax.axis_index("wide") // grid.ny, 0, 0),
            )
            for v in columns
        ]
        + [whole(v) for v in far]
        + [whole(v) for v in terms],
        out_specs=[whole(v) for v in out_shape],
        compiler_params=pltpu.CompilerParams(vmem_limit_bytes=62 * 2**20),
    )(*columns, *far, *terms)


def attention_bias(segment, labels_all, query_places, key_places):
    same_doc = segment[:, None] == labels_all[None, :]
    allowed = same_doc & (query_places[:, None] >= key_places[None, :])
    return jnp.where(allowed, 0.0, masked_value).astype(f32)


def body(
    wide,
    ep,
    activations,
    segment,
    routes,
    gain_attention,
    query_weight,
    key_weight,
    value_weight,
    output_weight,
    gain_experts,
    router_weight,
    shared_gate,
    shared_up,
    shared_down,
    expert_gate,
    expert_up,
    expert_down,
    cotangent,
):
    grid_of = functools.partial(Grid, wide, ep)
    grid = grid_of()
    nx, ny = grid.nx, grid.ny
    tok_rows, width = activations.shape
    heads = width // HD
    top_count = routes.shape[1]
    experts = router_weight.shape[1]
    local_experts = expert_gate.shape[0]
    mine = local_experts // ZP
    hidden_width = expert_gate.shape[2]
    sources = ZP * nx * NC
    capacity = min((tok_rows * top_count * 10 // (7 * experts) + 7) // 8 * 8, tok_rows)

    bundle = jnp.concatenate(
        [
            query_weight,
            key_weight,
            value_weight,
            output_weight,
            router_weight,
            gain_attention[:, None],
            gain_experts[:, None],
            jnp.zeros((gain_experts.shape[0], 128 - experts - 2), bf16),
        ],
        axis=1,
    )
    integers = jnp.concatenate([routes.T, segment[None, :]], axis=0)
    bundle_all, group_rows, cot_all, integers_all = gather_first(
        grid_of, bundle, activations, cotangent, integers
    )
    group_rows = group_rows.reshape(-1, width)
    integers_all = integers_all.reshape(sources, top_count + 1, tok_rows)
    bundle_all = bundle_all.reshape(width, bundle.shape[1])
    w_out = bundle_all[:, 3 * width : 4 * width]
    small_all = bundle_all[:, 4 * width :]
    gather_all = lambda v: lax.all_gather(v, BOTH, axis=0, tiled=True)
    shared_in, shared_out_in, integers_all = lax.optimization_barrier(
        (
            jnp.concatenate([shared_gate, shared_up], axis=1),
            shared_down,
            integers_all,
        )
    )
    s_both = gather_all(shared_in)
    s_down = gather_all(shared_out_in)
    w_router = small_all[:, :experts]
    gain_one = small_all[:, experts].astype(f32)
    gain_two = small_all[:, experts + 1].astype(f32)

    inputs = activations.astype(f32)
    inverse_one = norm_scale(inputs)
    group_inputs = group_rows.astype(f32)
    normed_group = (group_inputs * norm_scale(group_inputs) * gain_one).astype(bf16)
    normed_one = normed_group[:tok_rows]
    queries, keys_all, values_all = project(normed_group, bundle_all, tok_rows)
    labels_all = integers_all[: nx * NC, top_count].reshape(-1)
    steps = jnp.arange(tok_rows, dtype=jnp.int32)
    block_places = (
        (grid.x + jnp.arange(nx, dtype=jnp.int32)[:, None]) % nx * NC
        + (grid.c + jnp.arange(NC, dtype=jnp.int32)[None, :]) % NC
    ).reshape(-1)
    key_places = (block_places[:, None] * tok_rows + steps[None, :]).reshape(-1)
    query_places = (grid.x * NC + grid.c) * tok_rows + steps
    bias = attention_bias(segment, labels_all, query_places, key_places)
    attended = attention_forward(queries, keys_all, values_all, bias)
    middle = inputs + times(attended, w_out)
    inverse_two = norm_scale(middle)
    normed_two = (middle * inverse_two * gain_two).astype(bf16)

    rows_all = exchange(grid_of, ZP, 1, normed_two)
    rows_all = rows_all.reshape(sources, tok_rows, width)
    cot_all = cot_all.reshape(sources, tok_rows, width)
    router_probs_all = jax.nn.softmax(
        times(rows_all.reshape(-1, width), w_router).reshape(sources, tok_rows, experts),
        axis=-1,
    )
    router_probs = router_probs_all[0]
    first_expert = (grid.x * NC + grid.c) * local_experts + grid.zm * mine
    routes_all = integers_all[:, :top_count]
    numbers = first_expert + jnp.arange(mine, dtype=jnp.int32)
    marks = jnp.any(
        routes_all[None] == numbers[:, None, None, None], axis=2
    )
    earlier = (steps[:, None] < steps[None, :]).astype(bf16)
    ranks = jnp.einsum(
        "irt,tu->iru", marks.astype(bf16), earlier, preferred_element_type=f32
    ).astype(jnp.int32)
    ranks = jnp.where(marks, ranks, -1)
    gates_mine = jnp.moveaxis(
        lax.dynamic_slice_in_dim(router_probs_all, first_expert, mine, axis=2), 2, 0
    )
    def by_wide(v):
        return v.reshape(NZ, ny, v.shape[0] // wide, v.shape[1])

    names = [(i, k) for i in range(mine) for k in range(3)]
    grads, along_y, along_z = {}, {}, {}

    def jobs_of(which_y, which_z):
        tags = tuple("y" for _ in which_y) + tuple("z" for _ in which_z)
        return tags, [grads[n] for n in which_y] + [column[n] for n in which_z]

    def landed(which_y, which_z, moved):
        along_y.update(zip(which_y, moved))
        along_z.update(zip(which_z, moved[len(which_y) :]))

    def summed(name):
        total = lax.dynamic_index_in_dim(grads[name], grid.y, 1, keepdims=False).astype(f32)
        for d in range(ny - 1):
            total = total + along_y[name][d].astype(f32)
        return total.astype(bf16)

    column = {}
    both_parts = None
    prob_parts = []
    for i in range(mine):
        behind = (names[:1], []) if i else ([], [])
        (both_parts, probs_here, *made), moved = run_expert(
            grid_of,
            5 + i,
            i,
            rows_all,
            cot_all,
            ranks[i],
            gates_mine[i],
            (expert_gate, expert_up, expert_down),
            capacity,
            both_parts,
            *jobs_of(*behind),
        )
        landed(*behind, moved)
        prob_parts.append(probs_here[:, 0])
        grads.update({(i, k): by_wide(v) for k, v in enumerate(made)})
    column.update({name: summed(name) for name in along_y})
    behind = (names[1:3], names[:1])
    (
        sums,
        sent,
        shared_out,
        shared_back,
        shared_gate_grad,
        shared_up_grad,
        shared_down_grad,
    ), moved = sum_around(
        grid_of,
        ZP,
        2,
        both_parts.reshape(2, ZP, nx, NC, tok_rows, width),
        jnp.stack(prob_parts, axis=1).reshape(ZP, nx, NC, mine, tok_rows),
        (normed_two, cotangent, s_both, s_down),
        *jobs_of(*behind),
    )
    landed(*behind, moved)
    column.update({name: summed(name) for name in behind[0]})
    routed_grad = sums[0].astype(f32)
    routed = sums[1].astype(f32)
    dz = (grid.zm + jnp.arange(ZP, dtype=jnp.int32)) % ZP
    owner = block_places.reshape(1, nx, NC, 1) * local_experts
    owner = owner + dz[:, None, None, None] * mine + jnp.arange(mine, dtype=jnp.int32)
    same = owner.reshape(-1)[None, :] == jnp.arange(experts, dtype=jnp.int32)[:, None]
    prob_grad = jnp.sum(
        jnp.where(same[:, :, None], sent.reshape(1, experts, tok_rows), 0.0), axis=1
    ).T

    out_grad = cotangent.astype(f32)
    block_out = (middle + shared_out + routed).astype(bf16)

    logit_grad = router_probs * (
        prob_grad - jnp.sum(router_probs * prob_grad, axis=-1, keepdims=True)
    )
    router_grad = lax.dot_general(
        normed_two.astype(f32),
        logit_grad,
        (((0,), (0,)), ((), ())),
        precision=lax.Precision.HIGHEST,
        preferred_element_type=f32,
    )
    normed_two_grad = (
        shared_back
        + routed_grad
        + lax.dot_general(
            logit_grad,
            w_router.astype(f32),
            (((1,), (1,)), ((), ())),
            precision=lax.Precision.HIGHEST,
            preferred_element_type=f32,
        )
    )
    gain_two_grad, middle_part = norm_backward(
        middle, inverse_two, gain_two, normed_two_grad
    )
    middle_grad = out_grad + middle_part
    branch_grad = middle_grad.astype(bf16)

    behind = (names[3:4], names[1:2])
    query_act_grad, parts, output_weight_grad, moved = attention_backward(
        grid_of,
        1 + 8,
        queries,
        keys_all,
        values_all,
        branch_grad,
        bundle_all,
        attended,
        bias.T,
        *jobs_of(*behind),
    )
    landed(*behind, moved)
    behind = (names[4:], names[2:4])
    column.update({name: summed(name) for name in names[3:4]})
    ((value_key,), moved) = sum_around(
        grid_of,
        1,
        3,
        parts.reshape(2, 1, nx, NC, tok_rows, width),
        None,
        (),
        *jobs_of(*behind),
    )
    landed(*behind, moved)
    column.update({name: summed(name) for name in names[4:]})
    query_w_grad, key_w_grad, value_w_grad, normed_one_grad = project_back(
        normed_group, query_act_grad, value_key, bundle_all
    )
    gain_one_grad, input_part = norm_backward(
        inputs, inverse_one, gain_one, normed_one_grad
    )
    input_grad = middle_grad + input_part

    def by_place(v):
        return v.reshape((NZ, ny, nx, NC, v.shape[0] // (wide * ep)) + v.shape[1:])

    counts = jnp.sum(
        (routes[:, :, None] == jnp.arange(experts, dtype=jnp.int32)).astype(f32),
        axis=(0, 1),
    )
    share = gain_attention.shape[0]
    count_block = jnp.pad(
        jnp.tile(counts.reshape(1, ep, 1, local_experts), (wide, 1, 1, 1)),
        ((0, 0), (0, 0), (0, 0), (0, 128 - local_experts)),
    )
    extras = jnp.concatenate(
        [
            router_grad,
            gain_one_grad[:, None],
            gain_two_grad[:, None],
            jnp.zeros((width, 128 - experts - 2), f32),
        ],
        axis=1,
    ).reshape(wide, ep, share, 128)
    extras = jnp.concatenate(
        [extras, count_block, jnp.zeros((wide, ep, 7, 128), f32)], axis=2
    )
    dense = [
        output_weight_grad,
        shared_down_grad,
        shared_gate_grad,
        shared_up_grad,
        query_w_grad,
        key_w_grad,
        value_w_grad,
    ]
    terms, moved = reduce_dense(
        grid_of,
        4,
        [by_place(v.astype(bf16)) for v in dense]
        + [extras.reshape(NZ, ny, nx, NC, share + 8, 128)],
        *jobs_of([], names[4:]),
    )
    landed([], names[4:], moved)
    (
        expert_gate_grad,
        expert_up_grad,
        expert_down_grad,
        output_weight_sum,
        shared_down_sum,
        shared_gate_sum,
        shared_up_sum,
        query_sum,
        key_sum,
        value_sum,
        extra_sum,
    ) = finish(
        grid_of, mine, [column[n] for n in names], [along_z[n] for n in names], terms
    )
    expert_gate_grad, expert_up_grad, expert_down_grad = (
        v.reshape((local_experts,) + v.shape[2:])
        for v in (expert_gate_grad, expert_up_grad, expert_down_grad)
    )
    return (
        block_out,
        input_grad,
        extra_sum[:share, experts],
        query_sum,
        key_sum,
        value_sum,
        output_weight_sum,
        extra_sum[:share, experts + 1],
        extra_sum[:share, :experts],
        shared_gate_sum,
        shared_up_sum,
        shared_down_sum,
        expert_gate_grad,
        expert_up_grad,
        expert_down_grad,
        extra_sum[share, :local_experts].astype(jnp.int32),
    )


def solution(mesh):
    split = P(BOTH, None)
    line = P(BOTH)
    held = P("ep", None, None)
    out_held = P("ep", "wide", None)
    in_specs = (
        (split, line, split, line)
        + (split,) * 4
        + (line,)
        + (split,) * 4
        + (held,) * 3
        + (split,)
    )
    out_specs = (
        (split, split, line)
        + (split,) * 4
        + (line,)
        + (split,) * 4
        + (out_held,) * 3
        + (P("ep"),)
    )
    return jax.shard_map(
        functools.partial(body, mesh.shape["wide"], mesh.shape["ep"]),
        mesh=mesh,
        in_specs=in_specs,
        out_specs=out_specs,
        check_vma=False,
    )
```

```python
import functools

import jax
import jax.numpy as jnp
from jax import lax
from jax.experimental import pallas as pl
from jax.experimental.pallas import tpu as pltpu
from jax.sharding import PartitionSpec as P

HD = 128
NC = 2
NZ = 4
ZP = 2
epsilon = 1e-06
masked_value = -1e30
BOTH = ("wide", "ep")
f32 = jnp.float32
bf16 = jnp.bfloat16


def contract_rows(left, right):
    return lax.dot_general(
        left, right, (((0,), (0,)), ((), ())), preferred_element_type=f32
    )


def times_transposed(left, right):
    return lax.dot_general(
        left, right, (((1,), (1,)), ((), ())), preferred_element_type=f32
    )


def times(left, right):
    return jnp.dot(left, right, preferred_element_type=f32)


def norm_scale(values):
    return lax.rsqrt(jnp.mean(values * values, axis=-1, keepdims=True) + epsilon)


def norm_backward(values, inverse, gain, normed_grad):
    weighted = normed_grad * gain
    gain_grad = jnp.sum(normed_grad * values * inverse, axis=0)
    cubed = inverse * inverse * inverse
    values_grad = inverse * weighted - values * cubed * jnp.mean(
        weighted * values, axis=-1, keepdims=True
    )
    return (gain_grad, values_grad)


def silu_parts(gate_act):
    logistic = 0.5 * jnp.tanh(0.5 * gate_act) + 0.5
    return (gate_act * logistic, logistic * (1.0 + gate_act * (1.0 - logistic)))


class Grid:
    def __init__(self, wide, ep):
        self.ny, self.nx, self.ep = wide // NZ, ep // NC, ep
        w, e = lax.axis_index("wide"), lax.axis_index("ep")
        self.z, self.y, self.x, self.c = w // self.ny, w % self.ny, e // NC, e % NC
        self.zm = self.z % ZP

    def pairs(self, move):
        made = []
        for z in range(NZ):
            for y in range(self.ny):
                for x in range(self.nx):
                    for c in range(NC):
                        tz, ty, tx, tc = move(z, y, x, c)
                        made.append(
                            (
                                (z * self.ny + y) * self.ep + x * NC + c,
                                (tz * self.ny + ty) * self.ep + tx * NC + tc,
                            )
                        )
        return made

    def send(self, value, axis, step):
        moves = {
            "c": lambda z, y, x, c: (z, y, x, (c + step) % NC),
            "x": lambda z, y, x, c: (z, y, (x + step) % self.nx, c),
            "y": lambda z, y, x, c: (z, (y + step) % self.ny, x, c),
            "z": lambda z, y, x, c: ((z + step) % NZ, y, x, c),
            "p": lambda z, y, x, c: (z // ZP * ZP + (z % ZP + step) % ZP, y, x, c),
        }
        return lax.ppermute(value, BOTH, self.pairs(moves[axis]))

    def size(self, axis):
        return {"c": NC, "x": self.nx, "y": self.ny, "z": NZ, "p": ZP}[axis]

    def place(self, axis):
        return {"c": self.c, "x": self.x, "y": self.y, "z": self.z, "p": self.zm}[axis]

    def gather(self, value, axis, at):
        parts = [value] + [
            self.send(value, axis, -d) for d in range(1, self.size(axis))
        ]
        return jnp.stack(parts, axis=at)

    def scatter(self, value, axis, at):
        total = lax.index_in_dim(value, 0, at, keepdims=False).astype(f32)
        for d in range(1, self.size(axis)):
            part = lax.index_in_dim(value, d, at, keepdims=False)
            total = total + self.send(part, axis, d).astype(f32)
        return total.astype(value.dtype)

    def scatter_absolute(self, value, axis, at):
        n, me = self.size(axis), self.place(axis)
        take = lambda i: lax.dynamic_index_in_dim(value, i, at, keepdims=False)
        total = take(me).astype(f32)
        for d in range(1, n):
            total = total + self.send(take((me + d) % n), axis, d).astype(f32)
        return total.astype(value.dtype)


class Sender:
    def __init__(self, sems):
        self.sems, self.started = sems, []

    def __call__(self, src, dst, sem, target):
        copy = pltpu.make_async_remote_copy(
            src_ref=src,
            dst_ref=dst,
            send_sem=self.sems.at[len(self.started)],
            recv_sem=sem,
            device_id=target,
            device_id_type=pl.DeviceIdType.MESH,
        )
        copy.start()
        self.started.append(copy)

    def finish(self):
        for copy in self.started:
            copy.wait_send()


def arrived(dst, sem):
    pltpu.make_async_copy(dst, dst, sem).wait()


def greet(targets):
    barrier = pltpu.get_barrier_semaphore()
    for target in targets:
        pl.semaphore_signal(
            barrier, inc=1, device_id=target, device_id_type=pl.DeviceIdType.MESH
        )
    pl.semaphore_wait(barrier, len(targets))


def around(grid, zp):
    steps = [(a, b, e) for a in range(zp) for b in range(grid.nx) for e in range(NC)]
    return steps[1:]


def stepped(grid, zp, a, b, e):
    z = grid.z // zp * zp + (grid.z % zp + a) % zp
    return (
        z * grid.ny + grid.y,
        (grid.x + b) % grid.nx * NC + (grid.c + e) % NC,
    )


def gather_kernel(
    grid_of,
    wq_ref,
    wk_ref,
    wv_ref,
    wo_ref,
    rest_ref,
    rows_ref,
    cot_ref,
    ints_ref,
    w_all,
    rows_all,
    cot_all,
    ints_all,
    plane_sem,
    core_sem,
    rows_sem,
    cot_sem,
    ints_sem,
    send_sem,
    local_sem,
    z_in,
    z_out,
    x_out,
    y_out,
    c_out,
    piece_sem,
):
    grid = grid_of()
    z, y, x, c, nx, ny = grid.z, grid.y, grid.x, grid.c, grid.nx, grid.ny

    def device(tz, ty, tx, tc):
        return (tz * ny + ty, tx * NC + tc)

    def block(dz, dy, dx, tc):
        place = (z + NZ - dz) % NZ * ny + (y + ny - dy) % ny
        return w_all.at[place * (nx * NC) + (x + nx - dx) % nx * NC + tc]

    shift_z = lambda d: (z + d) % NZ
    shift_y = lambda d: (y + d) % ny
    shift_x = lambda d: (x + d) % nx
    back = lambda d: (nx - d) % nx
    other = (c + 1) % NC
    to = functools.partial(stepped, grid, ZP)
    mine = block(0, 0, 0, c)
    pieces, low = [], 0
    for n, piece in enumerate((wq_ref, wk_ref, wv_ref, wo_ref, rest_ref)):
        wide = piece.shape[1]
        pieces.append(
            pltpu.make_async_copy(piece, mine.at[:, pl.ds(low, wide)], piece_sem.at[n])
        )
        low += wide
    for copy in pieces:
        copy.start()
    greet(
        [device(shift_z(d), y, x, c) for d in range(1, NZ)]
        + [device(z, shift_y(d), x, c) for d in range(1, ny)]
        + [to(*s) for s in around(grid, ZP)]
    )
    send = Sender(send_sem)
    locals_ = [
        (rows_ref, rows_all.at[0, 0]),
        (cot_ref, cot_all.at[0, 0, 0]),
        (ints_ref, ints_all.at[0, 0, 0]),
    ]
    locals_ = [
        pltpu.make_async_copy(src, dst, local_sem.at[k])
        for k, (src, dst) in enumerate(locals_)
    ]
    for copy in locals_:
        copy.start()
    for copy in pieces:
        copy.wait()
    def start(src, dst, out_sem, in_sem, target):
        pltpu.make_async_remote_copy(
            src_ref=src,
            dst_ref=dst,
            send_sem=out_sem,
            recv_sem=in_sem,
            device_id=target,
            device_id_type=pl.DeviceIdType.MESH,
        ).start()

    def each_source(act, least=0, most=NZ - 1):
        for d in range(least, most + 1):
            for way in range(2):
                there = z - d >= 0 if way == 0 else z + d <= NZ - 1
                pl.when(there)(
                    functools.partial(act, way, d, d if way == 0 else (NZ - d) % NZ)
                )

    def pass_on(way, d, dz):
        here = block(dz, 0, 0, c)
        src = here
        if d:
            arrived(here, z_in.at[way, d])
        if d < NZ - 1:

            @pl.when(z < NZ - 1 if way == 0 else z > 0)
            def _():
                start(
                    src,
                    here,
                    z_out.at[way, d],
                    z_in.at[way, d + 1],
                    device(z + 1 if way == 0 else z - 1, y, x, c),
                )

        if d or way == 0:
            for b in range(1, nx):
                start(src, here, x_out.at[dz, b], plane_sem.at[dz, 0, b], device(z, y, shift_x(b), c))
            for b in range(1, ny):
                start(src, here, y_out.at[dz, 0, b], plane_sem.at[dz, b, 0], device(z, shift_y(b), x, c))
            start(src, here, c_out.at[dz, 0], core_sem.at[dz, 0, 0], device(z, y, x, other))

    def turn(way, d, dz):
        if d == 0 and way == 1:
            return
        for dx in range(1, nx):
            here = block(dz, 0, dx, c)
            arrived(here, plane_sem.at[dz, 0, dx])
            for b in range(1, ny):
                start(here, here, y_out.at[dz, dx, b], plane_sem.at[dz, b, dx], device(z, shift_y(b), x, c))
            start(here, here, c_out.at[dz, dx], core_sem.at[dz, 0, dx], device(z, y, x, other))

    for a, b, e in around(grid, ZP):
        mirror = ((ZP - a) % ZP, back(b), e)
        send(ints_ref, ints_all.at[mirror], ints_sem.at[mirror], to(a, b, e))
    each_source(pass_on, 0, 0)
    for d in range(1, NZ):
        each_source(pass_on, d, d)
        if d == NZ - 1:
            for a in range(1, ZP):
                send(cot_ref, cot_all.at[ZP - a, 0, 0], cot_sem.at[ZP - a, 0, 0, 0], to(a, 0, 0))
            for b in range(1, nx):
                send(cot_ref, cot_all.at[0, back(b), 0], cot_sem.at[0, back(b), 0, 0], to(0, b, 0))
                send(rows_ref, rows_all.at[back(b), 0], rows_sem.at[back(b), 0], to(0, b, 0))
        each_source(turn, d - 1, d - 1)
    each_source(turn, NZ - 1, NZ - 1)
    send(cot_ref, cot_all.at[0, 0, 1], cot_sem.at[0, 0, 1, 0], to(0, 0, 1))
    send(rows_ref, rows_all.at[0, 1], rows_sem.at[0, 1], to(0, 0, 1))
    for d in range(1, nx):
        here = rows_all.at[d, 0]
        arrived(here, rows_sem.at[d, 0])
        send(here, rows_all.at[d, 1], rows_sem.at[d, 1], to(0, 0, 1))
    width = cot_ref.shape[1]
    halves = [
        (slice(None), pl.ds(0, width // 2)),
        (slice(None), pl.ds(width // 2, width // 2)),
    ]
    for a in range(1, ZP):
        here = cot_all.at[a, 0, 0]
        arrived(here, cot_sem.at[a, 0, 0, 0])
        for b in range(1, nx):
            send(here.at[halves[0]], cot_all.at[a, back(b), 0].at[halves[0]], cot_sem.at[a, back(b), 0, 0], to(0, b, 0))
        send(here, cot_all.at[a, 0, 1], cot_sem.at[a, 0, 1, 0], to(0, 0, 1))
    for b in range(1, nx):
        here = cot_all.at[0, b, 0]
        arrived(here, cot_sem.at[0, b, 0, 0])
        for a in range(1, ZP):
            send(here.at[halves[1]], cot_all.at[ZP - a, b, 0].at[halves[1]], cot_sem.at[ZP - a, b, 0, 1], to(a, 0, 0))
        send(here, cot_all.at[0, b, 1], cot_sem.at[0, b, 1, 0], to(0, 0, 1))
    for dz in range(NZ):
        for dy in range(1, ny):
            for dx in range(nx):
                here = block(dz, dy, dx, c)
                arrived(here, plane_sem.at[dz, dy, dx])
                send(here, here, core_sem.at[dz, dy, dx], device(z, y, x, other))
    for a in range(1, ZP):
        for b in range(1, nx):
            here = cot_all.at[a, b, 0]
            for part in range(2):
                arrived(here.at[halves[part]], cot_sem.at[a, b, 0, part])
            send(here, cot_all.at[a, b, 1], cot_sem.at[a, b, 1, 0], to(0, 0, 1))
    for dx in range(nx):
        arrived(rows_all.at[dx, 1], rows_sem.at[dx, 1])
        for a in range(ZP):
            arrived(cot_all.at[a, dx, 1], cot_sem.at[a, dx, 1, 0])
    for a, b, e in around(grid, ZP):
        arrived(ints_all.at[a, b, e], ints_sem.at[a, b, e])
    for dz in range(NZ):
        for dy in range(ny):
            for dx in range(nx):
                arrived(block(dz, dy, dx, other), core_sem.at[dz, dy, dx])
    for copy in locals_:
        copy.wait()
    send.finish()

    def sent(way, d, dz):
        if d < NZ - 1:

            @pl.when(z < NZ - 1 if way == 0 else z > 0)
            def _():
                arrived(mine, z_out.at[way, d])

    each_source(sent)
    for dz in range(NZ):
        for b in range(1, nx):
            arrived(mine, x_out.at[dz, b])
        for dx in range(nx):
            for b in range(1, ny):
                arrived(mine, y_out.at[dz, dx, b])
            arrived(mine, c_out.at[dz, dx])


def gather_first(grid_of, weights, rows, cot, ints):
    grid = grid_of()
    nx, ny = grid.nx, grid.ny
    places = NZ * ny * nx * NC
    octet = ZP * nx * NC
    rest = weights[0].shape[0]
    sends = (NZ - 1) + NZ * (nx + ny) + 2 * nx + octet * 4 + NZ * nx * ny * (ny + 1)
    anywhere = pl.BlockSpec(memory_space=pl.ANY)
    dma = pltpu.SemaphoreType.DMA
    return pl.pallas_call(
        functools.partial(gather_kernel, grid_of),
        out_shape=(
            jax.ShapeDtypeStruct(
                (places, rest, sum(w.shape[1] for w in weights)), weights[0].dtype
            ),
            jax.ShapeDtypeStruct((nx, NC) + rows.shape, rows.dtype),
            jax.ShapeDtypeStruct((ZP, nx, NC) + cot.shape, cot.dtype),
            jax.ShapeDtypeStruct((ZP, nx, NC) + ints.shape, ints.dtype),
        ),
        in_specs=[anywhere] * 8,
        out_specs=(anywhere,) * 4,
        scratch_shapes=[
            dma((NZ, ny, nx)),
            dma((NZ, ny, nx)),
            dma((nx, NC)),
            dma((ZP, nx, NC, 2)),
            dma((ZP, nx, NC)),
            dma((sends,)),
            dma((4,)),
            dma((2, NZ)),
            dma((2, NZ)),
            dma((NZ, nx)),
            dma((NZ, nx, ny)),
            dma((NZ, nx)),
            dma((5,)),
        ],
        compiler_params=pltpu.CompilerParams(collective_id=0, has_side_effects=True),
    )(*weights, rows, cot, ints)


def shared_compute(n2, cot, w_in, w_down, out, back, dg, du, dd, h, ag, au):
    hidden, width = w_down.shape
    strip = 256
    for low in range(0, hidden, strip):
        cut = slice(low, min(low + strip, hidden))
        up_cut = slice(hidden + cut.start, hidden + cut.stop)
        gate_act = times(n2[...], w_in[:, cut])
        up_act = times(n2[...], w_in[:, up_cut])
        hidden_grad = times_transposed(cot[...], w_down[cut])
        activated, slope = silu_parts(gate_act)
        h[:, cut] = (activated * up_act).astype(bf16)
        ag[:, cut] = (hidden_grad * up_act * slope).astype(bf16)
        au[:, cut] = (hidden_grad * activated).astype(bf16)
    turned = h[...].T
    for low in range(0, width, strip):
        cut = slice(low, low + strip)
        out[:, cut] = times(h[...], w_down[:, cut])
        back[:, cut] = times_transposed(ag[...], w_in[cut, :hidden]) + times_transposed(
            au[...], w_in[cut, hidden:]
        )
        rows = n2[:, cut].T
        dg[cut] = times(rows, ag[...]).astype(bf16)
        du[cut] = times(rows, au[...]).astype(bf16)
        dd[:, cut] = times(turned, cot[:, cut]).astype(bf16)


def exchange_kernel(grid_of, zp, cut, src, out, plane_sem, core_sem, local_sem, send_sem):
    grid = grid_of()
    nx = grid.nx
    send = Sender(send_sem)
    to = functools.partial(stepped, grid, zp)
    greet([to(*s) for s in around(grid, zp)])
    back = lambda d: (nx - d) % nx
    for a in range(1, zp):
        send(src, out.at[zp - a, 0, 0], plane_sem.at[zp - a, 0, 0], to(a, 0, 0))
    for b in range(1, nx):
        send(src, out.at[0, back(b), 0], plane_sem.at[0, back(b), 0], to(0, b, 0))
    send(src, out.at[0, 0, 1], core_sem.at[0, 0], to(0, 0, 1))
    keep = pltpu.make_async_copy(src, out.at[0, 0, 0], local_sem)
    keep.start()
    h0 = (slice(None), pl.ds(0, cut))
    h1 = (slice(None), pl.ds(cut, src.shape[1] - cut))
    for a in range(1, zp):
        here = out.at[a, 0, 0]
        arrived(here, plane_sem.at[a, 0, 0])
        for b in range(1, nx):
            send(here.at[h0], out.at[a, back(b), 0].at[h0], plane_sem.at[a, back(b), 0], to(0, b, 0))
        send(here, out.at[a, 0, 1], core_sem.at[a, 0], to(0, 0, 1))
    for b in range(1, nx):
        here = out.at[0, b, 0]
        arrived(here, plane_sem.at[0, b, 0])
        for a in range(1, zp):
            send(here.at[h1], out.at[zp - a, b, 0].at[h1], plane_sem.at[zp - a, b, 1], to(a, 0, 0))
        send(here, out.at[0, b, 1], core_sem.at[0, b], to(0, 0, 1))
    for a in range(1, zp):
        for b in range(1, nx):
            here = out.at[a, b, 0]
            arrived(here.at[h0], plane_sem.at[a, b, 0])
            arrived(here.at[h1], plane_sem.at[a, b, 1])
            send(here, out.at[a, b, 1], core_sem.at[a, b], to(0, 0, 1))
    for a in range(zp):
        for b in range(nx):
            arrived(out.at[a, b, 1], core_sem.at[a, b])
    keep.wait()
    send.finish()


def exchange(grid_of, zp, number, rows):
    grid = grid_of()
    nx = grid.nx
    sends = zp * nx * 2 + zp * nx * nx * 2
    anywhere = pl.BlockSpec(memory_space=pl.ANY)
    dma = pltpu.SemaphoreType.DMA
    return pl.pallas_call(
        functools.partial(exchange_kernel, grid_of, zp, rows.shape[1] // 256 * 128),
        out_shape=jax.ShapeDtypeStruct((zp, nx, NC) + rows.shape, rows.dtype),
        in_specs=[anywhere],
        out_specs=anywhere,
        scratch_shapes=[dma((zp, nx, 2)), dma((zp, nx)), dma, dma((sends,))],
        compiler_params=pltpu.CompilerParams(
            collective_id=number, has_side_effects=True
        ),
    )(rows)


def add_into(dst, src, rows):
    for k in range(dst.shape[0]):

        @pl.loop(0, dst.shape[1], step=rows)
        def _(i):
            at = pl.ds(pl.multiple_of(i, rows), rows)
            dst[k, at] = (dst[k, at].astype(f32) + src[k, at].astype(f32)).astype(
                dst.dtype
            )


def sum_kernel(grid_of, zp, cut, small, jobs, parts, *refs):
    grid = grid_of()
    nx = grid.nx
    if small:
        pieces, refs = refs[0], refs[1:]
        shared_ins, refs = refs[:4], refs[4:]
    job_ins, refs = refs[: len(jobs)], refs[len(jobs) :]
    out, refs = refs[0], refs[1:]
    if small:
        pieces_out, refs = refs[0], refs[1:]
        shared_outs, refs = refs[:5], refs[5:]
    job_outs, refs = refs[: len(jobs)], refs[len(jobs) :]
    refs, (job_send, job_recv) = refs[:-2], refs[-2:]
    if small:
        shared_held, load_sem, refs = refs[-8:-1], refs[-1], refs[:-8]
        loads = [
            pltpu.make_async_copy(a, b, load_sem.at[k])
            for k, (a, b) in enumerate(zip(shared_ins, shared_held))
        ]
    each = functools.partial(each_job, grid, jobs, job_ins, job_outs, job_send, job_recv)
    own, got_c, turn_x, turn_p, got_p, got_x = refs[:6]
    local_sem, c_sem, turn_sem, p_sem, x_sem, small_sem, send_sem = refs[6:]
    send = Sender(send_sem)
    to = functools.partial(stepped, grid, zp)
    greet([to(*s) for s in around(grid, zp)] + job_targets(grid, jobs))
    width = parts.shape[-1]
    h0, h1 = pl.ds(0, cut), pl.ds(cut, width - cut)
    order = (
        [(a, b) for a in range(1, zp) for b in range(1, nx)]
        + [(a, 0) for a in range(1, zp)]
        + [(0, b) for b in range(1, nx)]
        + [(0, 0)]
    )
    for a, b in order:
        send(parts.at[:, a, b, 1], got_c.at[:, a, b], c_sem.at[a, b], to(0, 0, 1))
        pltpu.make_async_copy(
            parts.at[:, a, b, 0], own.at[:, a, b], local_sem.at[a, b]
        ).start()
    if small:
        for a, b, e in around(grid, zp):
            mirror = ((zp - a) % zp, (nx - b) % nx, e)
            send(
                pieces.at[a, b, e],
                pieces_out.at[mirror],
                small_sem.at[mirror],
                to(a, b, e),
            )
        pltpu.make_async_copy(
            pieces.at[0, 0, 0], pieces_out.at[0, 0, 0], small_sem.at[0, 0, 0]
        ).start()
    each(lambda copy: copy.start())
    if small:
        for load in loads:
            load.start()
    rows = 32

    def ready(a, b):
        arrived(got_c.at[:, a, b], c_sem.at[a, b])
        pltpu.make_async_copy(
            parts.at[:, a, b, 0], own.at[:, a, b], local_sem.at[a, b]
        ).wait()
        add_into(own.at[:, a, b], got_c.at[:, a, b], rows)

    for a in range(1, zp):
        for b in range(1, nx):
            ready(a, b)
            send(own.at[:, a, b, :, h0], turn_x.at[:, a - 1, b - 1], turn_sem.at[a - 1, b - 1, 0], to(0, b, 0))
            send(own.at[:, a, b, :, h1], turn_p.at[:, a - 1, b - 1], turn_sem.at[a - 1, b - 1, 1], to(a, 0, 0))
    for a in range(1, zp):
        ready(a, 0)
    for b in range(1, nx):
        ready(0, b)
    for a in range(1, zp):
        for b in range(1, nx):
            arrived(turn_x.at[:, a - 1, b - 1], turn_sem.at[a - 1, b - 1, 0])
            add_into(own.at[:, a, 0, :, h0], turn_x.at[:, a - 1, b - 1], rows)
        send(own.at[:, a, 0], got_p.at[:, a - 1], p_sem.at[a - 1], to(a, 0, 0))
    for b in range(1, nx):
        for a in range(1, zp):
            arrived(turn_p.at[:, a - 1, b - 1], turn_sem.at[a - 1, b - 1, 1])
            add_into(own.at[:, 0, b, :, h1], turn_p.at[:, a - 1, b - 1], rows)
        send(own.at[:, 0, b], got_x.at[:, b - 1], x_sem.at[b - 1], to(0, b, 0))
    ready(0, 0)
    if small:
        for load in loads:
            load.wait()
        shared_compute(*shared_held[:4], *shared_outs, *shared_held[4:])
    for a in range(1, zp):
        arrived(got_p.at[:, a - 1], p_sem.at[a - 1])
        add_into(own.at[:, 0, 0], got_p.at[:, a - 1], rows)
    for b in range(1, nx):
        arrived(got_x.at[:, b - 1], x_sem.at[b - 1])
        add_into(own.at[:, 0, 0], got_x.at[:, b - 1], rows)
    result = pltpu.make_async_copy(own.at[:, 0, 0], out, local_sem.at[0, 0])
    result.start()
    if small:
        for a, b, e in [(0, 0, 0)] + around(grid, zp):
            arrived(pieces_out.at[a, b, e], small_sem.at[a, b, e])
    result.wait()
    each(lambda copy: copy.wait())
    send.finish()


def sum_around(grid_of, zp, number, parts, pieces=None, shared=(), jobs=(), job_arrays=()):
    grid = grid_of()
    nx = grid.nx
    payloads, rows, width = parts.shape[0], parts.shape[-2], parts.shape[-1]
    cut = width // 640 * 512
    anywhere = pl.BlockSpec(memory_space=pl.ANY)
    dma = pltpu.SemaphoreType.DMA
    small = pieces is not None
    out_shape = [jax.ShapeDtypeStruct((payloads, rows, width), parts.dtype)]
    args = [parts]
    if small:
        out_shape.append(jax.ShapeDtypeStruct(pieces.shape, pieces.dtype))
        args += [pieces, *shared]
        tokens, hidden = shared[0].shape[0], shared[3].shape[0]
        out_shape += [jax.ShapeDtypeStruct((tokens, width), f32)] * 2
        out_shape += [jax.ShapeDtypeStruct((width, hidden), bf16)] * 2
        out_shape.append(jax.ShapeDtypeStruct((hidden, width), bf16))
    plain = len(out_shape)
    out_shape += job_shapes(grid, jobs, job_arrays)
    args += list(job_arrays)
    turns = (max(zp - 1, 1), max(nx - 1, 1))
    vmem = lambda shape: pltpu.VMEM(shape, parts.dtype)
    made = pl.pallas_call(
        functools.partial(sum_kernel, grid_of, zp, cut, small, jobs),
        out_shape=tuple(out_shape),
        in_specs=[anywhere] * len(args),
        out_specs=tuple(
            pl.BlockSpec(memory_space=pltpu.VMEM) if 2 <= n < plain else anywhere
            for n in range(len(out_shape))
        ),
        scratch_shapes=[
            vmem((payloads, zp, nx, rows, width)),
            vmem((payloads, zp, nx, rows, width)),
            vmem((payloads,) + turns + (rows, cut)),
            vmem((payloads,) + turns + (rows, width - cut)),
            vmem((payloads, turns[0], rows, width)),
            vmem((payloads, turns[1], rows, width)),
            dma((zp, nx)),
            dma((zp, nx)),
            dma(turns + (2,)),
            dma((turns[0],)),
            dma((turns[1],)),
            dma((zp, nx, NC)),
            dma((zp * nx * 6 + 8,)),
        ]
        + (
            [pltpu.VMEM(v.shape, bf16) for v in shared]
            + [pltpu.VMEM((tokens, hidden), bf16)] * 3
            + [dma((4,))]
            if small
            else []
        )
        + job_sems(grid, jobs),
        compiler_params=pltpu.CompilerParams(
            collective_id=number,
            has_side_effects=True,
            vmem_limit_bytes=56 * 2**20,
        ),
    )(*args)
    return made[:plain], made[plain:]


def project_kernel(rows_ref, wq_ref, wk_ref, wv_ref, q_ref, k_ref, v_ref):
    rows = rows_ref[...]
    q_ref[...] = times(rows[: q_ref.shape[0]], wq_ref[...]).astype(bf16)
    k_ref[...] = times(rows, wk_ref[...]).astype(bf16)
    v_ref[...] = times(rows, wv_ref[...]).astype(bf16)


def project(rows, weights, tokens):
    length, width = rows.shape
    strip = 256
    strips = width // strip
    block = pl.BlockSpec
    weight = lambda k: block((width, strip), lambda s: (0, k * strips + s))
    return pl.pallas_call(
        project_kernel,
        grid=(strips,),
        in_specs=[block((length, width), lambda s: (0, 0)), weight(0), weight(1), weight(2)],
        out_specs=[
            block((tokens, strip), lambda s: (0, s)),
            block((length, strip), lambda s: (0, s)),
            block((length, strip), lambda s: (0, s)),
        ],
        out_shape=[
            jax.ShapeDtypeStruct((n, width), bf16) for n in (tokens, length, length)
        ],
        compiler_params=pltpu.CompilerParams(vmem_limit_bytes=48 * 2**20),
        cost_estimate=pl.CostEstimate(
            flops=2 * (tokens + 2 * length) * width * width,
            bytes_accessed=6 * width * width + 6 * length * width,
            transcendentals=0,
        ),
    )(rows, weights, weights, weights)


def project_back_kernel(rows_ref, gq_ref, gvk_ref, w_ref, dq_ref, dk_ref, dv_ref, back_ref):
    turned = rows_ref[...].T
    width = gq_ref.shape[1]
    total = None
    for k, (grad, out) in enumerate(
        ((gq_ref[...], dq_ref), (gvk_ref[1], dk_ref), (gvk_ref[0], dv_ref))
    ):
        out[...] = times(turned, grad).astype(bf16)
        part = times_transposed(grad, w_ref[:, k * width : (k + 1) * width])
        total = part if total is None else total + part
    back_ref[...] = total


def project_back(rows, gq, gvk, weights):
    tokens, width = gq.shape
    strip = 256
    block = pl.BlockSpec
    return pl.pallas_call(
        project_back_kernel,
        grid=(width // strip,),
        in_specs=[
            block((tokens, strip), lambda s: (0, s)),
            block((tokens, width), lambda s: (0, 0)),
            block((2, tokens, width), lambda s: (0, 0, 0)),
            block((strip, 3 * width), lambda s: (s, 0)),
        ],
        out_specs=[block((strip, width), lambda s: (s, 0))] * 3
        + [block((tokens, strip), lambda s: (0, s))],
        out_shape=[jax.ShapeDtypeStruct((width, width), bf16)] * 3
        + [jax.ShapeDtypeStruct((tokens, width), f32)],
        compiler_params=pltpu.CompilerParams(vmem_limit_bytes=48 * 2**20),
        cost_estimate=pl.CostEstimate(
            flops=12 * tokens * width * width,
            bytes_accessed=12 * width * width + 12 * tokens * width,
            transcendentals=0,
        ),
    )(rows, gq, gvk, weights)


def attention_kernel(q_ref, k_ref, v_ref, bias_ref, out_ref):
    scores = times_transposed(q_ref[...], k_ref[...]) * HD ** (-0.5) + bias_ref[...]
    weights = jnp.exp(scores - jnp.max(scores, axis=1, keepdims=True))
    probs = weights * (1.0 / jnp.sum(weights, axis=1, keepdims=True))
    out_ref[...] = times(probs.astype(bf16), v_ref[...]).astype(bf16)


def attention_forward(queries, keys, values, bias):
    rows, width = queries.shape
    length = keys.shape[0]
    by_head = lambda n: pl.BlockSpec((n, HD), lambda h: (0, h))
    return pl.pallas_call(
        attention_kernel,
        grid=(width // HD,),
        out_shape=jax.ShapeDtypeStruct((rows, width), bf16),
        in_specs=[
            by_head(rows),
            by_head(length),
            by_head(length),
            pl.BlockSpec((rows, length), lambda h: (0, 0)),
        ],
        out_specs=by_head(rows),
        compiler_params=pltpu.CompilerParams(vmem_limit_bytes=40 * 2**20),
        cost_estimate=pl.CostEstimate(
            flops=4 * rows * length * width,
            bytes_accessed=4 * (rows + length) * width + 4 * rows * length,
            transcendentals=rows * length * width // HD,
        ),
    )(queries, keys, values, bias)


def attention_back_kernel(
    grid_of, jobs, q_ref, k_ref, v_ref, branch_ref, wo_ref, out_ref, bias_ref, *refs
):
    grid = grid_of()
    count = len(jobs)
    dq_ref, parts_ref, dwo_ref = refs[count : count + 3]
    job_send, job_recv = refs[-2:]
    each = functools.partial(
        each_job, grid, jobs, refs[:count], refs[count + 3 : -2], job_send, job_recv
    )
    if jobs:

        @pl.when(pl.program_id(0) == 0)
        def _():
            greet(job_targets(grid, jobs))
            each(lambda copy: copy.start())

    q, k, branch = q_ref[...], k_ref[...], branch_ref[...]
    g = times_transposed(branch, wo_ref[...]).astype(bf16)
    dwo_ref[...] = times(out_ref[...].T, branch).astype(bf16)
    scores = times_transposed(k, q) * HD ** (-0.5) + bias_ref[...]
    weights = jnp.exp(scores - jnp.max(scores, axis=0, keepdims=True))
    probs = weights * (1.0 / jnp.sum(weights, axis=0, keepdims=True))
    prob_grad = times_transposed(v_ref[...], g)
    centre = jnp.sum(probs * prob_grad, axis=0, keepdims=True)
    score_grad = (probs * (prob_grad - centre)).astype(bf16)
    parts_ref[0] = times(probs.astype(bf16), g).astype(bf16)
    parts_ref[1] = (times(score_grad, q) * HD ** (-0.5)).astype(bf16)
    dq_ref[...] = (contract_rows(score_grad, k) * HD ** (-0.5)).astype(bf16)
    if jobs:

        @pl.when(pl.program_id(0) == pl.num_programs(0) - 1)
        def _():
            each(lambda copy: copy.wait())


def attention_backward(
    grid_of, number, queries, keys, values, branch, weights, attended, bias, jobs, job_arrays
):
    grid = grid_of()
    rows, width = queries.shape
    length = keys.shape[0]
    by_head = lambda n: pl.BlockSpec((n, HD), lambda h: (0, h))
    whole = lambda *shape: pl.BlockSpec(shape, lambda h: (0, 0))
    anywhere = pl.BlockSpec(memory_space=pl.ANY)
    made = pl.pallas_call(
        functools.partial(attention_back_kernel, grid_of, jobs),
        grid=(width // HD,),
        out_shape=tuple(
            [
                jax.ShapeDtypeStruct((rows, width), bf16),
                jax.ShapeDtypeStruct((2, length, width), bf16),
                jax.ShapeDtypeStruct((width, width), bf16),
            ]
            + job_shapes(grid, jobs, job_arrays)
        ),
        in_specs=[
            by_head(rows),
            by_head(length),
            by_head(length),
            whole(rows, width),
            pl.BlockSpec((HD, width), lambda h: (h, 3)),
            by_head(rows),
            whole(length, rows),
        ]
        + [anywhere] * len(jobs),
        out_specs=(
            by_head(rows),
            pl.BlockSpec((2, length, HD), lambda h: (0, 0, h)),
            pl.BlockSpec((HD, width), lambda h: (h, 0)),
        )
        + (anywhere,) * len(jobs),
        scratch_shapes=job_sems(grid, jobs),
        compiler_params=pltpu.CompilerParams(
            vmem_limit_bytes=40 * 2**20,
            **(dict(collective_id=number, has_side_effects=True) if jobs else {}),
        ),
        cost_estimate=pl.CostEstimate(
            flops=10 * rows * length * width + 4 * rows * width * width,
            bytes_accessed=8 * rows * width + 8 * length * width + 4 * rows * length,
            transcendentals=rows * length * width // HD,
        ),
    )(queries, keys, values, branch, weights, attended, bias, *job_arrays)
    return made[0], made[1], made[2], made[3:]


ROW_SOURCES = 2


def expert_kernel(grid_of, capacity, steps, jobs, carry, *refs):
    grid = grid_of()
    count = len(jobs)
    take = lambda n: (refs[:n], refs[n:])
    (rows_ref, cot_ref, rank_row_ref, rank_col_ref, gate_ref, wg_ref, wu_ref, wd_ref), refs = take(8)
    before, refs = take(1 if carry else 0)
    job_ins, refs = take(count)
    (parts_ref, prob_ref, dg_ref, du_ref, dd_ref), refs = take(5)
    job_outs, refs = take(count)
    (x_keep, s_keep, c_keep, h_keep, ag_keep, au_keep, ht_keep), refs = take(7)
    each = functools.partial(each_job, grid, jobs, job_ins, job_outs, *refs)
    step = pl.program_id(0)
    width, hidden = x_keep.shape[1], h_keep.shape[1]
    tokens = rows_ref.shape[1]
    size = ROW_SOURCES * capacity
    strip = 256
    if jobs:

        @pl.when(step == 0)
        def _():
            greet(job_targets(grid, jobs))
            each(lambda copy: copy.start())

    @pl.when(step < steps)
    def _():
        at = pl.ds(pl.multiple_of(step * size, 32), size)
        picks, columns, gates = [], [], []
        for s in range(ROW_SOURCES):
            slots = lax.broadcasted_iota(jnp.int32, (capacity, tokens), 0)
            hit = slots == rank_row_ref[s]
            gate = jnp.sum(jnp.where(hit, gate_ref[s], 0.0), axis=1, keepdims=True)
            pick = hit.astype(f32).astype(bf16)
            picks.append(hit)
            gates.append(gate)
            across = lax.broadcasted_iota(jnp.int32, (tokens, capacity), 1)
            columns.append((across == rank_col_ref[s]).astype(f32).astype(bf16))
            to = pl.ds(pl.multiple_of(step * size + s * capacity, 16), capacity)
            x_keep[to] = times(pick, rows_ref[s]).astype(bf16)
            cot = times(pick, cot_ref[s])
            c_keep[pl.ds(s * capacity, capacity)] = cot.astype(bf16)
            s_keep[to] = (gate * cot).astype(bf16)
        x, slot = x_keep[at], s_keep[at]
        for low in range(0, hidden, strip):
            cut = slice(low, min(low + strip, hidden))
            gate_act = times(x, wg_ref[0, :, cut])
            up_act = times(x, wu_ref[0, :, cut])
            hidden_grad = times_transposed(slot, wd_ref[0, cut])
            activated, slope = silu_parts(gate_act)
            h_keep[at, cut] = (activated * up_act).astype(bf16)
            ag_keep[at, cut] = (hidden_grad * up_act * slope).astype(bf16)
            au_keep[at, cut] = (hidden_grad * activated).astype(bf16)
        h, ag, au = h_keep[at], ag_keep[at], au_keep[at]
        probs = jnp.zeros((size, 1), f32)
        for low in range(0, width, strip):
            cut = slice(low, low + strip)
            made = times(h, wd_ref[0, :, cut]).astype(bf16).astype(f32)
            probs += jnp.sum(made * c_keep[:, cut].astype(f32), axis=1, keepdims=True)
            back = (
                times_transposed(ag, wg_ref[0, cut]) + times_transposed(au, wu_ref[0, cut])
            ).astype(bf16)
            for s in range(ROW_SOURCES):
                mine = slice(s * capacity, (s + 1) * capacity)
                row = times(columns[s], back[mine])
                out = times(columns[s], (gates[s] * made[mine]).astype(bf16))
                if carry:
                    row += before[0][0, s, :, cut].astype(f32)
                    out += before[0][1, s, :, cut].astype(f32)
                parts_ref[0, s, :, cut] = row.astype(bf16)
                parts_ref[1, s, :, cut] = out.astype(bf16)
        for s in range(ROW_SOURCES):
            mine = slice(s * capacity, (s + 1) * capacity)
            prob_ref[s] = jnp.sum(
                jnp.where(picks[s], probs[mine], 0.0), axis=0, keepdims=True
            )

    @pl.when(step == steps)
    def _():
        ht_keep[...] = h_keep[...].T

    @pl.when(step >= steps)
    def _():
        cut = pl.ds(pl.multiple_of((step - steps) * strip, strip), strip)
        turned = x_keep[:, cut].T
        dg_ref[...] = times(turned, ag_keep[...]).astype(bf16)
        du_ref[...] = times(turned, au_keep[...]).astype(bf16)
        dd_ref[...] = times(ht_keep[...], s_keep[:, cut]).astype(bf16)

    if jobs:

        @pl.when(step == pl.num_programs(0) - 1)
        def _():
            each(lambda copy: copy.wait())


def run_expert(grid_of, number, expert, rows, cot, ranks, gates, weights, capacity, before, jobs, job_arrays):
    grid = grid_of()
    sources, tokens = ranks.shape
    width, hidden = weights[0].shape[1:]
    mine = weights[0].shape[0] // ZP
    steps = sources // ROW_SOURCES
    strip = 256
    strips = width // strip
    total = sources * capacity
    turn = lambda s: jnp.minimum(s, steps - 1)
    later = lambda s: jnp.maximum(s - steps, 0)
    block = pl.BlockSpec
    by_source = lambda *rest: block(
        (ROW_SOURCES,) + rest, lambda s: (turn(s),) + (0,) * len(rest)
    )
    held = lambda *rest: block(
        (1,) + rest,
        lambda s: (lax.axis_index("wide") // grid.ny % ZP * mine + expert, 0, 0),
    )
    parts = block((2, ROW_SOURCES, tokens, width), lambda s: (0, turn(s), 0, 0))
    anywhere = block(memory_space=pl.ANY)
    carry = before is not None
    made = pl.pallas_call(
        functools.partial(expert_kernel, grid_of, capacity, steps, jobs, carry),
        grid=(steps + strips,),
        in_specs=[
            by_source(tokens, width),
            by_source(tokens, width),
            by_source(1, tokens),
            by_source(tokens, 1),
            by_source(1, tokens),
            held(width, hidden),
            held(width, hidden),
            held(hidden, width),
        ]
        + [parts] * carry
        + [anywhere] * len(jobs),
        out_specs=[
            parts,
            by_source(1, tokens),
            block((strip, hidden), lambda s: (later(s), 0)),
            block((strip, hidden), lambda s: (later(s), 0)),
            block((hidden, strip), lambda s: (0, later(s))),
        ]
        + [anywhere] * len(jobs),
        scratch_shapes=[
            pltpu.VMEM((total, width), bf16),
            pltpu.VMEM((total, width), bf16),
            pltpu.VMEM((ROW_SOURCES * capacity, width), bf16),
            pltpu.VMEM((total, hidden), bf16),
            pltpu.VMEM((total, hidden), bf16),
            pltpu.VMEM((total, hidden), bf16),
            pltpu.VMEM((hidden, total), bf16),
        ]
        + job_sems(grid, jobs),
        out_shape=[
            jax.ShapeDtypeStruct((2, sources, tokens, width), bf16),
            jax.ShapeDtypeStruct((sources, 1, tokens), f32),
            jax.ShapeDtypeStruct((width, hidden), bf16),
            jax.ShapeDtypeStruct((width, hidden), bf16),
            jax.ShapeDtypeStruct((hidden, width), bf16),
        ]
        + job_shapes(grid, jobs, job_arrays),
        compiler_params=pltpu.CompilerParams(
            vmem_limit_bytes=58 * 2**20,
            **(dict(collective_id=number, has_side_effects=True) if jobs else {}),
        ),
        cost_estimate=pl.CostEstimate(
            flops=total * width * hidden * 18,
            bytes_accessed=width * hidden * 12 + 16 * sources * tokens * width,
            transcendentals=total * hidden,
        ),
    )(
        rows,
        cot,
        ranks[:, None, :],
        ranks[:, :, None],
        gates[:, None, :],
        *weights,
        *([before] if carry else []),
        *job_arrays,
    )
    return made[:5], made[5:]


def jobs_count(grid, jobs):
    return sum({"y": grid.ny, "z": NZ}[axis] - 1 for axis in jobs)


def job_targets(grid, jobs):
    axes = set(jobs)
    place = lambda z, y: (z * grid.ny + y, grid.x * NC + grid.c)
    made = []
    if "y" in axes:
        made += [place(grid.z, (grid.y + d) % grid.ny) for d in range(1, grid.ny)]
    if "z" in axes:
        made += [place((grid.z + d) % NZ, grid.y) for d in range(1, NZ)]
    return made


def each_job(grid, jobs, ins, outs, send_sem, recv_sem, act):
    at = 0
    for axis, src, out in zip(jobs, ins, outs):
        for d in range(1, {"y": grid.ny, "z": NZ}[axis]):
            if axis == "y":
                to = (grid.y + d) % grid.ny
                piece, target = src.at[:, to], (grid.z * grid.ny + to)
            else:
                to = (grid.z + d) % NZ
                piece, target = src.at[to], (to * grid.ny + grid.y)
            act(
                pltpu.make_async_remote_copy(
                    src_ref=piece,
                    dst_ref=out.at[d - 1],
                    send_sem=send_sem.at[at],
                    recv_sem=recv_sem.at[at],
                    device_id=(target, grid.x * NC + grid.c),
                    device_id_type=pl.DeviceIdType.MESH,
                )
            )
            at += 1


def job_shapes(grid, jobs, arrays):
    made = []
    for axis, v in zip(jobs, arrays):
        shape = (grid.ny - 1, NZ) + v.shape[2:] if axis == "y" else (NZ - 1,) + v.shape[1:]
        made.append(jax.ShapeDtypeStruct(shape, v.dtype))
    return made


def job_sems(grid, jobs):
    count = max(jobs_count(grid, jobs), 1)
    return [pltpu.SemaphoreType.DMA((count,)), pltpu.SemaphoreType.DMA((count,))]


def dense_kernel(grid_of, orders, jobs, items, *refs):
    grid = grid_of()
    z, y, x, c, nx, ny = grid.z, grid.y, grid.x, grid.c, grid.nx, grid.ny
    count, more = len(orders), len(jobs)
    wholes = items[-1][0] + 1
    take = lambda n: (refs[:n], refs[n:])
    ins, refs = take(wholes)
    job_ins, refs = take(more)
    outs, refs = take(wholes)
    job_outs, refs = take(more)
    strip = lambda v, low, wide: v.at[(slice(None),) * (len(v.shape) - 1) + (pl.ds(low, wide),)]
    ins = [strip(ins[k], low, wide) for k, low, wide in items]
    outs = [strip(outs[k], low, wide) for k, low, wide in items]
    held, refs = take(count)
    got_c, refs = take(count)
    got_one, refs = take(count)
    got_two, refs = take(count)
    got_z, refs = take(count)
    local_sem, c_sem, one_sem, two_sem, z_sem, out_sem, send_sem, job_send, job_recv = refs
    device = lambda tz, ty, tx, tc: (tz * ny + ty, tx * NC + tc)
    other = (c + 1) % NC
    greet(
        [device(z, y, x, other)]
        + [device(z, y, (x + d) % nx, c) for d in range(1, nx)]
        + [device(z, (y + d) % ny, x, c) for d in range(1, ny)]
        + [device((z + d) % NZ, y, x, c) for d in range(1, NZ)]
    )
    send = Sender(send_sem)
    loads = []

    def begin(k):
        send(ins[k].at[:, :, :, other], got_c[k], c_sem.at[k], device(z, y, x, other))
        load = pltpu.make_async_copy(ins[k].at[:, :, :, c], held[k], local_sem.at[k])
        load.start()
        loads.append(load)

    for k in range(min(3, count)):
        begin(k)
    each_job(grid, jobs, job_ins, job_outs, job_send, job_recv, lambda copy: copy.start())

    def add(dst, src):
        lead = dst.shape[:-2]
        total = 1
        for n in lead:
            total *= n

        @pl.loop(0, total)
        def _(i):
            index = []
            for n in reversed(lead):
                index.insert(0, i % n)
                i = i // n
            index = tuple(index)
            dst[index] = (dst[index].astype(f32) + src[index].astype(f32)).astype(dst.dtype)

    def first(k):
        if k + 3 < count:
            begin(k + 3)
        loads[k].wait()
        arrived(got_c[k], c_sem.at[k])
        add(held[k], got_c[k])
        if orders[k] == "xy":
            for d in range(1, nx):
                to = (x + d) % nx
                send(held[k].at[:, :, to], got_one[k].at[d - 1], one_sem.at[k, d - 1], device(z, y, to, c))
        else:
            for d in range(1, ny):
                to = (y + d) % ny
                send(held[k].at[:, to], got_one[k].at[d - 1], one_sem.at[k, d - 1], device(z, to, x, c))

    def second(k):
        mine = held[k].at[:, :, x] if orders[k] == "xy" else held[k].at[:, y]
        for d in range(1, nx if orders[k] == "xy" else ny):
            arrived(got_one[k].at[d - 1], one_sem.at[k, d - 1])
            add(mine, got_one[k].at[d - 1])
        if orders[k] == "xy":
            for d in range(1, ny):
                to = (y + d) % ny
                send(held[k].at[:, to, x], got_two[k].at[d - 1], two_sem.at[k, d - 1], device(z, to, x, c))
        else:
            for d in range(1, nx):
                to = (x + d) % nx
                send(held[k].at[:, y, to], got_two[k].at[d - 1], two_sem.at[k, d - 1], device(z, y, to, c))

    results = []

    def third(k):
        mine = held[k].at[:, y, x]
        for d in range(1, ny if orders[k] == "xy" else nx):
            arrived(got_two[k].at[d - 1], two_sem.at[k, d - 1])
            add(mine, got_two[k].at[d - 1])
        near = z // ZP * ZP + (z + 1) % ZP
        for n in range(NZ // ZP):
            to = (z + 1) % ZP + n * ZP
            send(held[k].at[to, y, x], got_z[k].at[n], z_sem.at[k, n], device(near, y, x, c))

    def fourth(k):
        for n in range(NZ // ZP):
            arrived(got_z[k].at[n], z_sem.at[k, n])
            at = (z % ZP + n * ZP, y, x)
            held[k][at] = (held[k][at].astype(f32) + got_z[k][n].astype(f32)).astype(held[k].dtype)
        for n in range(1, NZ // ZP):
            to = (z + n * ZP) % NZ
            send(held[k].at[to, y, x], outs[k].at[n], z_sem.at[k, NZ // ZP + n - 1], device(to, y, x, c))
        result = pltpu.make_async_copy(held[k].at[z, y, x], outs[k].at[0], out_sem.at[k])
        result.start()
        results.append(result)

    for t in range(count + 6):
        for stage, late in ((first, 0), (second, 2), (third, 4), (fourth, 6)):
            if 0 <= t - late < count:
                stage(t - late)
    for k in range(count):
        for n in range(1, NZ // ZP):
            arrived(outs[k].at[n], z_sem.at[k, NZ // ZP + n - 1])
        results[k].wait()
    each_job(grid, jobs, job_ins, job_outs, job_send, job_recv, lambda copy: copy.wait())
    send.finish()


def reduce_dense(grid_of, number, arrays, jobs, job_arrays):
    grid = grid_of()
    nx, ny = grid.nx, grid.ny
    items = []
    for k, v in enumerate(arrays):
        wide = v.shape[5]
        low = wide // 2 if wide % 256 == 0 else wide
        items += [(k, at, low) for at in range(0, wide, low)]
    orders = ["xy" if n % 2 == 0 else "yx" for n in range(len(items))]
    count = len(items)
    anywhere = pl.BlockSpec(memory_space=pl.ANY)
    dma = pltpu.SemaphoreType.DMA
    block = [(arrays[k].shape[4], wide) for k, _, wide in items]
    kind = [arrays[k].dtype for k, _, _ in items]
    far = max(nx, ny)
    held = [pltpu.VMEM((NZ, ny, nx) + b, t) for b, t in zip(block, kind)]
    one = [
        pltpu.VMEM((nx - 1, NZ, ny) + b if o == "xy" else (ny - 1, NZ, nx) + b, t)
        for b, t, o in zip(block, kind, orders)
    ]
    two = [
        pltpu.VMEM(((ny if o == "xy" else nx) - 1, NZ) + b, t)
        for b, t, o in zip(block, kind, orders)
    ]
    made = pl.pallas_call(
        functools.partial(dense_kernel, grid_of, orders, jobs, items),
        out_shape=tuple(
            [jax.ShapeDtypeStruct((NZ // ZP,) + v.shape[4:], v.dtype) for v in arrays]
            + job_shapes(grid, jobs, job_arrays)
        ),
        in_specs=[anywhere] * (len(arrays) + len(jobs)),
        out_specs=(anywhere,) * (len(arrays) + len(jobs)),
        scratch_shapes=held
        + held
        + one
        + two
        + [pltpu.VMEM((NZ // ZP,) + b, t) for b, t in zip(block, kind)]
        + [
            dma((count,)),
            dma((count,)),
            dma((count, far)),
            dma((count, far)),
            dma((count, NZ - 1)),
            dma((count,)),
            dma((count * (1 + nx + ny + NZ),)),
        ]
        + job_sems(grid, jobs),
        compiler_params=pltpu.CompilerParams(
            collective_id=number,
            has_side_effects=True,
            vmem_limit_bytes=60 * 2**20,
        ),
    )(*arrays, *job_arrays)
    return made[: len(arrays)], made[len(arrays) :]


def finish_kernel(grid_of, mine, dense, *refs):
    grid = grid_of()
    kinds = 3
    names = mine * kinds
    own, far = refs[:names], refs[names : 2 * names]
    terms = refs[2 * names : 2 * names + dense]
    outs = refs[2 * names + dense :]
    for n in range(names):
        i, kind = n // kinds, n % kinds
        sums = [own[n][0].astype(f32), None]
        for d in range(1, NZ):
            got = far[n][d - 1].astype(f32)
            sums[d % ZP] = got if sums[d % ZP] is None else sums[d % ZP] + got
        outs[kind][grid.zm, i] = sums[0]
        outs[kind][1 - grid.zm, i] = sums[1]
    for n in range(dense):
        total = terms[n][0].astype(f32)
        for d in range(1, terms[n].shape[0]):
            total = total + terms[n][d].astype(f32)
        outs[kinds + n][...] = total


def finish(grid_of, mine, columns, far, terms):
    grid = grid_of()
    whole = lambda v: pl.BlockSpec(v.shape, lambda _: (0,) * len(v.shape))
    out_shape = [
        jax.ShapeDtypeStruct((ZP, mine) + columns[k].shape[1:], f32) for k in range(3)
    ] + [jax.ShapeDtypeStruct(v.shape[1:], f32) for v in terms]
    return pl.pallas_call(
        functools.partial(finish_kernel, grid_of, mine, len(terms)),
        grid=(1,),
        out_shape=out_shape,
        in_specs=[
            pl.BlockSpec(
                (1,) + v.shape[1:],
                lambda _: (lax.axis_index("wide") // grid.ny, 0, 0),
            )
            for v in columns
        ]
        + [whole(v) for v in far]
        + [whole(v) for v in terms],
        out_specs=[whole(v) for v in out_shape],
        compiler_params=pltpu.CompilerParams(vmem_limit_bytes=62 * 2**20),
    )(*columns, *far, *terms)


def attention_bias(segment, labels_all, query_places, key_places):
    same_doc = segment[:, None] == labels_all[None, :]
    allowed = same_doc & (query_places[:, None] >= key_places[None, :])
    return jnp.where(allowed, 0.0, masked_value).astype(f32)


def body(
    wide,
    ep,
    activations,
    segment,
    routes,
    gain_attention,
    query_weight,
    key_weight,
    value_weight,
    output_weight,
    gain_experts,
    router_weight,
    shared_gate,
    shared_up,
    shared_down,
    expert_gate,
    expert_up,
    expert_down,
    cotangent,
):
    grid_of = functools.partial(Grid, wide, ep)
    grid = grid_of()
    nx, ny = grid.nx, grid.ny
    tok_rows, width = activations.shape
    heads = width // HD
    top_count = routes.shape[1]
    experts = router_weight.shape[1]
    local_experts = expert_gate.shape[0]
    mine = local_experts // ZP
    hidden_width = expert_gate.shape[2]
    sources = ZP * nx * NC
    capacity = min((tok_rows * top_count * 10 // (7 * experts) + 7) // 8 * 8, tok_rows)

    rest = jnp.concatenate(
        [
            router_weight,
            gain_attention[:, None],
            gain_experts[:, None],
            jnp.zeros((gain_experts.shape[0], 128 - experts - 2), bf16),
        ],
        axis=1,
    )
    bundle = (query_weight, key_weight, value_weight, output_weight, rest)
    integers = jnp.concatenate([routes.T, segment[None, :]], axis=0)
    bundle_all, group_rows, cot_all, integers_all = gather_first(
        grid_of, bundle, activations, cotangent, integers
    )
    group_rows = group_rows.reshape(-1, width)
    integers_all = integers_all.reshape(sources, top_count + 1, tok_rows)
    bundle_all = bundle_all.reshape(width, bundle_all.shape[2])
    w_out = bundle_all[:, 3 * width : 4 * width]
    small_all = bundle_all[:, 4 * width :]
    gather_all = lambda v: lax.all_gather(v, BOTH, axis=0, tiled=True)
    shared_in, shared_out_in, integers_all = lax.optimization_barrier(
        (
            jnp.concatenate([shared_gate, shared_up], axis=1),
            shared_down,
            integers_all,
        )
    )
    s_both = gather_all(shared_in)
    s_down = gather_all(shared_out_in)
    w_router = small_all[:, :experts]
    gain_one = small_all[:, experts].astype(f32)
    gain_two = small_all[:, experts + 1].astype(f32)

    inputs = activations.astype(f32)
    inverse_one = norm_scale(inputs)
    group_inputs = group_rows.astype(f32)
    normed_group = (group_inputs * norm_scale(group_inputs) * gain_one).astype(bf16)
    normed_one = normed_group[:tok_rows]
    queries, keys_all, values_all = project(normed_group, bundle_all, tok_rows)
    labels_all = integers_all[: nx * NC, top_count].reshape(-1)
    steps = jnp.arange(tok_rows, dtype=jnp.int32)
    block_places = (
        (grid.x + jnp.arange(nx, dtype=jnp.int32)[:, None]) % nx * NC
        + (grid.c + jnp.arange(NC, dtype=jnp.int32)[None, :]) % NC
    ).reshape(-1)
    key_places = (block_places[:, None] * tok_rows + steps[None, :]).reshape(-1)
    query_places = (grid.x * NC + grid.c) * tok_rows + steps
    bias = attention_bias(segment, labels_all, query_places, key_places)
    attended = attention_forward(queries, keys_all, values_all, bias)
    middle = inputs + times(attended, w_out)
    inverse_two = norm_scale(middle)
    normed_two = (middle * inverse_two * gain_two).astype(bf16)

    rows_all = exchange(grid_of, ZP, 1, normed_two)
    rows_all = rows_all.reshape(sources, tok_rows, width)
    cot_all = cot_all.reshape(sources, tok_rows, width)
    router_probs_all = jax.nn.softmax(
        times(rows_all.reshape(-1, width), w_router).reshape(sources, tok_rows, experts),
        axis=-1,
    )
    router_probs = router_probs_all[0]
    first_expert = (grid.x * NC + grid.c) * local_experts + grid.zm * mine
    routes_all = integers_all[:, :top_count]
    numbers = first_expert + jnp.arange(mine, dtype=jnp.int32)
    marks = jnp.any(
        routes_all[None] == numbers[:, None, None, None], axis=2
    )
    earlier = (steps[:, None] < steps[None, :]).astype(bf16)
    ranks = jnp.einsum(
        "irt,tu->iru", marks.astype(bf16), earlier, preferred_element_type=f32
    ).astype(jnp.int32)
    ranks = jnp.where(marks, ranks, -1)
    gates_mine = jnp.moveaxis(
        lax.dynamic_slice_in_dim(router_probs_all, first_expert, mine, axis=2), 2, 0
    )
    def by_wide(v):
        return v.reshape(NZ, ny, v.shape[0] // wide, v.shape[1])

    names = [(i, k) for i in range(mine) for k in range(3)]
    grads, along_y, along_z = {}, {}, {}

    def jobs_of(which_y, which_z):
        tags = tuple("y" for _ in which_y) + tuple("z" for _ in which_z)
        return tags, [grads[n] for n in which_y] + [column[n] for n in which_z]

    def landed(which_y, which_z, moved):
        along_y.update(zip(which_y, moved))
        along_z.update(zip(which_z, moved[len(which_y) :]))

    def summed(name):
        total = lax.dynamic_index_in_dim(grads[name], grid.y, 1, keepdims=False).astype(f32)
        for d in range(ny - 1):
            total = total + along_y[name][d].astype(f32)
        return total.astype(bf16)

    column = {}
    both_parts = None
    prob_parts = []
    for i in range(mine):
        behind = (names[:1], []) if i else ([], [])
        (both_parts, probs_here, *made), moved = run_expert(
            grid_of,
            5 + i,
            i,
            rows_all,
            cot_all,
            ranks[i],
            gates_mine[i],
            (expert_gate, expert_up, expert_down),
            capacity,
            both_parts,
            *jobs_of(*behind),
        )
        landed(*behind, moved)
        prob_parts.append(probs_here[:, 0])
        grads.update({(i, k): by_wide(v) for k, v in enumerate(made)})
    column.update({name: summed(name) for name in along_y})
    behind = (names[1:3], names[:1])
    (
        sums,
        sent,
        shared_out,
        shared_back,
        shared_gate_grad,
        shared_up_grad,
        shared_down_grad,
    ), moved = sum_around(
        grid_of,
        ZP,
        2,
        both_parts.reshape(2, ZP, nx, NC, tok_rows, width),
        jnp.stack(prob_parts, axis=1).reshape(ZP, nx, NC, mine, tok_rows),
        (normed_two, cotangent, s_both, s_down),
        *jobs_of(*behind),
    )
    landed(*behind, moved)
    column.update({name: summed(name) for name in behind[0]})
    routed_grad = sums[0].astype(f32)
    routed = sums[1].astype(f32)
    dz = (grid.zm + jnp.arange(ZP, dtype=jnp.int32)) % ZP
    owner = block_places.reshape(1, nx, NC, 1) * local_experts
    owner = owner + dz[:, None, None, None] * mine + jnp.arange(mine, dtype=jnp.int32)
    same = owner.reshape(-1)[None, :] == jnp.arange(experts, dtype=jnp.int32)[:, None]
    prob_grad = jnp.sum(
        jnp.where(same[:, :, None], sent.reshape(1, experts, tok_rows), 0.0), axis=1
    ).T

    out_grad = cotangent.astype(f32)
    block_out = (middle + shared_out + routed).astype(bf16)

    logit_grad = router_probs * (
        prob_grad - jnp.sum(router_probs * prob_grad, axis=-1, keepdims=True)
    )
    router_grad = lax.dot_general(
        normed_two.astype(f32),
        logit_grad,
        (((0,), (0,)), ((), ())),
        precision=lax.Precision.HIGHEST,
        preferred_element_type=f32,
    )
    normed_two_grad = (
        shared_back
        + routed_grad
        + lax.dot_general(
            logit_grad,
            w_router.astype(f32),
            (((1,), (1,)), ((), ())),
            precision=lax.Precision.HIGHEST,
            preferred_element_type=f32,
        )
    )
    gain_two_grad, middle_part = norm_backward(
        middle, inverse_two, gain_two, normed_two_grad
    )
    middle_grad = out_grad + middle_part
    branch_grad = middle_grad.astype(bf16)

    behind = (names[3:4], names[1:2])
    query_act_grad, parts, output_weight_grad, moved = attention_backward(
        grid_of,
        1 + 8,
        queries,
        keys_all,
        values_all,
        branch_grad,
        bundle_all,
        attended,
        bias.T,
        *jobs_of(*behind),
    )
    landed(*behind, moved)
    behind = (names[4:], names[2:4])
    column.update({name: summed(name) for name in names[3:4]})
    ((value_key,), moved) = sum_around(
        grid_of,
        1,
        3,
        parts.reshape(2, 1, nx, NC, tok_rows, width),
        None,
        (),
        *jobs_of(*behind),
    )
    landed(*behind, moved)
    column.update({name: summed(name) for name in names[4:]})
    query_w_grad, key_w_grad, value_w_grad, normed_one_grad = project_back(
        normed_group, query_act_grad, value_key, bundle_all
    )
    gain_one_grad, input_part = norm_backward(
        inputs, inverse_one, gain_one, normed_one_grad
    )
    input_grad = middle_grad + input_part

    def by_place(v):
        return v.reshape((NZ, ny, nx, NC, v.shape[0] // (wide * ep)) + v.shape[1:])

    counts = jnp.sum(
        (routes[:, :, None] == jnp.arange(experts, dtype=jnp.int32)).astype(f32),
        axis=(0, 1),
    )
    share = gain_attention.shape[0]
    count_block = jnp.pad(
        jnp.tile(counts.reshape(1, ep, 1, local_experts), (wide, 1, 1, 1)),
        ((0, 0), (0, 0), (0, 0), (0, 128 - local_experts)),
    )
    extras = jnp.concatenate(
        [
            router_grad,
            gain_one_grad[:, None],
            gain_two_grad[:, None],
            jnp.zeros((width, 128 - experts - 2), f32),
        ],
        axis=1,
    ).reshape(wide, ep, share, 128)
    extras = jnp.concatenate(
        [extras, count_block, jnp.zeros((wide, ep, 7, 128), f32)], axis=2
    )
    dense = [
        output_weight_grad,
        shared_down_grad,
        shared_gate_grad,
        shared_up_grad,
        query_w_grad,
        key_w_grad,
        value_w_grad,
    ]
    terms, moved = reduce_dense(
        grid_of,
        4,
        [by_place(v.astype(bf16)) for v in dense]
        + [extras.reshape(NZ, ny, nx, NC, share + 8, 128)],
        *jobs_of([], names[4:]),
    )
    landed([], names[4:], moved)
    (
        expert_gate_grad,
        expert_up_grad,
        expert_down_grad,
        output_weight_sum,
        shared_down_sum,
        shared_gate_sum,
        shared_up_sum,
        query_sum,
        key_sum,
        value_sum,
        extra_sum,
    ) = finish(
        grid_of, mine, [column[n] for n in names], [along_z[n] for n in names], terms
    )
    expert_gate_grad, expert_up_grad, expert_down_grad = (
        v.reshape((local_experts,) + v.shape[2:])
        for v in (expert_gate_grad, expert_up_grad, expert_down_grad)
    )
    return (
        block_out,
        input_grad,
        extra_sum[:share, experts],
        query_sum,
        key_sum,
        value_sum,
        output_weight_sum,
        extra_sum[:share, experts + 1],
        extra_sum[:share, :experts],
        shared_gate_sum,
        shared_up_sum,
        shared_down_sum,
        expert_gate_grad,
        expert_up_grad,
        expert_down_grad,
        extra_sum[share, :local_experts].astype(jnp.int32),
    )


def solution(mesh):
    split = P(BOTH, None)
    line = P(BOTH)
    held = P("ep", None, None)
    out_held = P("ep", "wide", None)
    in_specs = (
        (split, line, split, line)
        + (split,) * 4
        + (line,)
        + (split,) * 4
        + (held,) * 3
        + (split,)
    )
    out_specs = (
        (split, split, line)
        + (split,) * 4
        + (line,)
        + (split,) * 4
        + (out_held,) * 3
        + (P("ep"),)
    )
    return jax.shard_map(
        functools.partial(body, mesh.shape["wide"], mesh.shape["ep"]),
        mesh=mesh,
        in_specs=in_specs,
        out_specs=out_specs,
        check_vma=False,
    )
```
